32 devices in a mesh: dp: 8 (over y, x, core), tensor: 4 (over z).
Axes of the slice: x: 2, y: 2, z: 4, core: 2. Of those that a mesh axis runs over, the one named last changes fastest.
Arguments:
- in_streams: bfloat16 [4, 4096, 2048], P(None, ('dp', 'tensor')), may hold values from -6 to 6
- stored: bfloat16 [8, 4096, 2048], P(None, ('dp', 'tensor')), may hold values from -6 to 6
- cotangent: bfloat16 [4, 4096, 2048], P(None, ('dp', 'tensor')), may hold values from -8 to 8
- in_weights: float32 [2048, 14336], P('dp', 'tensor'), may hold values from -0.176776695 to 0.176776695
- in_moment: float32 [2048, 14336], P('dp', 'tensor'), may hold values from -9.387309e-05 to 9.387309e-05
- in_second: float32 [2048, 14336], P('dp', 'tensor'), may hold values from 1.0435448e-09 to 4.1741792e-09
- in_average: float32 [2048, 14336], P('dp', 'tensor'), may hold values from -0.125 to 0.125
- out_weights: float32 [2048, 10240], P('dp', 'tensor'), may hold values from -0.70710678 to 0.70710678
- out_moment: float32 [2048, 10240], P('dp', 'tensor'), may hold values from -9.387309e-05 to 9.387309e-05
- output_second_moment: float32 [2048, 10240], P('dp', 'tensor'), may hold values from 1.0435448e-09 to 4.1741792e-09
- out_average: float32 [2048, 10240], P('dp', 'tensor'), may hold values from -0.125 to 0.125
- small_params: float32 [50, 2048], replicated, may hold values from -2 to 2
- small_moment: float32 [50, 2048], replicated, may hold values from -0.001552825 to 0.001552825
- small_second: float32 [50, 2048], replicated, may hold values from 9.391903e-09 to 1.1421784e-06
- small_average: float32 [50, 2048], replicated, may hold values from -3 to 3
- mix_weights: float32 [37, 36], replicated, may hold values from -1 to 1
- mix_moment: float32 [37, 36], replicated, may hold values from -0.001552825 to 0.001552825
- mix_second: float32 [37, 36], replicated, may hold values from 2.855446e-07 to 1.1421783e-06
- mix_average: float32 [37, 36], replicated, may hold values from -1 to 1
Outputs:
- out_streams: bfloat16 [4, 4096, 2048], P(None, ('dp', 'tensor'))
- grad_streams: bfloat16 [4, 4096, 2048], P(None, ('dp', 'tensor'))
- grad_stored: bfloat16 [8, 4096, 2048], P(None, ('dp', 'tensor'))
- grad_norm: float32 [], replicated
- in_updated: float32 [2048, 14336], P('dp', 'tensor')
- in_moment_new: float32 [2048, 14336], P('dp', 'tensor')
- in_second_new: float32 [2048, 14336], P('dp', 'tensor')
- in_average_new: float32 [2048, 14336], P('dp', 'tensor')
- in_copy: bfloat16 [2048, 14336], P('dp', 'tensor')
- out_updated: float32 [2048, 10240], P('dp', 'tensor')
- out_moment_new: float32 [2048, 10240], P('dp', 'tensor')
- out_second_new: float32 [2048, 10240], P('dp', 'tensor')
- out_average_new: float32 [2048, 10240], P('dp', 'tensor')
- out_copy: bfloat16 [2048, 10240], P('dp', 'tensor')
- small_updated: float32 [50, 2048], replicated
- small_moment_new: float32 [50, 2048], replicated
- small_second_new: float32 [50, 2048], replicated
- small_average_new: float32 [50, 2048], replicated
- mix_updated: float32 [37, 36], replicated
- mix_moment_new: float32 [37, 36], replicated
- mix_second_new: float32 [37, 36], replicated
- mix_average_new: float32 [37, 36], replicated
The draws below stay inside these ranges and needn't reach their ends.
All inputs are finite; a program needn't handle non-finite values.
Results may differ from the reference program's by a relative error of at most 0.024.
Values may be sent and summed in bfloat16 or wider, within the bound.
A program may use at most 320 MiB of HBM per device.

```python
import math
import jax
import jax.numpy as jnp
from jax import lax

D = 2048
HEADS = 16
HD = 128
ROT = 32
FF = 8192
STREAMS = 4
LAYER = 8
STEP = 10
LEN = 512
LAYERS = 9
MIXH = 36
TOKENS = 4096
HEADS_RANK = 4
FF_RANK = 2048
NIN = 14336
NOUT = 10240
SROWS = 50
NPARAM = 50435380
N_TENSOR = 4


def draw_in_weights(key, part):
    key = jax.random.fold_in(key, 11)
    across = jnp.arange(NIN, dtype=jnp.float32) / NIN
    base_draw = jax.random.truncated_normal(key, -6.0, 6.0, (D, NIN), jnp.float32)
    rise_factor = 0.75 + 0.55 * across
    return base_draw * rise_factor[None, :] * D ** (-0.5)


def draw_out_weights(key, part):
    key = jax.random.fold_in(key, 12)
    columns = jnp.arange(NOUT, dtype=jnp.int32)
    within = columns % (HEADS_RANK * HD + FF_RANK)
    fan_scale = jnp.where(within < HEADS_RANK * HD, 4.0 * D ** (-0.5), FF ** (-0.5))
    across = columns.astype(jnp.float32) / NOUT
    base_draw = jax.random.truncated_normal(key, -6.0, 6.0, (D, NOUT), jnp.float32)
    rise_factor = 0.75 + 0.55 * across
    return base_draw * (rise_factor * fan_scale)[None, :]


def draw_small_params(key, part):
    key = jax.random.fold_in(key, 13)
    across = jnp.arange(D, dtype=jnp.float32) / D
    row_ids = jnp.arange(SROWS, dtype=jnp.int32)[:, None]
    noise_draw = jax.random.truncated_normal(key, -6.0, 6.0, (SROWS, D), jnp.float32)
    rise_factor = 0.6 + 0.5 * across
    gain_rows = rise_factor[None, :] * (1.0 + 0.1 * noise_draw)
    is_gain = (row_ids == 0) | (row_ids == 2) | (row_ids == 4)
    is_mix = row_ids >= SROWS - MIXH
    return jnp.where(is_gain, gain_rows, jnp.where(is_mix, noise_draw * D ** (-0.5), 0.3 * noise_draw))


def draw_cotangent(key, part):
    key = jax.random.fold_in(key, 14)
    across = jnp.arange(D, dtype=jnp.float32) / D
    base_draw = jax.random.truncated_normal(key, -6.0, 6.0, (STREAMS, TOKENS, D), jnp.float32)
    rise_factor = 0.75 + 0.55 * across
    return (base_draw * rise_factor[None, None, :]).astype(jnp.bfloat16)


def square_scale_rows():
    row_ids = jnp.arange(SROWS, dtype=jnp.int32)[:, None]
    return jnp.where(row_ids >= SROWS - MIXH, 0.4 / (MIXH * D), 9.0 / NPARAM).astype(jnp.float32)


def draw_small_moment(key, part):
    key = jax.random.fold_in(key, 15)
    scale_rows = jnp.where(jnp.arange(SROWS, dtype=jnp.int32)[:, None] >= SROWS - MIXH, (0.4 / (MIXH * D)) ** 0.5 / 9.0, 1.0 / (3.0 * NPARAM ** 0.5)).astype(jnp.float32)
    base_draw = jax.random.truncated_normal(key, -6.0, 6.0, (SROWS, D), jnp.float32)
    return base_draw * scale_rows


def draw_small_second(key, part):
    key = jax.random.fold_in(key, 16)
    scale_rows = square_scale_rows() / 19.0
    factor = jnp.exp(jax.random.uniform(key, (SROWS, D), jnp.float32, 0.0, 1.3862944))
    return scale_rows * factor


def block_levels(stream_key, extent, cuts, low, high):
    loudness, own = 1.0, jax.random.fold_in(stream_key, 6)
    for axis_at, blocks in cuts:
        draws = jnp.exp(jax.random.uniform(jax.random.fold_in(own, axis_at), (blocks,), jnp.float32, low / len(cuts), high / len(cuts)))
        loudness = loudness * jnp.repeat(draws, extent[axis_at] // blocks).reshape([-1 if axis == axis_at else 1 for axis in range(len(extent))])
    return loudness


def normal_values(rng, shape, deviation, most, shards=(), kind=jnp.bfloat16):
    factor_of = block_levels(rng, shape, shards, -0.22, 0.18) if shards else 1.0
    entries = jax.random.normal(rng, shape, jnp.float32) * deviation * factor_of
    return jnp.minimum(jnp.maximum(entries, -most), most).astype(kind)


def setup_inputs(seed: int = 0) -> dict:
    keys = jax.random.split(jax.random.key(seed), 20)
    return {
        "in_streams": normal_values(keys[0], (STREAMS, TOKENS, D), 1.0, 6.0, ((1, 32),)),
        "stored": normal_values(keys[1], (LAYER, TOKENS, D), 1.0, 6.0, ((1, 32),)),
        "cotangent": draw_cotangent(jax.random.fold_in(keys[19], 71), 0),
        "in_weights": draw_in_weights(jax.random.fold_in(keys[19], 71), 0),
        "in_moment": normal_values(keys[4], (D, NIN), (1 / (9 * NPARAM ** 0.5)), 9.38730881898664e-05, ((0, 8), (1, 4)), jnp.float32),
        "in_second": jnp.clip(jnp.exp(math.log(4.174179224492036e-09) - 1.3862944 * jax.random.uniform(keys[5], (D, NIN), jnp.float32) ** block_levels(keys[5], (D, NIN), ((0, 8), (1, 4)), -0.2, 0.2)), 1.043544806123009e-09, 4.174179224492036e-09),
        "in_average": normal_values(keys[6], (D, NIN), D ** -0.5, 0.125, ((0, 8), (1, 4)), jnp.float32),
        "out_weights": draw_out_weights(jax.random.fold_in(keys[19], 71), 0),
        "out_moment": normal_values(keys[8], (D, NOUT), (1 / (9 * NPARAM ** 0.5)), 9.38730881898664e-05, ((0, 8), (1, 4)), jnp.float32),
        "output_second_moment": jnp.clip(jnp.exp(math.log(4.174179224492036e-09) - 1.3862944 * jax.random.uniform(keys[9], (D, NOUT), jnp.float32) ** block_levels(keys[9], (D, NOUT), ((0, 8), (1, 4)), -0.2, 0.2)), 1.043544806123009e-09, 4.174179224492036e-09),
        "out_average": normal_values(keys[10], (D, NOUT), D ** -0.5, 0.125, ((0, 8), (1, 4)), jnp.float32),
        "small_params": draw_small_params(jax.random.fold_in(keys[19], 71), 0),
        "small_moment": draw_small_moment(jax.random.fold_in(keys[19], 71), 0),
        "small_second": draw_small_second(jax.random.fold_in(keys[19], 71), 0),
        "small_average": normal_values(keys[14], (SROWS, D), 0.5, 3.0, (), jnp.float32),
        "mix_weights": normal_values(keys[15], (MIXH + 1, MIXH), MIXH ** -0.5, 1.0, (), jnp.float32),
        "mix_moment": normal_values(keys[16], (MIXH + 1, MIXH), ((0.4 / (MIXH * D)) ** 0.5 / 9), 0.001552825, (), jnp.float32),
        "mix_second": jnp.clip(jnp.exp(jax.random.uniform(keys[17], (MIXH + 1, MIXH), jnp.float32, math.log(2.8554458708640595e-07), math.log(1.1421783483456238e-06))), 2.8554458708640595e-07, 1.1421783483456238e-06),
        "mix_average": normal_values(keys[18], (MIXH + 1, MIXH), MIXH ** -0.5, 1.0, (), jnp.float32),
    }


@jax.custom_vjp
def low(v):
    return lax.optimization_barrier(v.astype(jnp.bfloat16)).astype(jnp.float32)

@jax.custom_vjp
def low_back(v):
    return v

def low_keep(v):
    return (low(v), None)

def low_pass(kept, grad):
    return (grad,)

def back_keep(v):
    return (v, None)

def back_low(kept, grad):
    return (low(grad),)
low.defvjp(low_keep, low_pass)
low_back.defvjp(back_keep, back_low)
norm_eps = 1e-05
mix_eps = 1e-06
beta_first = 0.9
beta_second = 0.95
adam_eps = 1e-08
decay_rate = 0.01
learn_rate = 0.03
small_rate = 0.2
clip_norm = 1.0
average_keep = 0.5
masked_score = -1e+30
highest_precision = lax.Precision.HIGHEST

def layer_norm(values, gain, shift):
    centred = values - lax.optimization_barrier(jnp.mean(values, axis=-1, keepdims=True))
    spread = lax.optimization_barrier(jnp.mean(centred * centred, axis=-1, keepdims=True))
    return centred * lax.rsqrt(spread + norm_eps) * gain + shift

def rope_tables(length):
    half_rot = ROT // 2
    exponent = jnp.arange(half_rot, dtype=jnp.float32) * (2.0 / ROT)
    inverse = 1.0 / 10000.0 ** exponent
    angles = jnp.arange(length, dtype=jnp.float32)[:, None] * inverse[None, :]
    angles = jnp.concatenate([angles, angles], axis=1)
    return (jnp.cos(angles), jnp.sin(angles))

def rotate(values, cosine_table, sine_table):
    half_rot = ROT // 2
    leading = values[..., :ROT]
    turned = jnp.concatenate([-leading[..., half_rot:], leading[..., :half_rot]], axis=-1)
    leading = leading * cosine_table[:, None, :] + turned * sine_table[:, None, :]
    return jnp.concatenate([leading, values[..., ROT:]], axis=-1)

def attention(queries, key_heads, value_heads):
    length = queries.shape[0]
    block_rows = min(512, length)
    score_scale = HD ** (-0.5)

    def one_block(block_index):
        first_row = block_index * block_rows
        picked = lax.dynamic_slice_in_dim(queries, first_row, block_rows, 0)
        scores = low_back(jnp.einsum('qhe,khe->hqk', picked, key_heads, precision=highest_precision) * score_scale)
        places = first_row + jnp.arange(block_rows, dtype=jnp.int32)
        allowed = jnp.arange(length, dtype=jnp.int32)[None, :] <= places[:, None]
        scores = jnp.where(allowed[None], scores, masked_score)
        row_top = lax.optimization_barrier(jnp.max(scores, axis=-1, keepdims=True))
        raised = jnp.exp(scores - row_top)
        weights = low(raised / lax.optimization_barrier(jnp.sum(raised, axis=-1, keepdims=True)))
        return jnp.einsum('hqk,khe->qhe', weights, value_heads, precision=highest_precision)
    pieces = lax.map(jax.checkpoint(one_block), jnp.arange(length // block_rows, dtype=jnp.int32))
    return pieces.reshape(length, queries.shape[1], queries.shape[2])

def block_forward(in_low, out_low, small_params, mix_weights, streams, earlier):
    groups = N_TENSOR
    heads_group = HEADS // groups
    units_group = FF // groups
    attn_width = heads_group * 3 * HD
    in_view = in_low.reshape(D, groups, attn_width + units_group)
    attn_weights = in_view[:, :, :attn_width].reshape(D, HEADS, 3, HD)
    up_weights = in_view[:, :, attn_width:].reshape(D, FF)
    out_view = out_low.reshape(D, groups, heads_group * HD + units_group)
    proj_weights = out_view[:, :, :heads_group * HD]
    down_weights = out_view[:, :, heads_group * HD:]
    up_rows = FF // D
    bias_qkv = small_params[5:8].reshape(3, HEADS, HD)
    bias_up = small_params[10:10 + up_rows].reshape(FF)
    mix_in = small_params[10 + up_rows:]
    length = streams.shape[1]
    norm_q = low(layer_norm(streams[0], small_params[0], small_params[1]))
    norm_k = low(layer_norm(streams[1], small_params[0], small_params[1]))
    norm_v = low(layer_norm(streams[2], small_params[0], small_params[1]))
    norm_r = low(layer_norm(streams[3], small_params[2], small_params[3]))
    cosine_table, sine_table = rope_tables(length)
    pre_q = low_back(jnp.einsum('ld,dhe->lhe', norm_q, attn_weights[:, :, 0], precision=highest_precision) + bias_qkv[0])
    pre_k = low_back(jnp.einsum('ld,dhe->lhe', norm_k, attn_weights[:, :, 1], precision=highest_precision) + bias_qkv[1])
    pre_v = low_back(jnp.einsum('ld,dhe->lhe', norm_v, attn_weights[:, :, 2], precision=highest_precision) + bias_qkv[2])
    queries = low(rotate(pre_q, cosine_table, sine_table))
    key_heads = low(rotate(pre_k, cosine_table, sine_table))
    value_heads = low(pre_v)
    attended = low(low_back(attention(queries, key_heads, value_heads)))
    up_pre = low_back(jnp.dot(norm_r, up_weights, precision=highest_precision) + bias_up)
    hidden = low(jax.nn.gelu(up_pre, approximate=False))
    group_terms = jnp.einsum('lgc,dgc->gld', attended.reshape(length, groups, heads_group * HD), proj_weights, precision=highest_precision) + jnp.einsum('lgc,dgc->gld', hidden.reshape(length, groups, units_group), down_weights, precision=highest_precision)
    branch = low_back(lax.optimization_barrier(jnp.sum(low(group_terms), axis=0)))
    newest = streams[3] + branch + small_params[8] + small_params[9]
    inv_rms = lax.rsqrt(lax.optimization_barrier(jnp.mean(newest * newest, axis=-1, keepdims=True)) + mix_eps)
    mix_normed = low(newest * inv_rms * small_params[4])
    mix_pre = low_back(jnp.dot(mix_normed, low(mix_in).T, precision=highest_precision))
    mixing_weights = jnp.dot(jax.nn.gelu(mix_pre, approximate=False), mix_weights[:MIXH], precision=highest_precision) + mix_weights[MIXH]
    mixing_weights = mixing_weights.reshape(length, STREAMS, LAYERS)
    every_layer = jnp.concatenate([earlier, newest[None]], axis=0)
    return jnp.einsum('wrx,xwf->rwf', mixing_weights, every_layer, precision=highest_precision)

def adamw_step(weight, moment, second, average, gradient, factor, rate):
    clipped = gradient * factor
    moment = beta_first * moment + (1.0 - beta_first) * clipped
    second = beta_second * second + (1.0 - beta_second) * clipped * clipped
    step_ratio = moment / (1.0 - beta_first ** STEP) / (jnp.sqrt(second / (1.0 - beta_second ** STEP)) + adam_eps)
    weight = weight - rate * (step_ratio + decay_rate * weight)
    average = average_keep * average + (1.0 - average_keep) * weight
    return (weight, moment, second, average)

def reference(in_streams, stored, cotangent, in_weights, in_moment, in_second, in_average, out_weights, out_moment, output_second_moment, out_average, small_params, small_moment, small_second, small_average, mix_weights, mix_moment, mix_second, mix_average):
    in_low = in_weights.astype(jnp.bfloat16).astype(jnp.float32)
    out_low = out_weights.astype(jnp.bfloat16).astype(jnp.float32)
    seq_count = TOKENS // LEN

    def by_sequence(source):
        return jnp.swapaxes(source.astype(jnp.float32).reshape(source.shape[0], seq_count, LEN, D), 0, 1)

    def one_sequence(totals, pieces):
        flow_seq, earlier_seq, back_seq = pieces
        result, pullback = jax.vjp(block_forward, in_low, out_low, small_params, mix_weights, flow_seq, earlier_seq)
        grads_all = pullback(back_seq)
        totals = tuple((total + part for total, part in zip(totals, grads_all[:4])))
        return (totals, (result, grads_all[4], grads_all[5]))
    zero_grads = (jnp.zeros_like(in_low), jnp.zeros_like(out_low), jnp.zeros_like(small_params), jnp.zeros_like(mix_weights))
    totals, (results, flow_grads, earlier_grads) = lax.scan(one_sequence, zero_grads, (by_sequence(in_streams), by_sequence(stored), by_sequence(cotangent)))

    def by_token(source):
        return jnp.swapaxes(source, 0, 1).reshape(source.shape[1], TOKENS, D)
    squares = sum((jnp.sum(part * part) for part in totals))
    grad_norm = jnp.sqrt(squares)
    factor = clip_norm / jnp.maximum(grad_norm, clip_norm)
    in_new = adamw_step(in_weights, in_moment, in_second, in_average, totals[0], factor, learn_rate)
    out_new = adamw_step(out_weights, out_moment, output_second_moment, out_average, totals[1], factor, learn_rate)
    small_new = adamw_step(small_params, small_moment, small_second, small_average, totals[2], factor, small_rate)
    mix_new = adamw_step(mix_weights, mix_moment, mix_second, mix_average, totals[3], factor, small_rate)
    return (by_token(results).astype(jnp.bfloat16), by_token(flow_grads).astype(jnp.bfloat16), by_token(earlier_grads).astype(jnp.bfloat16), grad_norm, in_new[0], in_new[1], in_new[2], in_new[3], in_new[0].astype(jnp.bfloat16), out_new[0], out_new[1], out_new[2], out_new[3], out_new[0].astype(jnp.bfloat16), small_new[0], small_new[1], small_new[2], small_new[3], mix_new[0], mix_new[1], mix_new[2], mix_new[3])
```

```python
import jax
import jax.numpy as jnp
from jax import lax
from jax.experimental import pallas as pl
from jax.experimental.pallas import tpu as pltpu
from jax.sharding import PartitionSpec as P

D = 2048
HEADS = 16
HD = 128
ROT = 32
FF = 8192
STREAMS = 4
LAYER = 8
STEP = 10
LAYERS = 9
MIXH = 36


norm_eps = 1e-05
mix_eps = 1e-06
beta_first = 0.9
beta_second = 0.95
adam_eps = 1e-08
decay_rate = 0.01
learn_rate = 0.03
small_rate = 0.2
clip_norm = 1.0
average_keep = 0.5
masked_score = -1e30
highest_precision = lax.Precision.HIGHEST
bfloat = jnp.bfloat16
single = jnp.float32
MESH = pl.DeviceIdType.MESH


def rope_tables(length):
    half_rot = ROT // 2
    exponent = jnp.arange(half_rot, dtype=jnp.float32) * (2.0 / ROT)
    inverse = 1.0 / 10000.0**exponent
    angles = jnp.arange(length, dtype=jnp.float32)[:, None] * inverse[None, :]
    angles = jnp.concatenate([angles, angles], axis=1)
    return (jnp.cos(angles), jnp.sin(angles))


def rotate(values, cosine_table, sine_table):
    half_rot = ROT // 2
    leading = values[..., :ROT]
    turned = jnp.concatenate([-leading[..., half_rot:], leading[..., :half_rot]], axis=-1)
    leading = leading * cosine_table[:, None, :] + turned * sine_table[:, None, :]
    return jnp.concatenate([leading, values[..., ROT:]], axis=-1)


def rotate_back(gradients, cosine_table, sine_table):
    half_rot = ROT // 2
    leading = gradients[..., :ROT]
    spun_part = leading * sine_table[:, None, :]
    turned = jnp.concatenate([spun_part[..., half_rot:], -spun_part[..., :half_rot]], axis=-1)
    leading = leading * cosine_table[:, None, :] + turned
    return jnp.concatenate([leading, gradients[..., ROT:]], axis=-1)


def gelu_value(values):
    return jax.nn.gelu(values, approximate=False)


def gelu_slope(values):
    normal_cdf = 0.5 * (1.0 + lax.erf(values * 0.7071067811865476))
    return normal_cdf + values * jnp.exp(-0.5 * values * values) * 0.3989422804014327


def contract_last(left_side, right_side):
    return lax.dot_general(
        left_side,
        right_side,
        (((left_side.ndim - 1,), (right_side.ndim - 1,)), ((), ())),
        preferred_element_type=single,
    )


def contract_first(left_side, right_side):
    return lax.dot_general(
        left_side, right_side, (((0,), (0,)), ((), ())), preferred_element_type=single
    )


def causal_mask(first_row, block_rows, length):
    places = first_row + jnp.arange(block_rows, dtype=jnp.int32)
    return jnp.arange(length, dtype=jnp.int32)[None, :] <= places[:, None]


def adamw_step(weight, moment, second, average, gradient, factor, rate):
    clipped = gradient * factor
    moment = beta_first * moment + (1.0 - beta_first) * clipped
    second = beta_second * second + (1.0 - beta_second) * clipped * clipped
    step_ratio = (
        moment
        / (1.0 - beta_first**STEP)
        / (jnp.sqrt(second / (1.0 - beta_second**STEP)) + adam_eps)
    )
    weight = weight - rate * (step_ratio + decay_rate * weight)
    average = average_keep * average + (1.0 - average_keep) * weight
    return (weight, moment, second, average)


def enter(partners):
    barrier = pltpu.get_barrier_semaphore()
    for present, device in partners:

        @pl.when(present)
        def _():
            pl.semaphore_signal(barrier, inc=1, device_id=device, device_id_type=MESH)

    pl.semaphore_wait(barrier, sum(present.astype(jnp.int32) for present, _ in partners))


def row_chunks(streams, rows, cut):
    return [(s, r, rows // cut) for s in range(streams) for r in range(0, rows, rows // cut)]


def line_gather_kernel(size, chunks, own, out, send_sem, recv_sem, local_sem):
    here = lax.axis_index("tensor")
    sides = ((0, 1), (1, -1))
    enter([(here < size - 1, {"tensor": here + 1}), (here > 0, {"tensor": here - 1})])

    def onward(side, way, step, place):
        s, r, n = chunks[place]
        origin = here - way * step
        target = out.at[s, origin, pl.ds(r, n)]
        return pltpu.make_async_remote_copy(
            src_ref=own.at[s, pl.ds(r, n)] if step == 0 else target,
            dst_ref=target,
            send_sem=send_sem.at[side, step, place],
            recv_sem=recv_sem.at[side, step, place],
            device_id={"tensor": here + way},
            device_id_type=MESH,
        )

    def has_next(way):
        return here < size - 1 if way > 0 else here > 0

    def has_origin(way, step):
        return here >= step if way > 0 else here < size - step

    for place in range(len(chunks)):
        for side, way in sides:
            pl.when(has_next(way))(onward(side, way, 0, place).start)
    local = pltpu.make_async_copy(own, out.at[:, here], local_sem)
    local.start()
    for step in range(1, size):
        for place in range(len(chunks)):
            for side, way in sides:

                @pl.when(has_origin(way, step))
                def _():
                    s, r, n = chunks[place]
                    landed = out.at[s, here - way * step, pl.ds(r, n)]
                    pltpu.make_async_remote_copy(
                        src_ref=landed,
                        dst_ref=landed,
                        send_sem=send_sem.at[side, step - 1, place],
                        recv_sem=recv_sem.at[side, step - 1, place],
                        device_id={"tensor": here - way},
                        device_id_type=MESH,
                    ).wait_recv()
                    pl.when(has_next(way))(onward(side, way, step, place).start)

    for step in range(size):
        for place in range(len(chunks)):
            for side, way in sides:

                @pl.when(jnp.logical_and(has_next(way), has_origin(way, step)))
                def _():
                    onward(side, way, step, place).wait_send()

    local.wait()


def line_gather(own, size, cut, identity):
    streams, rows, width = own.shape
    chunks = row_chunks(streams, rows, cut)
    return pl.pallas_call(
        lambda *refs: line_gather_kernel(size, chunks, *refs),
        out_shape=jax.ShapeDtypeStruct((streams, size, rows, width), own.dtype),
        in_specs=[pl.BlockSpec(memory_space=pl.ANY)],
        out_specs=pl.BlockSpec(memory_space=pl.ANY),
        scratch_shapes=[
            pltpu.SemaphoreType.DMA((2, size, len(chunks))),
            pltpu.SemaphoreType.DMA((2, size, len(chunks))),
            pltpu.SemaphoreType.DMA,
        ],
        compiler_params=pltpu.CompilerParams(collective_id=identity, has_side_effects=True),
        cost_estimate=pl.CostEstimate(
            flops=0, bytes_accessed=size * own.size * 40, transcendentals=0
        ),
        name="line_gather_%d" % identity,
    )(own)


def line_scatter_kernel(size, chunks, parts, out, held, left, right, load_sem, send_sem, recv_sem):
    here = lax.axis_index("tensor")
    enter([(here < size - 1, {"tensor": here + 1}), (here > 0, {"tensor": here - 1})])
    sides = ((0, 1, left), (1, -1, right))

    def has_next(way):
        return here < size - 1 if way > 0 else here > 0

    def load(place, dest):
        s, r, n = chunks[place]
        return pltpu.make_async_copy(
            parts.at[s, dest, pl.ds(r, n)],
            held.at[s, dest, pl.ds(r, n)],
            load_sem.at[dest, place],
        )

    def onward(side, way, dest, place, landing):
        s, r, n = chunks[place]
        return pltpu.make_async_remote_copy(
            src_ref=held.at[s, dest, pl.ds(r, n)],
            dst_ref=landing.at[s, dest, pl.ds(r, n)],
            send_sem=send_sem.at[side, dest, place],
            recv_sem=recv_sem.at[side, dest, place],
            device_id={"tensor": here + way},
            device_id_type=MESH,
        )

    def arrived(side, way, dest, place, landing):
        s, r, n = chunks[place]
        spot = landing.at[s, dest, pl.ds(r, n)]
        pltpu.make_async_remote_copy(
            src_ref=spot,
            dst_ref=spot,
            send_sem=send_sem.at[side, dest, place],
            recv_sem=recv_sem.at[side, dest, place],
            device_id={"tensor": here - way},
            device_id_type=MESH,
        ).wait_recv()

    def reach(way, far):
        return here + far < size if way > 0 else here >= far

    for far in range(size - 1, -1, -1):
        for place in range(len(chunks)):
            for side, way, landing in sides[: 2 if far else 1]:
                pl.when(reach(way, far))(load(place, here + way * far).start)
    for far in range(size - 1, 0, -1):
        for place in range(len(chunks)):
            for side, way, landing in sides:

                @pl.when(reach(way, far))
                def _():
                    s, r, n = chunks[place]
                    dest = here + way * far
                    load(place, dest).wait()

                    @pl.when(has_next(-way))
                    def _():
                        arrived(side, way, dest, place, landing)
                        spot = (s, dest, pl.ds(r, n))
                        held[spot] = (
                            held[spot].astype(single) + landing[spot].astype(single)
                        ).astype(held.dtype)

                    onward(side, way, dest, place, landing).start()

    for place in range(len(chunks)):
        s, r, n = chunks[place]
        load(place, here).wait()
        spot = (s, here, pl.ds(r, n))
        out[s, pl.ds(r, n)] = held[spot].astype(single)
        for side, way, landing in sides:

            @pl.when(has_next(-way))
            def _():
                arrived(side, way, here, place, landing)
                out[s, pl.ds(r, n)] += landing[spot].astype(single)

    for far in range(size - 1, 0, -1):
        for place in range(len(chunks)):
            for side, way, landing in sides:
                pl.when(reach(way, far))(
                    onward(side, way, here + way * far, place, landing).wait_send
                )


def line_scatter(parts, size, cut, identity):
    streams, _, rows, width = parts.shape
    chunks = row_chunks(streams, rows, cut)
    return pl.pallas_call(
        lambda *refs: line_scatter_kernel(size, chunks, *refs),
        out_shape=jax.ShapeDtypeStruct((streams, rows, width), single),
        in_specs=[pl.BlockSpec(memory_space=pl.ANY)],
        out_specs=pl.BlockSpec(memory_space=pltpu.VMEM),
        scratch_shapes=[pltpu.VMEM(parts.shape, parts.dtype) for _ in range(3)]
        + [
            pltpu.SemaphoreType.DMA((size, len(chunks))),
            pltpu.SemaphoreType.DMA((2, size, len(chunks))),
            pltpu.SemaphoreType.DMA((2, size, len(chunks))),
        ],
        compiler_params=pltpu.CompilerParams(
            collective_id=identity, has_side_effects=True, vmem_limit_bytes=56 * 2**20
        ),
        cost_estimate=pl.CostEstimate(
            flops=0, bytes_accessed=parts.size * 40, transcendentals=0
        ),
        name="line_scatter_%d" % identity,
    )(parts)


def cube_sum_kernel(bits, value, out, total, landing, send_a, recv_a, send_b, recv_b):
    rows, columns = value.shape

    def partner(axis, size):
        place = lax.axis_index(axis)
        bit = lax.rem(place // size, 2)
        return bit, {axis: place + (1 - 2 * bit) * size}

    ends = [partner(*entry) for entry in bits]
    enter([(jnp.bool_(True), device) for _, device in ends])
    total[...] = value[...]
    regions = [(0, rows, 0, columns)]
    for step, (bit, device) in enumerate(ends):
        r, n, c, m = regions[-1]
        if n > 8:
            n = n // 2
            keep, give = (r + bit * n, n, c, m), (r + (1 - bit) * n, n, c, m)
        else:
            m = m // 2
            keep, give = (r, n, c + bit * m, m), (r, n, c + (1 - bit) * m, m)
        regions.append(keep)

        def spot(region):
            return (
                pl.ds(pl.multiple_of(region[0], 8), region[1]),
                pl.ds(pl.multiple_of(region[2], 128), region[3]),
            )

        copy = pltpu.make_async_remote_copy(
            src_ref=total.at[spot(give)],
            dst_ref=landing.at[step, pl.ds(0, n), pl.ds(0, m)],
            send_sem=send_a.at[step],
            recv_sem=recv_a.at[step],
            device_id=device,
            device_id_type=MESH,
        )
        copy.start()
        copy.wait()
        total[spot(keep)] += landing[step, pl.ds(0, n), pl.ds(0, m)]
    out[spot(regions[-1])] = total[spot(regions[-1])]
    for step in range(len(ends) - 1, -1, -1):
        region = out.at[spot(regions[step + 1])]
        copy = pltpu.make_async_remote_copy(
            src_ref=region,
            dst_ref=region,
            send_sem=send_b.at[step],
            recv_sem=recv_b.at[step],
            device_id=ends[step][1],
            device_id_type=MESH,
        )
        copy.start()
        copy.wait()


def cube_sum(value, bits, identity):
    steps = len(bits)
    rows, columns = value.shape
    return pl.pallas_call(
        lambda *refs: cube_sum_kernel(bits, *refs),
        out_shape=jax.ShapeDtypeStruct(value.shape, value.dtype),
        in_specs=[pl.BlockSpec(memory_space=pltpu.VMEM)],
        out_specs=pl.BlockSpec(memory_space=pltpu.VMEM),
        scratch_shapes=[
            pltpu.VMEM(value.shape, value.dtype),
            pltpu.VMEM((steps, rows // 2, columns), value.dtype),
        ]
        + [pltpu.SemaphoreType.DMA((steps,))] * 4,
        compiler_params=pltpu.CompilerParams(
            collective_id=identity, has_side_effects=True, vmem_limit_bytes=32 * 2**20
        ),
        name="cube_sum_%d" % identity,
    )(value)


def axis_bits(axis):
    return [(axis, 2**bit) for bit in range(lax.axis_size(axis).bit_length() - 1)]


def shards(
    in_streams,
    stored,
    cotangent,
    in_weights,
    in_moment,
    in_second,
    in_average,
    out_weights,
    out_moment,
    output_second_moment,
    out_average,
    small_params,
    small_moment,
    small_second,
    small_average,
    mix_weights,
    mix_moment,
    mix_second,
    mix_average,
):
    groups = lax.axis_size("tensor")
    group_index = lax.axis_index("tensor")
    heads_group = HEADS // groups
    units_group = FF // groups
    attn_width = heads_group * 3 * HD
    proj_width = heads_group * HD
    own_rows = in_streams.shape[1]
    length = own_rows * groups
    up_rows = FF // D
    block_rows = min(512, length)
    block_count = length // block_rows
    score_scale = HD ** (-0.5)
    shard_rows = D // lax.axis_size("dp")
    full_in, full_out = (
        lax.all_gather(in_weights.astype(bfloat), "dp", axis=0, tiled=True),
        lax.all_gather(out_weights.astype(bfloat), "dp", axis=0, tiled=True),
    )
    gain_mix = small_params[4]
    bias_heads = lax.dynamic_slice_in_dim(
        small_params[5:8].reshape(3, HEADS, HD), group_index * heads_group, heads_group, 1
    )
    bias_units = lax.dynamic_slice_in_dim(
        small_params[10 : 10 + up_rows].reshape(FF), group_index * units_group, units_group, 0
    )
    mix_low = small_params[10 + up_rows :].astype(bfloat)
    flow_rows = in_streams.astype(single)
    centred = flow_rows - jnp.mean(flow_rows, axis=-1, keepdims=True)
    inverse = lax.rsqrt(jnp.mean(centred * centred, axis=-1, keepdims=True) + norm_eps)
    unit_flows = centred * inverse
    gain_all = jnp.stack([small_params[0], small_params[0], small_params[0], small_params[2]])[
        :, None, :
    ]
    shift_all = jnp.stack([small_params[1], small_params[1], small_params[1], small_params[3]])[
        :, None, :
    ]
    normed_own = (unit_flows * gain_all + shift_all).astype(bfloat)
    normed = line_gather(normed_own, groups, 1, 0).reshape(STREAMS, length, D)
    attn_weights = full_in[:, :attn_width].reshape(D, heads_group, 3, HD)
    up_weights = full_in[:, attn_width:]
    cosine_table, sine_table = rope_tables(length)

    def project(part_index):
        return (
            jnp.einsum(
                "ld,dhe->lhe",
                normed[part_index],
                attn_weights[:, :, part_index, :],
                preferred_element_type=single,
            )
            + bias_heads[part_index][None]
        )

    queries = rotate(project(0), cosine_table, sine_table).astype(bfloat)
    key_heads = rotate(project(1), cosine_table, sine_table).astype(bfloat)
    value_heads = project(2).astype(bfloat)
    up_pre = jnp.dot(normed[3], up_weights, preferred_element_type=single) + bias_units
    hidden = gelu_value(up_pre).astype(bfloat)

    def forward_block(block_index):
        first_row = block_index * block_rows
        scores = (
            jnp.einsum("qhe,khe->hqk", queries, key_heads, preferred_element_type=single)
            * score_scale
        )
        scores = jnp.where(causal_mask(first_row, block_rows, length)[None], scores, masked_score)
        row_top = jnp.max(scores, axis=-1, keepdims=True)
        raised = jnp.exp(scores - row_top)
        row_sum = jnp.sum(raised, axis=-1, keepdims=True)
        weights_low = (raised / row_sum).astype(bfloat)
        mixed_heads = jnp.einsum(
            "hqk,khe->qhe", weights_low, value_heads, preferred_element_type=single
        )
        return (mixed_heads, (row_top + jnp.log(row_sum))[..., 0])

    attended, log_sums = lax.map(forward_block, jnp.arange(block_count, dtype=jnp.int32))
    attended = attended.reshape(length, heads_group, HD).astype(bfloat)
    joined = jnp.concatenate([attended.reshape(length, proj_width), hidden], axis=1)
    partial_value = contract_last(joined, full_out)
    branch = line_scatter(
        partial_value.astype(bfloat).reshape(1, groups, own_rows, D), groups, 4, 1
    )[0]
    newest = flow_rows[3] + branch + small_params[8] + small_params[9]
    inv_rms = lax.rsqrt(jnp.mean(newest * newest, axis=-1, keepdims=True) + mix_eps)
    mix_normed = (newest * inv_rms * gain_mix).astype(bfloat)
    mix_pre = contract_last(mix_normed, mix_low)
    mixing_activation = gelu_value(mix_pre)
    mixing_weights = (
        jnp.dot(mixing_activation, mix_weights[:MIXH], precision=highest_precision)
        + mix_weights[MIXH]
    )
    mixing_weights = mixing_weights.reshape(own_rows, STREAMS, LAYERS)
    composed = mixing_weights[:, :, LAYER].T[:, :, None] * newest[None]
    for layer_index in range(LAYER):
        composed = (
            composed
            + mixing_weights[:, :, layer_index].T[:, :, None]
            * stored[layer_index].astype(single)[None]
        )
    out_streams = composed.astype(bfloat)
    back_flows = cotangent.astype(single)
    d_stored = jnp.einsum("srd,jrd->rsj", cotangent, stored, preferred_element_type=single)
    d_newest_col = jnp.einsum("srd,rd->rs", back_flows, newest, precision=highest_precision)
    d_mixing = jnp.concatenate([d_stored, d_newest_col[:, :, None]], axis=2).reshape(own_rows, MIXH)
    spread_gradient = jnp.einsum(
        "rsj,srd->jrd", mixing_weights, back_flows, precision=highest_precision
    )
    grad_stored = spread_gradient[:LAYER].astype(bfloat)
    d_act = jnp.dot(d_mixing, mix_weights[:MIXH].T, precision=highest_precision)
    grad_mix_out = jnp.dot(mixing_activation.T, d_mixing, precision=highest_precision)
    grad_mix_bias = jnp.sum(d_mixing, axis=0)
    d_mix_pre = (d_act * gelu_slope(mix_pre)).astype(bfloat)
    grad_mix_in = contract_first(d_mix_pre, mix_normed)
    d_mix_normed = jnp.dot(d_mix_pre, mix_low, preferred_element_type=single)
    scaled_back = d_mix_normed * gain_mix
    grad_gain_mix = jnp.sum(d_mix_normed * newest * inv_rms, axis=0)
    d_newest = (
        spread_gradient[LAYER]
        + inv_rms * scaled_back
        - newest * inv_rms**3 * jnp.mean(scaled_back * newest, axis=-1, keepdims=True)
    )
    grad_bias_out = jnp.sum(d_newest, axis=0)
    branch_grads = line_gather(d_newest.astype(bfloat)[None], groups, 4, 2).reshape(length, D)
    d_joined = jnp.dot(branch_grads, full_out, preferred_element_type=single)
    d_attended = d_joined[:, :proj_width].reshape(length, heads_group, HD).astype(bfloat)
    d_up = (d_joined[:, proj_width:] * gelu_slope(up_pre)).astype(bfloat)

    def backward_block(carried, block_index):
        key_sum, value_sum = carried
        first_row = block_index * block_rows
        scores = (
            jnp.einsum("qhe,khe->hqk", queries, key_heads, preferred_element_type=single)
            * score_scale
        )
        scores = jnp.where(causal_mask(first_row, block_rows, length)[None], scores, masked_score)
        chances = jnp.exp(scores - log_sums[block_index][..., None])
        chances_low = chances.astype(bfloat)
        d_chances = jnp.einsum(
            "qhe,khe->hqk", d_attended, value_heads, preferred_element_type=single
        )
        centre = jnp.sum(d_chances * chances, axis=-1, keepdims=True)
        d_scores = (chances * (d_chances - centre)).astype(bfloat)
        d_picked = (
            jnp.einsum("hqk,khe->qhe", d_scores, key_heads, preferred_element_type=single)
            * score_scale
        )
        key_sum = (
            key_sum
            + jnp.einsum("hqk,qhe->khe", d_scores, queries, preferred_element_type=single)
            * score_scale
        )
        value_sum = value_sum + jnp.einsum(
            "hqk,qhe->khe", chances_low, d_attended, preferred_element_type=single
        )
        return ((key_sum, value_sum), d_picked)

    zero_heads = jnp.zeros((length, heads_group, HD), single)
    (d_key_heads, value_head_gradient), d_queries = lax.scan(
        backward_block, (zero_heads, zero_heads), jnp.arange(block_count, dtype=jnp.int32)
    )
    d_queries = d_queries.reshape(length, heads_group, HD)
    d_pre_q = rotate_back(d_queries, cosine_table, sine_table).astype(bfloat)
    d_pre_k = rotate_back(d_key_heads, cosine_table, sine_table).astype(bfloat)
    d_pre_v = value_head_gradient.astype(bfloat)
    d_pres = jnp.stack([d_pre_q, d_pre_k, d_pre_v], axis=2)
    bias_grads = jnp.sum(d_pres, axis=0, dtype=single)
    unit_grads = jnp.sum(d_up, axis=0, dtype=single)
    d_norm_parts = [
        jnp.einsum(
            "lhe,dhe->ld",
            d_pres[:, :, part_index],
            attn_weights[:, :, part_index, :],
            preferred_element_type=single,
        )
        for part_index in range(3)
    ]
    d_norm_parts.append(contract_last(d_up, up_weights))
    d_normed = jnp.stack(d_norm_parts)
    d_own = line_scatter(
        d_normed.astype(bfloat).reshape(STREAMS, groups, own_rows, D), groups, 1, 3
    )
    d_unit = d_own * gain_all
    d_flows = inverse * (
        d_unit
        - jnp.mean(d_unit, axis=-1, keepdims=True)
        - unit_flows * jnp.mean(d_unit * unit_flows, axis=-1, keepdims=True)
    )
    grad_streams = jnp.concatenate([d_flows[:3], (d_flows[3] + d_newest)[None]], axis=0).astype(
        bfloat
    )
    gain_grads = jnp.sum(d_own * unit_flows, axis=1)
    shift_grads = jnp.sum(d_own, axis=1)
    head_rows = lax.dynamic_update_slice_in_dim(
        jnp.zeros((HEADS, 3, HD), single), bias_grads, group_index * heads_group, 0
    )
    head_rows = jnp.transpose(head_rows, (1, 0, 2)).reshape(3, D)
    unit_full = lax.dynamic_update_slice_in_dim(
        jnp.zeros((FF,), single), unit_grads, group_index * units_group, 0
    )
    small_grad = jnp.concatenate(
        [
            jnp.stack(
                [
                    gain_grads[0] + gain_grads[1] + gain_grads[2],
                    shift_grads[0] + shift_grads[1] + shift_grads[2],
                    gain_grads[3],
                    shift_grads[3],
                    grad_gain_mix,
                ]
            ),
            head_rows,
            jnp.stack([grad_bias_out, grad_bias_out]),
            unit_full.reshape(up_rows, D),
            grad_mix_in,
        ],
        axis=0,
    )
    mix_grad = jnp.concatenate([grad_mix_out, grad_mix_bias[None]], axis=0)
    attn_part = jnp.einsum(
        "pld,lhpe->dhpe", normed[:3], d_pres, preferred_element_type=single
    ).reshape(D, attn_width)
    up_part = contract_first(normed[3], d_up)

    def owned(part):
        return lax.psum_scatter(
            part.astype(bfloat), "dp", scatter_dimension=0, tiled=True
        ).astype(single)

    grad_out = owned(contract_first(branch_grads, joined))
    grad_in = owned(jnp.concatenate([attn_part, up_part], axis=1))
    big_square = jnp.sum(grad_in * grad_in) + jnp.sum(grad_out * grad_out)
    small_rows = small_grad.shape[0]
    mix_row = jnp.concatenate([mix_grad.reshape(-1), big_square[None]])
    mix_row = jnp.pad(mix_row, (0, D - mix_row.shape[0]))
    packed = jnp.concatenate(
        [small_grad, mix_row[None], jnp.zeros((63 - small_rows, D), single)], axis=0
    )
    packed = cube_sum(packed, axis_bits("dp") + axis_bits("tensor"), 4)
    small_parameter_total = packed[:small_rows]
    mix_total = packed[small_rows, : mix_grad.size].reshape(mix_grad.shape)
    big_total = packed[small_rows, mix_grad.size]
    grad_norm = jnp.sqrt(
        big_total
        + jnp.sum(small_parameter_total * small_parameter_total)
        + jnp.sum(mix_total * mix_total)
    )
    factor = clip_norm / jnp.maximum(grad_norm, clip_norm)
    in_new = adamw_step(in_weights, in_moment, in_second, in_average, grad_in, factor, learn_rate)
    out_new = adamw_step(
        out_weights, out_moment, output_second_moment, out_average, grad_out, factor, learn_rate
    )
    small_new = adamw_step(
        small_params,
        small_moment,
        small_second,
        small_average,
        small_parameter_total,
        factor,
        small_rate,
    )
    mix_new = adamw_step(
        mix_weights, mix_moment, mix_second, mix_average, mix_total, factor, small_rate
    )
    return (
        out_streams,
        grad_streams,
        grad_stored,
        grad_norm,
        in_new[0],
        in_new[1],
        in_new[2],
        in_new[3],
        in_new[0].astype(bfloat),
        out_new[0],
        out_new[1],
        out_new[2],
        out_new[3],
        out_new[0].astype(bfloat),
        small_new[0],
        small_new[1],
        small_new[2],
        small_new[3],
        mix_new[0],
        mix_new[1],
        mix_new[2],
        mix_new[3],
    )


def solution(mesh):
    in_specs = (
        P(None, ("dp", "tensor"), None),
        P(None, ("dp", "tensor"), None),
        P(None, ("dp", "tensor"), None),
        P("dp", "tensor"),
        P("dp", "tensor"),
        P("dp", "tensor"),
        P("dp", "tensor"),
        P("dp", "tensor"),
        P("dp", "tensor"),
        P("dp", "tensor"),
        P("dp", "tensor"),
        P(),
        P(),
        P(),
        P(),
        P(),
        P(),
        P(),
        P(),
    )
    out_specs = (
        P(None, ("dp", "tensor"), None),
        P(None, ("dp", "tensor"), None),
        P(None, ("dp", "tensor"), None),
        P(),
        P("dp", "tensor"),
        P("dp", "tensor"),
        P("dp", "tensor"),
        P("dp", "tensor"),
        P("dp", "tensor"),
        P("dp", "tensor"),
        P("dp", "tensor"),
        P("dp", "tensor"),
        P("dp", "tensor"),
        P("dp", "tensor"),
        P(),
        P(),
        P(),
        P(),
        P(),
        P(),
        P(),
        P(),
    )
    return jax.shard_map(shards, mesh=mesh, in_specs=in_specs, out_specs=out_specs, check_vma=False)
```

```python
import jax
import jax.numpy as jnp
from jax import lax
from jax.experimental import pallas as pl
from jax.experimental.pallas import tpu as pltpu
from jax.sharding import PartitionSpec as P

D = 2048
HEADS = 16
HD = 128
ROT = 32
FF = 8192
STREAMS = 4
LAYER = 8
STEP = 10
LAYERS = 9
MIXH = 36


norm_eps = 1e-05
mix_eps = 1e-06
beta_first = 0.9
beta_second = 0.95
adam_eps = 1e-08
decay_rate = 0.01
learn_rate = 0.03
small_rate = 0.2
clip_norm = 1.0
average_keep = 0.5
masked_score = -1e30
highest_precision = lax.Precision.HIGHEST
bfloat = jnp.bfloat16
single = jnp.float32
MESH = pl.DeviceIdType.MESH


def rope_tables(length):
    half_rot = ROT // 2
    exponent = jnp.arange(half_rot, dtype=jnp.float32) * (2.0 / ROT)
    inverse = 1.0 / 10000.0**exponent
    angles = jnp.arange(length, dtype=jnp.float32)[:, None] * inverse[None, :]
    angles = jnp.concatenate([angles, angles], axis=1)
    return (jnp.cos(angles), jnp.sin(angles))


def rotate(values, cosine_table, sine_table):
    half_rot = ROT // 2
    leading = values[..., :ROT]
    turned = jnp.concatenate([-leading[..., half_rot:], leading[..., :half_rot]], axis=-1)
    leading = leading * cosine_table[:, None, :] + turned * sine_table[:, None, :]
    return jnp.concatenate([leading, values[..., ROT:]], axis=-1)


def rotate_back(gradients, cosine_table, sine_table):
    half_rot = ROT // 2
    leading = gradients[..., :ROT]
    spun_part = leading * sine_table[:, None, :]
    turned = jnp.concatenate([spun_part[..., half_rot:], -spun_part[..., :half_rot]], axis=-1)
    leading = leading * cosine_table[:, None, :] + turned
    return jnp.concatenate([leading, gradients[..., ROT:]], axis=-1)


def gelu_value(values):
    return jax.nn.gelu(values, approximate=False)


def gelu_slope(values):
    normal_cdf = 0.5 * (1.0 + lax.erf(values * 0.7071067811865476))
    return normal_cdf + values * jnp.exp(-0.5 * values * values) * 0.3989422804014327


def contract_last(left_side, right_side):
    return lax.dot_general(
        left_side,
        right_side,
        (((left_side.ndim - 1,), (right_side.ndim - 1,)), ((), ())),
        preferred_element_type=single,
    )


def contract_first(left_side, right_side):
    return lax.dot_general(
        left_side, right_side, (((0,), (0,)), ((), ())), preferred_element_type=single
    )


def causal_mask(first_row, block_rows, length):
    places = first_row + jnp.arange(block_rows, dtype=jnp.int32)
    return jnp.arange(length, dtype=jnp.int32)[None, :] <= places[:, None]


def adamw_step(weight, moment, second, average, gradient, factor, rate):
    clipped = gradient * factor
    moment = beta_first * moment + (1.0 - beta_first) * clipped
    second = beta_second * second + (1.0 - beta_second) * clipped * clipped
    step_ratio = (
        moment
        / (1.0 - beta_first**STEP)
        / (jnp.sqrt(second / (1.0 - beta_second**STEP)) + adam_eps)
    )
    weight = weight - rate * (step_ratio + decay_rate * weight)
    average = average_keep * average + (1.0 - average_keep) * weight
    return (weight, moment, second, average)


def enter(partners):
    barrier = pltpu.get_barrier_semaphore()
    for present, device in partners:

        @pl.when(present)
        def _():
            pl.semaphore_signal(barrier, inc=1, device_id=device, device_id_type=MESH)

    pl.semaphore_wait(barrier, sum(present.astype(jnp.int32) for present, _ in partners))


def row_chunks(streams, rows, cut):
    return [(s, r, rows // cut) for s in range(streams) for r in range(0, rows, rows // cut)]


def line_gather_kernel(size, chunks, own, out, send_sem, recv_sem, local_sem):
    here = lax.axis_index("tensor")
    sides = ((0, 1), (1, -1))
    enter([(here < size - 1, {"tensor": here + 1}), (here > 0, {"tensor": here - 1})])

    def onward(side, way, step, place):
        s, r, n = chunks[place]
        origin = here - way * step
        target = out.at[s, origin, pl.ds(r, n)]
        return pltpu.make_async_remote_copy(
            src_ref=own.at[s, pl.ds(r, n)] if step == 0 else target,
            dst_ref=target,
            send_sem=send_sem.at[side, step, place],
            recv_sem=recv_sem.at[side, step, place],
            device_id={"tensor": here + way},
            device_id_type=MESH,
        )

    def has_next(way):
        return here < size - 1 if way > 0 else here > 0

    def has_origin(way, step):
        return here >= step if way > 0 else here < size - step

    for place in range(len(chunks)):
        for side, way in sides:
            pl.when(has_next(way))(onward(side, way, 0, place).start)
    local = pltpu.make_async_copy(own, out.at[:, here], local_sem)
    local.start()
    for step in range(1, size):
        for place in range(len(chunks)):
            for side, way in sides:

                @pl.when(has_origin(way, step))
                def _():
                    s, r, n = chunks[place]
                    landed = out.at[s, here - way * step, pl.ds(r, n)]
                    pltpu.make_async_remote_copy(
                        src_ref=landed,
                        dst_ref=landed,
                        send_sem=send_sem.at[side, step - 1, place],
                        recv_sem=recv_sem.at[side, step - 1, place],
                        device_id={"tensor": here - way},
                        device_id_type=MESH,
                    ).wait_recv()
                    pl.when(has_next(way))(onward(side, way, step, place).start)

    for step in range(size):
        for place in range(len(chunks)):
            for side, way in sides:

                @pl.when(jnp.logical_and(has_next(way), has_origin(way, step)))
                def _():
                    onward(side, way, step, place).wait_send()

    local.wait()


def line_gather(own, size, cut, identity):
    streams, rows, width = own.shape
    chunks = row_chunks(streams, rows, cut)
    return pl.pallas_call(
        lambda *refs: line_gather_kernel(size, chunks, *refs),
        out_shape=jax.ShapeDtypeStruct((streams, size, rows, width), own.dtype),
        in_specs=[pl.BlockSpec(memory_space=pl.ANY)],
        out_specs=pl.BlockSpec(memory_space=pl.ANY),
        scratch_shapes=[
            pltpu.SemaphoreType.DMA((2, size, len(chunks))),
            pltpu.SemaphoreType.DMA((2, size, len(chunks))),
            pltpu.SemaphoreType.DMA,
        ],
        compiler_params=pltpu.CompilerParams(collective_id=identity, has_side_effects=True),
        cost_estimate=pl.CostEstimate(
            flops=0, bytes_accessed=size * own.size * 40, transcendentals=0
        ),
        name="line_gather_%d" % identity,
    )(own)


def line_scatter_kernel(size, chunks, parts, out, held, left, right, load_sem, send_sem, recv_sem):
    here = lax.axis_index("tensor")
    enter([(here < size - 1, {"tensor": here + 1}), (here > 0, {"tensor": here - 1})])
    sides = ((0, 1, left), (1, -1, right))

    def has_next(way):
        return here < size - 1 if way > 0 else here > 0

    def load(place, dest):
        s, r, n = chunks[place]
        return pltpu.make_async_copy(
            parts.at[s, dest, pl.ds(r, n)],
            held.at[s, dest, pl.ds(r, n)],
            load_sem.at[dest, place],
        )

    def onward(side, way, dest, place, landing):
        s, r, n = chunks[place]
        return pltpu.make_async_remote_copy(
            src_ref=held.at[s, dest, pl.ds(r, n)],
            dst_ref=landing.at[s, dest, pl.ds(r, n)],
            send_sem=send_sem.at[side, dest, place],
            recv_sem=recv_sem.at[side, dest, place],
            device_id={"tensor": here + way},
            device_id_type=MESH,
        )

    def arrived(side, way, dest, place, landing):
        s, r, n = chunks[place]
        spot = landing.at[s, dest, pl.ds(r, n)]
        pltpu.make_async_remote_copy(
            src_ref=spot,
            dst_ref=spot,
            send_sem=send_sem.at[side, dest, place],
            recv_sem=recv_sem.at[side, dest, place],
            device_id={"tensor": here - way},
            device_id_type=MESH,
        ).wait_recv()

    def reach(way, far):
        return here + far < size if way > 0 else here >= far

    for far in range(size - 1, -1, -1):
        for place in range(len(chunks)):
            for side, way, landing in sides[: 2 if far else 1]:
                pl.when(reach(way, far))(load(place, here + way * far).start)
    for far in range(size - 1, 0, -1):
        for place in range(len(chunks)):
            for side, way, landing in sides:

                @pl.when(reach(way, far))
                def _():
                    s, r, n = chunks[place]
                    dest = here + way * far
                    load(place, dest).wait()

                    @pl.when(has_next(-way))
                    def _():
                        arrived(side, way, dest, place, landing)
                        spot = (s, dest, pl.ds(r, n))
                        held[spot] = (
                            held[spot].astype(single) + landing[spot].astype(single)
                        ).astype(held.dtype)

                    onward(side, way, dest, place, landing).start()

    for place in range(len(chunks)):
        s, r, n = chunks[place]
        load(place, here).wait()
        spot = (s, here, pl.ds(r, n))
        out[s, pl.ds(r, n)] = held[spot].astype(single)
        for side, way, landing in sides:

            @pl.when(has_next(-way))
            def _():
                arrived(side, way, here, place, landing)
                out[s, pl.ds(r, n)] += landing[spot].astype(single)

    for far in range(size - 1, 0, -1):
        for place in range(len(chunks)):
            for side, way, landing in sides:
                pl.when(reach(way, far))(
                    onward(side, way, here + way * far, place, landing).wait_send
                )


def line_scatter(parts, size, cut, identity):
    streams, _, rows, width = parts.shape
    chunks = row_chunks(streams, rows, cut)
    return pl.pallas_call(
        lambda *refs: line_scatter_kernel(size, chunks, *refs),
        out_shape=jax.ShapeDtypeStruct((streams, rows, width), single),
        in_specs=[pl.BlockSpec(memory_space=pl.ANY)],
        out_specs=pl.BlockSpec(memory_space=pltpu.VMEM),
        scratch_shapes=[pltpu.VMEM(parts.shape, parts.dtype) for _ in range(3)]
        + [
            pltpu.SemaphoreType.DMA((size, len(chunks))),
            pltpu.SemaphoreType.DMA((2, size, len(chunks))),
            pltpu.SemaphoreType.DMA((2, size, len(chunks))),
        ],
        compiler_params=pltpu.CompilerParams(
            collective_id=identity, has_side_effects=True, vmem_limit_bytes=56 * 2**20
        ),
        cost_estimate=pl.CostEstimate(
            flops=0, bytes_accessed=parts.size * 40, transcendentals=0
        ),
        name="line_scatter_%d" % identity,
    )(parts)


def cube_sum_kernel(bits, value, out, total, landing, send_a, recv_a, send_b, recv_b):
    rows, columns = value.shape

    def partner(axis, size):
        place = lax.axis_index(axis)
        bit = lax.rem(place // size, 2)
        return bit, {axis: place + (1 - 2 * bit) * size}

    ends = [partner(*entry) for entry in bits]
    enter([(jnp.bool_(True), device) for _, device in ends])
    total[...] = value[...]
    regions = [(0, rows, 0, columns)]
    for step, (bit, device) in enumerate(ends):
        r, n, c, m = regions[-1]
        if n > 8:
            n = n // 2
            keep, give = (r + bit * n, n, c, m), (r + (1 - bit) * n, n, c, m)
        else:
            m = m // 2
            keep, give = (r, n, c + bit * m, m), (r, n, c + (1 - bit) * m, m)
        regions.append(keep)

        def spot(region):
            return (
                pl.ds(pl.multiple_of(region[0], 8), region[1]),
                pl.ds(pl.multiple_of(region[2], 128), region[3]),
            )

        copy = pltpu.make_async_remote_copy(
            src_ref=total.at[spot(give)],
            dst_ref=landing.at[step, pl.ds(0, n), pl.ds(0, m)],
            send_sem=send_a.at[step],
            recv_sem=recv_a.at[step],
            device_id=device,
            device_id_type=MESH,
        )
        copy.start()
        copy.wait()
        total[spot(keep)] += landing[step, pl.ds(0, n), pl.ds(0, m)]
    out[spot(regions[-1])] = total[spot(regions[-1])]
    for step in range(len(ends) - 1, -1, -1):
        region = out.at[spot(regions[step + 1])]
        copy = pltpu.make_async_remote_copy(
            src_ref=region,
            dst_ref=region,
            send_sem=send_b.at[step],
            recv_sem=recv_b.at[step],
            device_id=ends[step][1],
            device_id_type=MESH,
        )
        copy.start()
        copy.wait()


def cube_sum(value, bits, identity):
    steps = len(bits)
    rows, columns = value.shape
    return pl.pallas_call(
        lambda *refs: cube_sum_kernel(bits, *refs),
        out_shape=jax.ShapeDtypeStruct(value.shape, value.dtype),
        in_specs=[pl.BlockSpec(memory_space=pltpu.VMEM)],
        out_specs=pl.BlockSpec(memory_space=pltpu.VMEM),
        scratch_shapes=[
            pltpu.VMEM(value.shape, value.dtype),
            pltpu.VMEM((steps, rows // 2, columns), value.dtype),
        ]
        + [pltpu.SemaphoreType.DMA((steps,))] * 4,
        compiler_params=pltpu.CompilerParams(
            collective_id=identity, has_side_effects=True, vmem_limit_bytes=32 * 2**20
        ),
        name="cube_sum_%d" % identity,
    )(value)


def axis_bits(axis):
    return [(axis, 2**bit) for bit in range(lax.axis_size(axis).bit_length() - 1)]


def plus_flips(place, bits):
    moved = place
    for bit in bits:
        moved = moved + (1 - 2 * lax.rem(place // 2**bit, 2)) * 2**bit
    return moved


def cube_routes(count):
    bits = list(range(1, count))
    pieces = []
    for turn in range(len(bits)):
        order = bits[turn:] + bits[:turn]
        arrivals = [()]
        steps = []
        for bit in order:
            fresh = [held + (bit,) for held in arrivals]
            steps.append([(bit, held, whole) for held, whole in zip(arrivals, fresh)])
            arrivals = arrivals + fresh
        pieces.append((arrivals, steps))
    return pieces


class CubeGather:
    def __init__(self, whole, rows, count, sems):
        self.whole, self.rows, self.count = whole, rows, count
        self.send_sem, self.recv_sem, self.pair_send, self.pair_recv = sems
        self.routes = cube_routes(count.bit_length() - 1)
        self.me = lax.axis_index("dp")
        self.piece_rows = rows // len(self.routes)

    def region(self, piece, held):
        first = plus_flips(self.me, held) * self.rows + piece * self.piece_rows
        return self.whole.at[pl.ds(pl.multiple_of(first, 16), self.piece_rows)]

    def hop(self, piece, bit, held, slot, pair=False):
        block = self.region(piece, held)
        return pltpu.make_async_remote_copy(
            src_ref=block,
            dst_ref=block,
            send_sem=(self.pair_send if pair else self.send_sem).at[piece, slot],
            recv_sem=(self.pair_recv if pair else self.recv_sem).at[piece, slot],
            device_id={"dp": plus_flips(self.me, (bit,))},
            device_id_type=MESH,
        )

    def slot(self, piece, held):
        return self.routes[piece][0].index(held)

    def sends_of(self, piece, held):
        found = []
        for step in self.routes[piece][1]:
            for bit, source, landed in step:
                if source == held:
                    found.append(self.hop(piece, bit, held, self.slot(piece, landed)))
        found.append(self.hop(piece, 0, held, self.slot(piece, held), True))
        return found

    def start(self):
        for piece in range(len(self.routes)):
            for copy in self.sends_of(piece, ()):
                copy.start()

    def step(self, index):
        for piece, (_, steps) in enumerate(self.routes):
            for bit, _, landed in steps[index]:
                self.hop(piece, bit, landed, self.slot(piece, landed)).wait_recv()
                for copy in self.sends_of(piece, landed):
                    copy.start()

    def steps(self):
        return len(self.routes)

    def finish(self):
        for piece, (arrivals, _) in enumerate(self.routes):
            for held in arrivals:
                self.hop(piece, 0, (0,) + held, self.slot(piece, held), True).wait_recv()

    def drain(self):
        for piece, (arrivals, _) in enumerate(self.routes):
            for held in arrivals:
                for copy in self.sends_of(piece, held):
                    copy.wait_send()


FLOW_ORDER = (1, 2, 3, 0)


def forward_kernel(
    size,
    count,
    flows,
    w_in,
    w_out,
    small,
    rope,
    all_in,
    all_out,
    all_normed,
    joined_out,
    slope_out,
    heads_out,
    chances_out,
    newest,
    w_in_low,
    w_out_low,
    normed,
    heads,
    chances,
    joined,
    slope,
    total,
    give,
    terms,
    stage_sem,
    line_send,
    line_recv,
    term_send,
    term_recv,
    save_sem,
    flow_sem,
    *cube_sems,
):
    here = lax.axis_index("tensor")
    me = lax.axis_index("dp")
    own = flows.shape[1]
    rows_in = w_in.shape[0]
    length = own * size
    width_in, width_out = w_in.shape[1], w_out.shape[1]
    head_width = heads.shape[2]
    group_heads = head_width // HD
    attn_width = 3 * head_width
    units = width_in - attn_width
    bits = count.bit_length() - 1
    sides = ((0, 1), (1, -1))
    tile = 512

    def rows_of(block):
        return pl.ds(pl.multiple_of(block * own, own), own)

    def stage(source, width):
        spans = [(0, min(width, D))] + ([(D, width - D)] if width > D else [])
        return [
            pltpu.make_async_copy(
                source.at[:, pl.ds(first, span)],
                total.at[pl.ds(place * rows_in, rows_in), pl.ds(0, span)],
                stage_sem.at[place],
            )
            for place, (first, span) in enumerate(spans)
        ]

    def settle(source, width, target):
        for place, copy in enumerate(stage(source, width)):
            copy.wait()
            span = min(D, width - place * D)

            def cast(index, carry):
                low = pl.multiple_of(index * 16, 16)
                into = pl.multiple_of(me * rows_in + index * 16, 16)
                target[pl.ds(into, 16), pl.ds(place * D, span)] = total[
                    pl.ds(place * rows_in + low, 16), pl.ds(0, span)
                ].astype(bfloat)
                return carry

            lax.fori_loop(0, rows_in // 16, cast, 0)

    for copy in stage(w_in, width_in):
        copy.start()
    others = [lax.rem(here + step, size) for step in range(1, size)]
    enter(
        [(jnp.bool_(True), {"tensor": other}) for other in others]
        + [(jnp.bool_(True), {"dp": plus_flips(me, (bit,))}) for bit in range(bits)]
    )

    def line_hop(side, way, step, flow):
        block = normed.at[flow, rows_of(here - way * step)]
        return pltpu.make_async_remote_copy(
            src_ref=block,
            dst_ref=block,
            send_sem=line_send.at[side, step, flow],
            recv_sem=line_recv.at[side, step, flow],
            device_id={"tensor": here + way},
            device_id_type=MESH,
        )

    def line_landed(side, way, step, flow):
        block = normed.at[flow, rows_of(here - way * step)]
        return pltpu.make_async_remote_copy(
            src_ref=block,
            dst_ref=block,
            send_sem=line_send.at[side, step - 1, flow],
            recv_sem=line_recv.at[side, step - 1, flow],
            device_id={"tensor": here - way},
            device_id_type=MESH,
        )

    def has_next(way):
        return here < size - 1 if way > 0 else here > 0

    def has_origin(way, step):
        return here >= step if way > 0 else here < size - step

    def keep_flow(flow, block):
        return pltpu.make_async_copy(
            normed.at[flow, rows_of(block)],
            all_normed.at[flow, rows_of(block)],
            flow_sem.at[flow, block],
        )

    for flow in FLOW_ORDER:
        which = 2 if flow == 3 else 0

        def normalize(index, carry):
            spot = pl.ds(pl.multiple_of(index * 16, 16), 16)
            values = flows[flow, spot].astype(single)
            centred = values - jnp.mean(values, axis=-1, keepdims=True)
            inverse = lax.rsqrt(jnp.mean(centred * centred, axis=-1, keepdims=True) + norm_eps)
            into = pl.ds(pl.multiple_of(here * own + index * 16, 16), 16)
            normed[flow, into] = (
                centred * inverse * small[which : which + 1, :] + small[which + 1 : which + 2, :]
            ).astype(bfloat)
            return carry

        lax.fori_loop(0, own // 16, normalize, 0)
        for side, way in sides:
            pl.when(has_next(way))(line_hop(side, way, 0, flow).start)
        keep_flow(flow, here).start()

    cube_in = CubeGather(w_in_low, rows_in, count, cube_sems[:4])
    cube_out = CubeGather(w_out_low, rows_in, count, cube_sems[4:])
    settle(w_in, width_in, w_in_low)
    cube_in.start()
    for copy in stage(w_out, width_out):
        copy.start()
    settle(w_out, width_out, w_out_low)

    def line_step(step, flow_list):
        for flow in flow_list:
            for side, way in sides:

                @pl.when(has_origin(way, step))
                def _():
                    line_landed(side, way, step, flow).wait_recv()
                    pl.when(has_next(way))(line_hop(side, way, step, flow).start)
                    keep_flow(flow, here - way * step).start()

    def at_distance(step, action):
        if step == 0:
            action(here)
            return
        for side, way in sides:

            @pl.when(has_origin(way, step))
            def _():
                action(here - way * step)

    def project(block, part):
        rows = rows_of(block)
        source = normed[part, rows]
        pre = jnp.dot(
            source,
            jnp.concatenate(
                [
                    w_in_low[:, pl.ds((head * 3 + part) * HD, HD)]
                    for head in range(group_heads)
                ],
                axis=1,
            ),
            preferred_element_type=single,
        )
        first = pl.multiple_of(here * head_width, HD)
        pre = pre + small[5 + part : 6 + part, pl.ds(first, head_width)]
        if part == 2:
            heads[part, rows] = pre.astype(bfloat)
            return
        cosine, sine_low, sine_high = rope[0, rows], rope[1, rows], rope[2, rows]
        for head in range(group_heads):
            values = pre[:, head * HD : (head + 1) * HD]
            turned = (
                values * cosine
                + pltpu.roll(values, HD - ROT // 2, 1) * sine_low
                + pltpu.roll(values, ROT // 2, 1) * sine_high
            )
            heads[part, rows, pl.ds(head * HD, HD)] = turned.astype(bfloat)

    def expand(block):
        rows = rows_of(block)

        def one(index, carry):
            first = pl.multiple_of(index * tile, tile)
            pre = jnp.dot(
                normed[3, rows],
                w_in_low[:, pl.ds(attn_width + first, tile)],
                preferred_element_type=single,
            )
            pre = pre + small[pl.ds(10 + here, 1), pl.ds(first, tile)]
            normal = 0.5 * (1.0 + lax.erf(pre * 0.7071067811865476))
            joined[rows, pl.ds(head_width + first, tile)] = (pre * normal).astype(bfloat)
            slope[rows, pl.ds(first, tile)] = (
                normal + pre * jnp.exp(-0.5 * pre * pre) * 0.3989422804014327
            ).astype(bfloat)
            return carry

        lax.fori_loop(0, units // tile, one, 0)

    def contract(block):
        rows = rows_of(block)

        def one(index, carry):
            first = pl.multiple_of(index * tile, tile)
            total[rows, pl.ds(first, tile)] = contract_last(
                joined[rows, pl.ds(head_width, units)],
                w_out_low[pl.ds(first, tile), pl.ds(head_width, units)],
            )
            return carry

        lax.fori_loop(0, D // tile, one, 0)

    def attend(block):
        rows = rows_of(block)
        places = block * own + lax.broadcasted_iota(jnp.int32, (own, length), 0)
        allowed = lax.broadcasted_iota(jnp.int32, (own, length), 1) <= places
        for head in range(group_heads):
            lanes = pl.ds(head * HD, HD)
            scores = contract_last(heads[0, rows, lanes], heads[1, :, lanes]) * HD ** (-0.5)
            scores = jnp.where(allowed, scores, masked_score)
            raised = jnp.exp(scores - jnp.max(scores, axis=-1, keepdims=True))
            low = (raised / jnp.sum(raised, axis=-1, keepdims=True)).astype(bfloat)
            chances[head, rows] = low
            joined[rows, lanes] = jnp.dot(
                low, heads[2, :, lanes], preferred_element_type=single
            ).astype(bfloat)

    def term_hop(dest):
        return pltpu.make_async_remote_copy(
            src_ref=give.at[rows_of(dest)],
            dst_ref=terms.at[here],
            send_sem=term_send.at[dest],
            recv_sem=term_recv.at[here],
            device_id={"tensor": dest},
            device_id_type=MESH,
        )

    def finish_block(block):
        attend(block)
        rows = rows_of(block)

        def one(index, carry):
            first = pl.multiple_of(index * tile, tile)
            spot = (rows, pl.ds(first, tile))
            give[spot] = (
                total[spot]
                + contract_last(
                    joined[rows, pl.ds(0, head_width)],
                    w_out_low[pl.ds(first, tile), pl.ds(0, head_width)],
                )
            ).astype(bfloat)
            return carry

        lax.fori_loop(0, D // tile, one, 0)
        pl.when(block != here)(term_hop(block).start)

    def save(place, source, target):
        return pltpu.make_async_copy(source, target, save_sem.at[place])

    line_step(1, FLOW_ORDER[:2])
    cube_in.step(0)
    cube_out.start()
    line_step(1, FLOW_ORDER[2:])
    for index in range(1, cube_in.steps()):
        cube_in.step(index)
    cube_in.finish()
    save(0, w_in_low, all_in).start()

    def early(block):
        project(block, 1)
        project(block, 2)
        expand(block)
        project(block, 0)

    at_distance(0, early)
    line_step(2, FLOW_ORDER[:2])
    at_distance(1, early)
    cube_out.step(0)
    line_step(2, FLOW_ORDER[2:])
    at_distance(2, early)
    for index in range(1, cube_out.steps()):
        cube_out.step(index)
    cube_out.finish()
    save(1, w_out_low, all_out).start()
    for step in range(size - 1):
        at_distance(step, contract)
    for step in range(3, size):
        line_step(step, FLOW_ORDER[:2])

    def keys_values(block):
        project(block, 1)
        project(block, 2)

    for step in range(3, size):
        at_distance(step, keys_values)
    for step in range(min(3, size)):
        at_distance(step, finish_block)
    for step in range(3, size):
        line_step(step, FLOW_ORDER[2:3])

        def late(block):
            expand(block)
            contract(block)

        at_distance(step, late)
        line_step(step, FLOW_ORDER[3:])

        def last(block):
            project(block, 0)
            finish_block(block)

        at_distance(step, last)
    saves = [
        save(2, joined, joined_out),
        save(3, slope, slope_out),
        save(4, heads, heads_out),
        save(5, chances, chances_out),
    ]
    for copy in saves:
        copy.start()
    for other in others:
        pltpu.make_async_remote_copy(
            src_ref=terms.at[other],
            dst_ref=terms.at[other],
            send_sem=term_send.at[other],
            recv_sem=term_recv.at[other],
            device_id={"tensor": other},
            device_id_type=MESH,
        ).wait_recv()
    terms[here] = give[rows_of(here)]

    def gather_terms(index, carry):
        spot = pl.ds(pl.multiple_of(index * 16, 16), 16)
        branch = terms[0, spot].astype(single)
        for term in range(1, size):
            branch = branch + terms[term, spot].astype(single)
        newest[spot] = flows[3, spot].astype(single) + branch + small[8:9, :] + small[9:10, :]
        return carry

    lax.fori_loop(0, own // 16, gather_terms, 0)
    for step in range(size):
        for flow in FLOW_ORDER:
            for side, way in sides:

                @pl.when(jnp.logical_and(has_next(way), has_origin(way, step)))
                def _():
                    line_hop(side, way, step, flow).wait_send()

    cube_in.drain()
    cube_out.drain()
    for other in others:
        term_hop(other).wait_send()
    for flow in FLOW_ORDER:
        for block in range(size):
            keep_flow(flow, block).wait()
    save(0, w_in_low, all_in).wait()
    save(1, w_out_low, all_out).wait()
    for copy in saves:
        copy.wait()


def forward(flows, w_in, w_out, small, size, count, identity):
    own = flows.shape[1]
    length = own * size
    rows, width_in = w_in.shape
    width_out = w_out.shape[1]
    head_width = HEADS // size * HD
    units = FF // size
    cosine, sine = rope_tables(length)
    half = ROT // 2
    blank = jnp.zeros((length, HD - ROT), single)
    none = jnp.zeros((length, half), single)
    rope = jnp.stack(
        [
            jnp.concatenate([cosine, blank + 1.0], axis=1),
            jnp.concatenate([-sine[:, :half], none, blank], axis=1),
            jnp.concatenate([none, sine[:, half:], blank], axis=1),
        ]
    )
    pieces = count.bit_length() - 2
    cube = [pltpu.SemaphoreType.DMA((pieces, 2**pieces))] * 8
    low = lambda *shape: jax.ShapeDtypeStruct(shape, bfloat)
    hbm = pl.BlockSpec(memory_space=pl.ANY)
    vmem = pl.BlockSpec(memory_space=pltpu.VMEM)
    return pl.pallas_call(
        lambda *refs: forward_kernel(size, count, *refs),
        out_shape=[
            low(D, width_in),
            low(D, width_out),
            low(STREAMS, length, D),
            low(length, width_out),
            low(length, units),
            low(3, length, head_width),
            low(HEADS // size, length, length),
            jax.ShapeDtypeStruct((own, D), single),
        ],
        in_specs=[vmem, hbm, hbm, vmem, vmem],
        out_specs=[hbm] * 7 + [vmem],
        scratch_shapes=[
            pltpu.VMEM((D, width_in), bfloat),
            pltpu.VMEM((D, width_out), bfloat),
            pltpu.VMEM((STREAMS, length, D), bfloat),
            pltpu.VMEM((3, length, head_width), bfloat),
            pltpu.VMEM((HEADS // size, length, length), bfloat),
            pltpu.VMEM((length, width_out), bfloat),
            pltpu.VMEM((length, units), bfloat),
            pltpu.VMEM((length, D), single),
            pltpu.VMEM((length, D), bfloat),
            pltpu.VMEM((size, own, D), bfloat),
            pltpu.SemaphoreType.DMA((2,)),
            pltpu.SemaphoreType.DMA((2, size, STREAMS)),
            pltpu.SemaphoreType.DMA((2, size, STREAMS)),
            pltpu.SemaphoreType.DMA((size,)),
            pltpu.SemaphoreType.DMA((size,)),
            pltpu.SemaphoreType.DMA((6,)),
            pltpu.SemaphoreType.DMA((STREAMS, size)),
        ]
        + cube,
        compiler_params=pltpu.CompilerParams(
            collective_id=identity, has_side_effects=True, vmem_limit_bytes=60 * 2**20
        ),
        name="forward_%d" % identity,
    )(flows, w_in, w_out, small, rope)


def shards(
    in_streams,
    stored,
    cotangent,
    in_weights,
    in_moment,
    in_second,
    in_average,
    out_weights,
    out_moment,
    output_second_moment,
    out_average,
    small_params,
    small_moment,
    small_second,
    small_average,
    mix_weights,
    mix_moment,
    mix_second,
    mix_average,
):
    groups = lax.axis_size("tensor")
    group_index = lax.axis_index("tensor")
    heads_group = HEADS // groups
    units_group = FF // groups
    attn_width = heads_group * 3 * HD
    proj_width = heads_group * HD
    own_rows = in_streams.shape[1]
    length = own_rows * groups
    up_rows = FF // D
    score_scale = HD ** (-0.5)
    shard_rows = D // lax.axis_size("dp")
    full_in, full_out, normed, joined, slope, heads, chances, newest = forward(
        in_streams, in_weights, out_weights, small_params, groups, lax.axis_size("dp"), 0
    )
    queries, key_heads, value_heads = (
        heads[part].reshape(length, heads_group, HD) for part in range(3)
    )
    gain_mix = small_params[4]
    mix_low = small_params[10 + up_rows :].astype(bfloat)
    flow_rows = in_streams.astype(single)
    centred = flow_rows - jnp.mean(flow_rows, axis=-1, keepdims=True)
    inverse = lax.rsqrt(jnp.mean(centred * centred, axis=-1, keepdims=True) + norm_eps)
    unit_flows = centred * inverse
    gain_all = jnp.stack([small_params[0], small_params[0], small_params[0], small_params[2]])[
        :, None, :
    ]
    attn_weights = full_in[:, :attn_width].reshape(D, heads_group, 3, HD)
    up_weights = full_in[:, attn_width:]
    cosine_table, sine_table = rope_tables(length)

    inv_rms = lax.rsqrt(jnp.mean(newest * newest, axis=-1, keepdims=True) + mix_eps)
    mix_normed = (newest * inv_rms * gain_mix).astype(bfloat)
    mix_pre = contract_last(mix_normed, mix_low)
    mixing_activation = gelu_value(mix_pre)
    mixing_weights = (
        jnp.dot(mixing_activation, mix_weights[:MIXH], precision=highest_precision)
        + mix_weights[MIXH]
    )
    mixing_weights = mixing_weights.reshape(own_rows, STREAMS, LAYERS)
    composed = mixing_weights[:, :, LAYER].T[:, :, None] * newest[None]
    for layer_index in range(LAYER):
        composed = (
            composed
            + mixing_weights[:, :, layer_index].T[:, :, None]
            * stored[layer_index].astype(single)[None]
        )
    out_streams = composed.astype(bfloat)
    back_flows = cotangent.astype(single)
    d_stored = jnp.einsum("srd,jrd->rsj", cotangent, stored, preferred_element_type=single)
    d_newest_col = jnp.einsum("srd,rd->rs", back_flows, newest, precision=highest_precision)
    d_mixing = jnp.concatenate([d_stored, d_newest_col[:, :, None]], axis=2).reshape(own_rows, MIXH)
    spread_gradient = jnp.einsum(
        "rsj,srd->jrd", mixing_weights, back_flows, precision=highest_precision
    )
    grad_stored = spread_gradient[:LAYER].astype(bfloat)
    d_act = jnp.dot(d_mixing, mix_weights[:MIXH].T, precision=highest_precision)
    grad_mix_out = jnp.dot(mixing_activation.T, d_mixing, precision=highest_precision)
    grad_mix_bias = jnp.sum(d_mixing, axis=0)
    d_mix_pre = (d_act * gelu_slope(mix_pre)).astype(bfloat)
    grad_mix_in = contract_first(d_mix_pre, mix_normed)
    d_mix_normed = jnp.dot(d_mix_pre, mix_low, preferred_element_type=single)
    scaled_back = d_mix_normed * gain_mix
    grad_gain_mix = jnp.sum(d_mix_normed * newest * inv_rms, axis=0)
    d_newest = (
        spread_gradient[LAYER]
        + inv_rms * scaled_back
        - newest * inv_rms**3 * jnp.mean(scaled_back * newest, axis=-1, keepdims=True)
    )
    grad_bias_out = jnp.sum(d_newest, axis=0)
    branch_grads = line_gather(d_newest.astype(bfloat)[None], groups, 4, 2).reshape(length, D)
    d_joined = jnp.dot(branch_grads, full_out, preferred_element_type=single)
    d_attended = d_joined[:, :proj_width].reshape(length, heads_group, HD).astype(bfloat)
    d_up = (d_joined[:, proj_width:] * slope).astype(bfloat)

    d_chances = jnp.einsum("qhe,khe->hqk", d_attended, value_heads, preferred_element_type=single)
    centre = jnp.sum(d_chances * chances, axis=-1, keepdims=True)
    d_scores = (chances * (d_chances - centre)).astype(bfloat)
    d_queries = (
        jnp.einsum("hqk,khe->qhe", d_scores, key_heads, preferred_element_type=single) * score_scale
    )
    d_key_heads = (
        jnp.einsum("hqk,qhe->khe", d_scores, queries, preferred_element_type=single) * score_scale
    )
    value_head_gradient = jnp.einsum(
        "hqk,qhe->khe", chances, d_attended, preferred_element_type=single
    )
    d_pre_q = rotate_back(d_queries, cosine_table, sine_table).astype(bfloat)
    d_pre_k = rotate_back(d_key_heads, cosine_table, sine_table).astype(bfloat)
    d_pre_v = value_head_gradient.astype(bfloat)
    d_pres = jnp.stack([d_pre_q, d_pre_k, d_pre_v], axis=2)
    bias_grads = jnp.sum(d_pres, axis=0, dtype=single)
    unit_grads = jnp.sum(d_up, axis=0, dtype=single)
    d_norm_parts = [
        jnp.einsum(
            "lhe,dhe->ld",
            d_pres[:, :, part_index],
            attn_weights[:, :, part_index, :],
            preferred_element_type=single,
        )
        for part_index in range(3)
    ]
    d_norm_parts.append(contract_last(d_up, up_weights))
    d_normed = jnp.stack(d_norm_parts)
    d_own = line_scatter(
        d_normed.astype(bfloat).reshape(STREAMS, groups, own_rows, D), groups, 1, 3
    )
    d_unit = d_own * gain_all
    d_flows = inverse * (
        d_unit
        - jnp.mean(d_unit, axis=-1, keepdims=True)
        - unit_flows * jnp.mean(d_unit * unit_flows, axis=-1, keepdims=True)
    )
    grad_streams = jnp.concatenate([d_flows[:3], (d_flows[3] + d_newest)[None]], axis=0).astype(
        bfloat
    )
    gain_grads = jnp.sum(d_own * unit_flows, axis=1)
    shift_grads = jnp.sum(d_own, axis=1)
    head_rows = lax.dynamic_update_slice_in_dim(
        jnp.zeros((HEADS, 3, HD), single), bias_grads, group_index * heads_group, 0
    )
    head_rows = jnp.transpose(head_rows, (1, 0, 2)).reshape(3, D)
    unit_full = lax.dynamic_update_slice_in_dim(
        jnp.zeros((FF,), single), unit_grads, group_index * units_group, 0
    )
    small_grad = jnp.concatenate(
        [
            jnp.stack(
                [
                    gain_grads[0] + gain_grads[1] + gain_grads[2],
                    shift_grads[0] + shift_grads[1] + shift_grads[2],
                    gain_grads[3],
                    shift_grads[3],
                    grad_gain_mix,
                ]
            ),
            head_rows,
            jnp.stack([grad_bias_out, grad_bias_out]),
            unit_full.reshape(up_rows, D),
            grad_mix_in,
        ],
        axis=0,
    )
    mix_grad = jnp.concatenate([grad_mix_out, grad_mix_bias[None]], axis=0)
    attn_part = jnp.einsum(
        "pld,lhpe->dhpe", normed[:3], d_pres, preferred_element_type=single
    ).reshape(D, attn_width)
    up_part = contract_first(normed[3], d_up)

    def owned(part):
        return lax.psum_scatter(
            part.astype(bfloat), "dp", scatter_dimension=0, tiled=True
        ).astype(single)

    grad_out = owned(contract_first(branch_grads, joined))
    grad_in = owned(jnp.concatenate([attn_part, up_part], axis=1))
    big_square = jnp.sum(grad_in * grad_in) + jnp.sum(grad_out * grad_out)
    small_rows = small_grad.shape[0]
    mix_row = jnp.concatenate([mix_grad.reshape(-1), big_square[None]])
    mix_row = jnp.pad(mix_row, (0, D - mix_row.shape[0]))
    packed = jnp.concatenate(
        [small_grad, mix_row[None], jnp.zeros((63 - small_rows, D), single)], axis=0
    )
    packed = cube_sum(packed, axis_bits("dp") + axis_bits("tensor"), 4)
    small_parameter_total = packed[:small_rows]
    mix_total = packed[small_rows, : mix_grad.size].reshape(mix_grad.shape)
    big_total = packed[small_rows, mix_grad.size]
    grad_norm = jnp.sqrt(
        big_total
        + jnp.sum(small_parameter_total * small_parameter_total)
        + jnp.sum(mix_total * mix_total)
    )
    factor = clip_norm / jnp.maximum(grad_norm, clip_norm)
    in_new = adamw_step(in_weights, in_moment, in_second, in_average, grad_in, factor, learn_rate)
    out_new = adamw_step(
        out_weights, out_moment, output_second_moment, out_average, grad_out, factor, learn_rate
    )
    small_new = adamw_step(
        small_params,
        small_moment,
        small_second,
        small_average,
        small_parameter_total,
        factor,
        small_rate,
    )
    mix_new = adamw_step(
        mix_weights, mix_moment, mix_second, mix_average, mix_total, factor, small_rate
    )
    return (
        out_streams,
        grad_streams,
        grad_stored,
        grad_norm,
        in_new[0],
        in_new[1],
        in_new[2],
        in_new[3],
        in_new[0].astype(bfloat),
        out_new[0],
        out_new[1],
        out_new[2],
        out_new[3],
        out_new[0].astype(bfloat),
        small_new[0],
        small_new[1],
        small_new[2],
        small_new[3],
        mix_new[0],
        mix_new[1],
        mix_new[2],
        mix_new[3],
    )


def solution(mesh):
    in_specs = (
        P(None, ("dp", "tensor"), None),
        P(None, ("dp", "tensor"), None),
        P(None, ("dp", "tensor"), None),
        P("dp", "tensor"),
        P("dp", "tensor"),
        P("dp", "tensor"),
        P("dp", "tensor"),
        P("dp", "tensor"),
        P("dp", "tensor"),
        P("dp", "tensor"),
        P("dp", "tensor"),
        P(),
        P(),
        P(),
        P(),
        P(),
        P(),
        P(),
        P(),
    )
    out_specs = (
        P(None, ("dp", "tensor"), None),
        P(None, ("dp", "tensor"), None),
        P(None, ("dp", "tensor"), None),
        P(),
        P("dp", "tensor"),
        P("dp", "tensor"),
        P("dp", "tensor"),
        P("dp", "tensor"),
        P("dp", "tensor"),
        P("dp", "tensor"),
        P("dp", "tensor"),
        P("dp", "tensor"),
        P("dp", "tensor"),
        P("dp", "tensor"),
        P(),
        P(),
        P(),
        P(),
        P(),
        P(),
        P(),
        P(),
    )
    return jax.shard_map(shards, mesh=mesh, in_specs=in_specs, out_specs=out_specs, check_vma=False)
```

```python
import jax
import jax.numpy as jnp
import numpy as np
from jax import lax
from jax.experimental import pallas as pl
from jax.experimental.pallas import tpu as pltpu
from jax.sharding import PartitionSpec as P

D = 2048
HEADS = 16
HD = 128
ROT = 32
FF = 8192
STREAMS = 4
LAYER = 8
STEP = 10
LAYERS = 9
MIXH = 36


norm_eps = 1e-05
mix_eps = 1e-06
beta_first = 0.9
beta_second = 0.95
adam_eps = 1e-08
decay_rate = 0.01
learn_rate = 0.03
small_rate = 0.2
clip_norm = 1.0
average_keep = 0.5
masked_score = -1e30
highest_precision = lax.Precision.HIGHEST
bfloat = jnp.bfloat16
single = jnp.float32
MESH = pl.DeviceIdType.MESH


def contract_last(left_side, right_side):
    return lax.dot_general(
        left_side,
        right_side,
        (((left_side.ndim - 1,), (right_side.ndim - 1,)), ((), ())),
        preferred_element_type=single,
    )


def contract_first(left_side, right_side):
    return lax.dot_general(
        left_side, right_side, (((0,), (0,)), ((), ())), preferred_element_type=single
    )


def adamw_step(weight, moment, second, average, gradient, factor, rate):
    clipped = gradient * factor
    moment = beta_first * moment + (1.0 - beta_first) * clipped
    second = beta_second * second + (1.0 - beta_second) * clipped * clipped
    step_ratio = (
        moment
        / (1.0 - beta_first**STEP)
        / (jnp.sqrt(second / (1.0 - beta_second**STEP)) + adam_eps)
    )
    weight = weight - rate * (step_ratio + decay_rate * weight)
    average = average_keep * average + (1.0 - average_keep) * weight
    return (weight, moment, second, average)


def enter(partners):
    barrier = pltpu.get_barrier_semaphore()
    for present, device in partners:

        @pl.when(present)
        def _():
            pl.semaphore_signal(barrier, inc=1, device_id=device, device_id_type=MESH)

    pl.semaphore_wait(barrier, sum(present.astype(jnp.int32) for present, _ in partners))


class LineSum:
    def __init__(self, size, give, landing, send_sem, recv_sem, cut):
        self.size, self.give, self.landing = size, give, landing
        self.send_sem, self.recv_sem, self.cut = send_sem, recv_sem, cut
        self.here = lax.axis_index("tensor")
        self.own = landing.shape[1]
        self.rows = self.own // cut
        self.near = lax.select(2 * self.here < size, 1, -1)

    def has_next(self, way):
        return jnp.logical_and(self.here + way >= 0, self.here + way < self.size)

    def spot(self, dest, place):
        return pl.ds(pl.multiple_of(dest * self.own + place * self.rows, 16), self.rows)

    def landed(self, way, dest, place):
        rows = pl.ds(pl.multiple_of(place * self.rows, 16), self.rows)
        return self.landing.at[dest + (1 + way) // 2, rows]

    def hop(self, way, dest, place):
        return pltpu.make_async_remote_copy(
            src_ref=self.give.at[self.spot(dest, place)],
            dst_ref=self.landed(way, dest, place),
            send_sem=self.send_sem.at[(1 - way) // 2, dest, place],
            recv_sem=self.recv_sem.at[(1 - way) // 2, dest, place],
            device_id={"tensor": self.here + way},
            device_id_type=MESH,
        )

    def arrive(self, way, dest, place):
        block = self.landed(way, dest, place)
        pltpu.make_async_remote_copy(
            src_ref=block,
            dst_ref=block,
            send_sem=self.send_sem.at[(1 - way) // 2, dest, place],
            recv_sem=self.recv_sem.at[(1 - way) // 2, dest, place],
            device_id={"tensor": self.here - way},
            device_id_type=MESH,
        ).wait_recv()

    def relay(self, way, dest):
        @pl.when((dest - self.here) * way > 0)
        def _():
            def one(place, carry):
                @pl.when(self.has_next(-way))
                def _():
                    self.arrive(way, dest, place)
                    spot = self.spot(dest, place)
                    self.give[spot] = (
                        self.give[spot].astype(single)
                        + self.landed(way, dest, place)[...].astype(single)
                    ).astype(bfloat)

                self.hop(way, dest, place).start()
                return carry

            lax.fori_loop(0, self.cut, one, 0)

    def far(self, rank, way):
        return (self.size - 1) * ((1 + way) // 2) - rank * way

    def collect(self, place, into):
        rows = pl.ds(place * self.rows, self.rows)
        into[rows] = self.give[self.spot(self.here, place)].astype(single)
        for way in (1, -1):

            @pl.when(self.has_next(-way))
            def _():
                self.arrive(way, self.here, place)
                into[rows] += self.landed(way, self.here, place)[...].astype(single)

    def drain(self):
        for rank in range(self.size - 1):
            for way in (1, -1):
                dest = self.far(rank, way)

                @pl.when((dest - self.here) * way > 0)
                def _():
                    for place in range(self.cut):
                        self.hop(way, dest, place).wait_send()


def cube_sum_steps(bits, value, out, total, landing, send_a, recv_a, send_b, recv_b):
    rows, columns = value.shape

    def partner(axis, size):
        place = lax.axis_index(axis)
        bit = lax.rem(place // size, 2)
        return bit, {axis: place + (1 - 2 * bit) * size}

    ends = [partner(*entry) for entry in bits]
    enter([(jnp.bool_(True), device) for _, device in ends])
    total[...] = value[...]
    regions = [(0, rows, 0, columns)]
    for step, (bit, device) in enumerate(ends):
        r, n, c, m = regions[-1]
        if n > 8:
            n = n // 2
            keep, give = (r + bit * n, n, c, m), (r + (1 - bit) * n, n, c, m)
        else:
            m = m // 2
            keep, give = (r, n, c + bit * m, m), (r, n, c + (1 - bit) * m, m)
        regions.append(keep)

        def spot(region):
            return (
                pl.ds(pl.multiple_of(region[0], 8), region[1]),
                pl.ds(pl.multiple_of(region[2], 128), region[3]),
            )

        copy = pltpu.make_async_remote_copy(
            src_ref=total.at[spot(give)],
            dst_ref=landing.at[step, pl.ds(0, n), pl.ds(0, m)],
            send_sem=send_a.at[step],
            recv_sem=recv_a.at[step],
            device_id=device,
            device_id_type=MESH,
        )
        copy.start()
        copy.wait()
        total[spot(keep)] += landing[step, pl.ds(0, n), pl.ds(0, m)]
    out[spot(regions[-1])] = total[spot(regions[-1])]
    for step in range(len(ends) - 1, -1, -1):
        region = out.at[spot(regions[step + 1])]
        copy = pltpu.make_async_remote_copy(
            src_ref=region,
            dst_ref=region,
            send_sem=send_b.at[step],
            recv_sem=recv_b.at[step],
            device_id=ends[step][1],
            device_id_type=MESH,
        )
        copy.start()
        copy.wait()


def axis_bits(axis):
    return [(axis, 2**bit) for bit in range(lax.axis_size(axis).bit_length() - 1)]


def plus_flips(place, bits):
    moved = place
    for bit in bits:
        moved = moved + (1 - 2 * lax.rem(place // 2**bit, 2)) * 2**bit
    return moved


def cube_routes(count):
    bits = list(range(1, count))
    pieces = []
    for turn in range(len(bits)):
        order = bits[turn:] + bits[:turn]
        arrivals = [()]
        steps = []
        for bit in order:
            fresh = [tuple(sorted(held + (bit,))) for held in arrivals]
            steps.append([(bit, held, whole) for held, whole in zip(arrivals, fresh)])
            arrivals = arrivals + fresh
        pieces.append((arrivals, steps))
    return pieces


class CubeGather:
    def __init__(self, whole, rows, count, sems):
        self.whole, self.rows, self.count = whole, rows, count
        self.send_sem, self.recv_sem, self.pair_send, self.pair_recv = sems
        self.routes = cube_routes(count.bit_length() - 1)
        self.me = lax.axis_index("dp")
        self.piece_rows = rows // len(self.routes)

    def region(self, piece, held):
        first = plus_flips(self.me, held) * self.rows + piece * self.piece_rows
        return self.whole.at[pl.ds(pl.multiple_of(first, 16), self.piece_rows)]

    def hop(self, piece, bit, held, slot, pair=False):
        block = self.region(piece, held)
        return pltpu.make_async_remote_copy(
            src_ref=block,
            dst_ref=block,
            send_sem=(self.pair_send if pair else self.send_sem).at[piece, slot],
            recv_sem=(self.pair_recv if pair else self.recv_sem).at[piece, slot],
            device_id={"dp": plus_flips(self.me, (bit,))},
            device_id_type=MESH,
        )

    def slot(self, piece, held):
        return self.routes[piece][0].index(held)

    def sends_of(self, piece, held):
        found = []
        for step in self.routes[piece][1]:
            for bit, source, landed in step:
                if source == held:
                    found.append(self.hop(piece, bit, held, self.slot(piece, landed)))
        found.append(self.hop(piece, 0, held, self.slot(piece, held), True))
        return found

    def start(self):
        for piece in range(len(self.routes)):
            for copy in self.sends_of(piece, ()):
                copy.start()

    def step(self, index):
        for piece, (_, steps) in enumerate(self.routes):
            for bit, _, landed in steps[index]:
                self.hop(piece, bit, landed, self.slot(piece, landed)).wait_recv()
                for copy in self.sends_of(piece, landed):
                    copy.start()

    def steps(self):
        return len(self.routes)

    def finish(self):
        for piece, (arrivals, _) in enumerate(self.routes):
            for held in arrivals:
                self.hop(piece, 0, (0,) + held, self.slot(piece, held), True).wait_recv()

    def drain(self):
        for piece, (arrivals, _) in enumerate(self.routes):
            for held in arrivals:
                for copy in self.sends_of(piece, held):
                    copy.wait_send()


FLOW_ORDER = (1, 2, 3, 0)
CUT = 4
SMALL_MIX = 10 + FF // D


def rope_lanes(length):
    half = ROT // 2
    inverse = 10000.0 ** (-2.0 * np.arange(half) / ROT)
    angles = np.arange(length)[:, None] * inverse[None, :]
    tables = np.zeros((3, length, HD), np.float32)
    tables[0] = 1.0
    tables[0, :, :half] = tables[0, :, half:ROT] = np.cos(angles)
    tables[1, :, :half] = -np.sin(angles)
    tables[2, :, half:ROT] = np.sin(angles)
    return tables


def forward_kernel(
    size,
    count,
    flows,
    w_in,
    w_out,
    small,
    rope,
    stored,
    cotangent,
    mix,
    all_in,
    all_out,
    all_normed,
    joined_out,
    slope_out,
    heads_out,
    chances_out,
    newest,
    d_newest,
    d_branch,
    weights,
    row_grads,
    mix_in_grad,
    mix_out_grad,
    w_in_low,
    w_out_low,
    normed,
    heads,
    chances,
    joined,
    slope,
    total,
    give,
    terms,
    back,
    earlier,
    dots,
    scales,
    sums,
    mix_low,
    mix_table,
    stage_sem,
    back_sem,
    earlier_sem,
    line_send,
    line_recv,
    term_send,
    term_recv,
    save_sem,
    flow_sem,
    *cube_sems,
):
    here = lax.axis_index("tensor")
    me = lax.axis_index("dp")
    own = flows.shape[1]
    rows_in = w_in.shape[0]
    length = own * size
    width_in, width_out = w_in.shape[1], w_out.shape[1]
    head_width = heads.shape[2]
    group_heads = head_width // HD
    attn_width = 3 * head_width
    units = width_in - attn_width
    bits = count.bit_length() - 1
    sides = ((0, 1), (1, -1))
    tile = 512

    def rows_of(block):
        return pl.ds(pl.multiple_of(block * own, own), own)

    def stage(source, width):
        spans = [(0, min(width, D))] + ([(D, width - D)] if width > D else [])
        return [
            pltpu.make_async_copy(
                source.at[:, pl.ds(first, span)],
                total.at[pl.ds(place * rows_in, rows_in), pl.ds(0, span)],
                stage_sem.at[place],
            )
            for place, (first, span) in enumerate(spans)
        ]

    def settle(source, width, target):
        for place, copy in enumerate(stage(source, width)):
            copy.wait()
            span = min(D, width - place * D)

            def cast(index, carry):
                low = pl.multiple_of(index * 16, 16)
                into = pl.multiple_of(me * rows_in + index * 16, 16)
                target[pl.ds(into, 16), pl.ds(place * D, span)] = total[
                    pl.ds(place * rows_in + low, 16), pl.ds(0, span)
                ].astype(bfloat)
                return carry

            lax.fori_loop(0, rows_in // 16, cast, 0)

    for copy in stage(w_in, width_in):
        copy.start()
    load_back = pltpu.make_async_copy(cotangent, back, back_sem)
    load_back.start()

    def load_earlier(layer):
        return pltpu.make_async_copy(
            stored.at[layer], earlier.at[layer % 2], earlier_sem.at[layer % 2]
        )

    load_earlier(0).start()
    enter(
        [(here < size - 1, {"tensor": here + 1}), (here > 0, {"tensor": here - 1})]
        + [(jnp.bool_(True), {"dp": plus_flips(me, (bit,))}) for bit in range(bits)]
    )

    def line_hop(side, way, step, flow):
        block = normed.at[flow, rows_of(here - way * step)]
        return pltpu.make_async_remote_copy(
            src_ref=block,
            dst_ref=block,
            send_sem=line_send.at[side, step, flow],
            recv_sem=line_recv.at[side, step, flow],
            device_id={"tensor": here + way},
            device_id_type=MESH,
        )

    def line_landed(side, way, step, flow):
        block = normed.at[flow, rows_of(here - way * step)]
        return pltpu.make_async_remote_copy(
            src_ref=block,
            dst_ref=block,
            send_sem=line_send.at[side, step - 1, flow],
            recv_sem=line_recv.at[side, step - 1, flow],
            device_id={"tensor": here - way},
            device_id_type=MESH,
        )

    def has_next(way):
        return here < size - 1 if way > 0 else here > 0

    def has_origin(way, step):
        return here >= step if way > 0 else here < size - step

    def keep_flow(flow, block):
        return pltpu.make_async_copy(
            normed.at[flow, rows_of(block)],
            all_normed.at[flow, rows_of(block)],
            flow_sem.at[flow, block],
        )

    for flow in FLOW_ORDER:
        which = 2 if flow == 3 else 0

        def normalize(index, carry):
            spot = pl.ds(pl.multiple_of(index * 16, 16), 16)
            values = flows[flow, spot].astype(single)
            centred = values - jnp.mean(values, axis=-1, keepdims=True)
            inverse = lax.rsqrt(jnp.mean(centred * centred, axis=-1, keepdims=True) + norm_eps)
            into = pl.ds(pl.multiple_of(here * own + index * 16, 16), 16)
            normed[flow, into] = (
                centred * inverse * small[which : which + 1, :] + small[which + 1 : which + 2, :]
            ).astype(bfloat)
            return carry

        lax.fori_loop(0, own // 16, normalize, 0)
        if flow:
            for side, way in sides:
                pl.when(has_next(way))(line_hop(side, way, 0, flow).start)
        keep_flow(flow, here).start()

    cube_in = CubeGather(w_in_low, rows_in, count, cube_sems[:4])
    cube_out = CubeGather(w_out_low, rows_in, count, cube_sems[4:])
    settle(w_in, width_in, w_in_low)
    cube_in.start()
    for copy in stage(w_out, width_out):
        copy.start()
    settle(w_out, width_out, w_out_low)
    mix_low[...] = jnp.zeros_like(mix_low)
    mix_low[0:MIXH] = small[SMALL_MIX : SMALL_MIX + MIXH].astype(bfloat)
    mix_table[...] = jnp.zeros_like(mix_table)
    mix_table[0:MIXH, 0:MIXH] = mix[0:MIXH]
    mix_table[HD : HD + 1, 0:MIXH] = mix[MIXH : MIXH + 1]
    lane = lax.broadcasted_iota(jnp.int32, (16, HD), 1)
    load_back.wait()
    for layer in range(LAYER):
        if layer + 1 < LAYER:
            load_earlier(layer + 1).start()
        load_earlier(layer).wait()

        def correlate(index, carry):
            spot = pl.ds(pl.multiple_of(index * 16, 16), 16)
            held = earlier[layer % 2, spot].astype(single)
            found = jnp.zeros((16, HD), single) if layer == 0 else dots[spot]
            for stream in range(STREAMS):
                value = jnp.sum(back[stream, spot].astype(single) * held, axis=-1, keepdims=True)
                found = found + jnp.where(lane == stream * LAYERS + layer, value, 0.0)
            dots[spot] = found
            return carry

        lax.fori_loop(0, own // 16, correlate, 0)

    def line_step(step, flow_list):
        for flow in flow_list:
            for side, way in sides:

                @pl.when(has_origin(way, step))
                def _():
                    line_landed(side, way, step, flow).wait_recv()
                    pl.when(has_next(way))(line_hop(side, way, step, flow).start)
                    keep_flow(flow, here - way * step).start()

    def at_distance(step, action):
        if step == 0:
            action(here)
            return

        def one(side, carry):
            block = here - step + 2 * step * side

            @pl.when(jnp.logical_and(block >= 0, block < size))
            def _():
                action(block)

            return carry

        lax.fori_loop(0, 2, one, 0)

    def project(block, part):
        rows = rows_of(block)
        source = normed[part, rows]
        pre = jnp.dot(
            source,
            jnp.concatenate(
                [
                    w_in_low[:, pl.ds((head * 3 + part) * HD, HD)]
                    for head in range(group_heads)
                ],
                axis=1,
            ),
            preferred_element_type=single,
        )
        first = pl.multiple_of(here * head_width, HD)
        pre = pre + small[5 + part : 6 + part, pl.ds(first, head_width)]
        if part == 2:
            heads[part, rows] = pre.astype(bfloat)
            return
        cosine, sine_low, sine_high = rope[0, rows], rope[1, rows], rope[2, rows]
        for head in range(group_heads):
            values = pre[:, head * HD : (head + 1) * HD]
            turned = (
                values * cosine
                + pltpu.roll(values, HD - ROT // 2, 1) * sine_low
                + pltpu.roll(values, ROT // 2, 1) * sine_high
            )
            heads[part, rows, pl.ds(head * HD, HD)] = turned.astype(bfloat)

    def expand(block):
        rows = rows_of(block)

        def one(index, carry):
            first = pl.multiple_of(index * tile, tile)
            pre = jnp.dot(
                normed[3, rows],
                w_in_low[:, pl.ds(attn_width + first, tile)],
                preferred_element_type=single,
            )
            pre = pre + small[pl.ds(10 + here, 1), pl.ds(first, tile)]
            normal = 0.5 * (1.0 + lax.erf(pre * 0.7071067811865476))
            joined[rows, pl.ds(head_width + first, tile)] = (pre * normal).astype(bfloat)
            slope[rows, pl.ds(first, tile)] = (
                normal + pre * jnp.exp(-0.5 * pre * pre) * 0.3989422804014327
            ).astype(bfloat)
            return carry

        lax.fori_loop(0, units // tile, one, 0)

    def contract(block):
        rows = rows_of(block)

        def one(index, carry):
            first = pl.multiple_of(index * tile, tile)
            total[rows, pl.ds(first, tile)] = contract_last(
                joined[rows, pl.ds(head_width, units)],
                w_out_low[pl.ds(first, tile), pl.ds(head_width, units)],
            )
            return carry

        lax.fori_loop(0, D // tile, one, 0)

    def attend(block):
        rows = rows_of(block)
        places = block * own + lax.broadcasted_iota(jnp.int32, (own, length), 0)
        allowed = lax.broadcasted_iota(jnp.int32, (own, length), 1) <= places
        for head in range(group_heads):
            lanes = pl.ds(head * HD, HD)
            scores = contract_last(heads[0, rows, lanes], heads[1, :, lanes]) * HD ** (-0.5)
            scores = jnp.where(allowed, scores, masked_score)
            raised = jnp.exp(scores - jnp.max(scores, axis=-1, keepdims=True))
            low = (raised / jnp.sum(raised, axis=-1, keepdims=True)).astype(bfloat)
            chances[head, rows] = low
            joined[rows, lanes] = jnp.dot(
                low, heads[2, :, lanes], preferred_element_type=single
            ).astype(bfloat)

    def finish_block(block):
        attend(block)
        rows = rows_of(block)

        def one(index, carry):
            first = pl.multiple_of(index * tile, tile)
            spot = (rows, pl.ds(first, tile))
            give[spot] = (
                total[spot]
                + contract_last(
                    joined[rows, pl.ds(0, head_width)],
                    w_out_low[pl.ds(first, tile), pl.ds(0, head_width)],
                )
            ).astype(bfloat)
            return carry

        lax.fori_loop(0, D // tile, one, 0)

    def save(place, source, target):
        return pltpu.make_async_copy(source, target, save_sem.at[place])

    chain = LineSum(size, give, terms, term_send, term_recv, CUT)
    ending = jnp.logical_or(here == 0, here == size - 1)

    def query_pass(side, way, step):
        @pl.when(has_origin(way, step))
        def _():
            line_landed(side, way, step, 0).wait_recv()
            pl.when(has_next(way))(line_hop(side, way, step, 0).start)
            keep_flow(0, here - way * step).start()

    def query_side(side, way):
        for step in range(size - 1, 0, -1):
            query_pass(side, way, step)
        pl.when(has_next(way))(line_hop(side, way, 0, 0).start)

    cube_in.step(0)
    cube_out.start()
    line_step(1, FLOW_ORDER[:3])
    lower = 2 * here < size
    pl.when(lower)(lambda: query_side(0, 1))
    pl.when(jnp.logical_not(lower))(lambda: query_side(1, -1))
    for index in range(1, cube_in.steps()):
        cube_in.step(index)
    cube_in.finish()
    save(0, w_in_low, all_in).start()

    def early(block):
        project(block, 1)
        project(block, 2)
        expand(block)

    at_distance(0, early)
    line_step(2, FLOW_ORDER[:3])
    at_distance(1, early)
    cube_out.step(0)
    at_distance(2, early)
    project(here, 0)

    @pl.when(jnp.logical_not(ending))
    def _():
        pl.when(lower)(lambda: query_side(1, -1))
        pl.when(jnp.logical_not(lower))(lambda: query_side(0, 1))

    for index in range(1, cube_out.steps()):
        cube_out.step(index)
    cube_out.finish()
    save(1, w_out_low, all_out).start()
    for step in range(min(3, size)):
        at_distance(step, contract)
    for step in range(3, size):
        line_step(step, FLOW_ORDER[:3])

        def rest(block):
            early(block)
            contract(block)

        at_distance(step, rest)
    finish_block(here)

    @pl.when(jnp.logical_not(ending))
    def _():
        def one(index, carry):
            block = lax.rem(here + 1 + index, size)
            project(block, 0)
            finish_block(block)
            return carry

        lax.fori_loop(0, size - 1, one, 0)

    for rank in range(size - 1):
        step = size - 1 - rank

        @pl.when(ending)
        def _():
            dest = lax.select(here == 0, size - 1 - rank, rank)
            side = lax.select(here == 0, 1, 0)
            block = normed.at[0, rows_of(dest)]
            pltpu.make_async_remote_copy(
                src_ref=block,
                dst_ref=block,
                send_sem=line_send.at[side, step - 1, 0],
                recv_sem=line_recv.at[side, step - 1, 0],
                device_id={"tensor": lax.select(here == 0, 1, size - 2)},
                device_id_type=MESH,
            ).wait_recv()
            keep_flow(0, dest).start()
            project(dest, 0)
            finish_block(dest)

        for way in (chain.near, -chain.near):
            chain.relay(way, chain.far(rank, way))

    saves = [
        save(2, joined, joined_out),
        save(3, slope, slope_out),
        save(4, heads, heads_out),
        save(5, chances, chances_out),
    ]
    for copy in saves:
        copy.start()
    for place in range(CUT):
        chain.collect(place, newest)

    def sixteen(index):
        spot = pl.ds(pl.multiple_of(index * 16, 16), 16)
        return spot, pl.ds(pl.multiple_of(here * own + index * 16, 16), 16)

    def compose(index, carry):
        spot, inner = sixteen(index)
        value = flows[3, spot].astype(single) + newest[spot] + small[8:9, :] + small[9:10, :]
        newest[spot] = value
        inverse = lax.rsqrt(jnp.mean(value * value, axis=-1, keepdims=True) + mix_eps)
        scales[spot] = jnp.broadcast_to(inverse, (16, HD))
        give[inner] = (value * inverse * small[4:5, :]).astype(bfloat)
        found = dots[spot]
        for stream in range(STREAMS):
            dot = jnp.sum(back[stream, spot].astype(single) * value, axis=-1, keepdims=True)
            found = found + jnp.where(lane == stream * LAYERS + LAYER, dot, 0.0)
        dots[spot] = found
        return carry

    lax.fori_loop(0, own // 16, compose, 0)
    mix_normed = give[rows_of(here)]
    mix_pre = contract_last(mix_normed, mix_low[...])
    normal = 0.5 * (1.0 + lax.erf(mix_pre * 0.7071067811865476))
    act = mix_pre * normal
    act_slope = normal + mix_pre * jnp.exp(-0.5 * mix_pre * mix_pre) * 0.3989422804014327
    table = mix_table[0:HD]
    weights[...] = (
        jnp.dot(act, table, precision=highest_precision, preferred_element_type=single)
        + mix_table[HD : HD + 1]
    )
    d_mixing = dots[...]
    d_act = lax.dot_general(
        d_mixing,
        table,
        (((1,), (1,)), ((), ())),
        precision=highest_precision,
        preferred_element_type=single,
    )
    d_mix_pre = (d_act * act_slope).astype(bfloat)
    out_grad = lax.dot_general(
        act,
        d_mixing,
        (((0,), (0,)), ((), ())),
        precision=highest_precision,
        preferred_element_type=single,
    )
    mix_out_grad[...] = jnp.zeros_like(mix_out_grad)
    mix_out_grad[0:MIXH] = out_grad[0:MIXH]
    mix_out_grad[MIXH : MIXH + 1] = jnp.sum(d_mixing, axis=0, keepdims=True)

    def spread(index, carry):
        lanes = pl.ds(pl.multiple_of(index * tile, tile), tile)
        total[0:own, lanes] = jnp.dot(
            d_mix_pre, mix_low[:, lanes], preferred_element_type=single
        )
        mix_in_grad[:, lanes] = contract_first(d_mix_pre, give[rows_of(here), lanes])[
            0 : mix_in_grad.shape[0]
        ]
        return carry

    lax.fori_loop(0, D // tile, spread, 0)
    sums[...] = jnp.zeros_like(sums)

    def descend(index, carry):
        spot, inner = sixteen(index)
        value, inverse = newest[spot], scales[spot][:, 0:1]
        d_normed = total[spot]
        scaled = d_normed * small[4:5, :]
        middle = jnp.mean(scaled * value, axis=-1, keepdims=True)
        result = inverse * scaled - value * (inverse * inverse * inverse * middle)
        for stream in range(STREAMS):
            column = stream * LAYERS + LAYER
            result = result + weights[spot][:, column : column + 1] * back[stream, spot].astype(
                single
            )
        d_newest[spot] = result
        d_branch[spot] = result.astype(bfloat)
        gain = d_normed * value * inverse
        sums[0] += gain[0:8] + gain[8:16]
        sums[1] += result[0:8] + result[8:16]
        return carry

    lax.fori_loop(0, own // 16, descend, 0)
    row_grads[0:1] = jnp.sum(sums[0], axis=0, keepdims=True)
    row_grads[1:2] = jnp.sum(sums[1], axis=0, keepdims=True)
    for step in range(size):
        for flow in FLOW_ORDER:
            for side, way in sides:

                @pl.when(jnp.logical_and(has_next(way), has_origin(way, step)))
                def _():
                    line_hop(side, way, step, flow).wait_send()

    cube_in.drain()
    cube_out.drain()
    chain.drain()
    for flow in FLOW_ORDER:
        for block in range(size):
            keep_flow(flow, block).wait()
    save(0, w_in_low, all_in).wait()
    save(1, w_out_low, all_out).wait()
    for copy in saves:
        copy.wait()


def forward(flows, w_in, w_out, small, rope, stored, cotangent, mix_weights, size, count, identity):
    own = flows.shape[1]
    length = own * size
    rows, width_in = w_in.shape
    width_out = w_out.shape[1]
    head_width = HEADS // size * HD
    units = FF // size
    pieces = count.bit_length() - 2
    cube = [pltpu.SemaphoreType.DMA((pieces, 2**pieces))] * 8
    low = lambda *shape: jax.ShapeDtypeStruct(shape, bfloat)
    hbm = pl.BlockSpec(memory_space=pl.ANY)
    vmem = pl.BlockSpec(memory_space=pltpu.VMEM)
    return pl.pallas_call(
        lambda *refs: forward_kernel(size, count, *refs),
        out_shape=[
            low(D, width_in),
            low(D, width_out),
            low(STREAMS, length, D),
            low(length, width_out),
            low(length, units),
            low(3, length, head_width),
            low(HEADS // size, length, length),
            jax.ShapeDtypeStruct((own, D), single),
            jax.ShapeDtypeStruct((own, D), single),
            low(own, D),
            jax.ShapeDtypeStruct((own, HD), single),
            jax.ShapeDtypeStruct((8, D), single),
            jax.ShapeDtypeStruct((40, D), single),
            jax.ShapeDtypeStruct((40, HD), single),
        ],
        in_specs=[vmem, hbm, hbm, vmem, vmem, hbm, hbm, vmem],
        out_specs=[hbm] * 7 + [vmem] * 7,
        scratch_shapes=[
            pltpu.VMEM((D, width_in), bfloat),
            pltpu.VMEM((D, width_out), bfloat),
            pltpu.VMEM((STREAMS, length, D), bfloat),
            pltpu.VMEM((3, length, head_width), bfloat),
            pltpu.VMEM((HEADS // size, length, length), bfloat),
            pltpu.VMEM((length, width_out), bfloat),
            pltpu.VMEM((length, units), bfloat),
            pltpu.VMEM((length, D), single),
            pltpu.VMEM((length, D), bfloat),
            pltpu.VMEM((size + 1, own, D), bfloat),
            pltpu.VMEM((STREAMS, own, D), bfloat),
            pltpu.VMEM((2, own, D), bfloat),
            pltpu.VMEM((own, HD), single),
            pltpu.VMEM((own, HD), single),
            pltpu.VMEM((2, 8, D), single),
            pltpu.VMEM((HD, D), bfloat),
            pltpu.VMEM((HD + 8, HD), single),
            pltpu.SemaphoreType.DMA((2,)),
            pltpu.SemaphoreType.DMA,
            pltpu.SemaphoreType.DMA((2,)),
            pltpu.SemaphoreType.DMA((2, size, STREAMS)),
            pltpu.SemaphoreType.DMA((2, size, STREAMS)),
            pltpu.SemaphoreType.DMA((2, size, CUT)),
            pltpu.SemaphoreType.DMA((2, size, CUT)),
            pltpu.SemaphoreType.DMA((6,)),
            pltpu.SemaphoreType.DMA((STREAMS, size)),
        ]
        + cube,
        compiler_params=pltpu.CompilerParams(
            collective_id=identity, has_side_effects=True, vmem_limit_bytes=60 * 2**20
        ),
        name="forward_%d" % identity,
    )(flows, w_in, w_out, small, rope, stored, cotangent, mix_weights)


def backward_kernel(
    size,
    d_branch,
    rope,
    all_in,
    all_out,
    slope_in,
    heads_in,
    chances_in,
    all_back,
    all_up,
    all_pre,
    all_normed,
    d_residual,
    bias_grads,
    w_in_low,
    w_out_low,
    slope,
    heads,
    chances,
    back,
    d_heads,
    d_up,
    d_pre,
    part,
    terms,
    d_normed,
    load_sem,
    line_send,
    line_recv,
    term_send,
    term_recv,
    save_sem,
):
    here = lax.axis_index("tensor")
    own = d_branch.shape[0]
    length = own * size
    head_width = heads.shape[2]
    group_heads = head_width // HD
    attn_width = 3 * head_width
    units = slope.shape[1]
    sides = ((0, 1), (1, -1))
    tile = 512
    scale = HD ** (-0.5)

    def rows_of(block):
        return pl.ds(pl.multiple_of(block * own, own), own)

    loads = [
        pltpu.make_async_copy(source, target, load_sem.at[place])
        for place, (source, target) in enumerate(
            [
                (all_out, w_out_low),
                (slope_in, slope),
                (all_in, w_in_low),
                (heads_in, heads),
                (chances_in, chances),
            ]
        )
    ]
    enter([(here < size - 1, {"tensor": here + 1}), (here > 0, {"tensor": here - 1})])

    def has_next(way):
        return here < size - 1 if way > 0 else here > 0

    def has_origin(way, step):
        return here >= step if way > 0 else here < size - step

    def line_hop(side, way, step):
        block = back.at[rows_of(here - way * step)]
        return pltpu.make_async_remote_copy(
            src_ref=d_branch if step == 0 else block,
            dst_ref=block,
            send_sem=line_send.at[side, step],
            recv_sem=line_recv.at[side, step],
            device_id={"tensor": here + way},
            device_id_type=MESH,
        )

    def line_landed(side, way, step):
        block = back.at[rows_of(here - way * step)]
        return pltpu.make_async_remote_copy(
            src_ref=block,
            dst_ref=block,
            send_sem=line_send.at[side, step - 1],
            recv_sem=line_recv.at[side, step - 1],
            device_id={"tensor": here - way},
            device_id_type=MESH,
        )

    for side, way in sides:
        pl.when(has_next(way))(line_hop(side, way, 0).start)
    for copy in loads:
        copy.start()
    back[rows_of(here)] = d_branch[...]

    def pull(block):
        rows = rows_of(block)
        d_heads[rows] = jnp.dot(
            back[rows], w_out_low[:, 0:head_width], preferred_element_type=single
        ).astype(bfloat)

        def one(index, carry):
            first = pl.multiple_of(index * tile, tile)
            d_hidden = jnp.dot(
                back[rows],
                w_out_low[:, pl.ds(head_width + first, tile)],
                preferred_element_type=single,
            )
            d_up[rows, pl.ds(first, tile)] = (
                d_hidden * slope[rows, pl.ds(first, tile)].astype(single)
            ).astype(bfloat)
            return carry

        lax.fori_loop(0, units // tile, one, 0)

    def push(block):
        rows = rows_of(block)

        def one(index, carry):
            first = pl.multiple_of(index * tile, tile)
            part[rows, pl.ds(first, tile)] = contract_last(
                d_up[rows], w_in_low[pl.ds(first, tile), pl.ds(attn_width, units)]
            ).astype(bfloat)
            return carry

        lax.fori_loop(0, D // tile, one, 0)

    chain = LineSum(size, part, terms, term_send, term_recv, CUT)
    ending = jnp.logical_or(here == 0, here == size - 1)

    def stage(step):
        for way in (chain.near, -chain.near):
            chain.relay(way, chain.far(size - 1 - step, way))

    loads[0].wait()
    loads[1].wait()
    pull(here)
    for step in range(1, size):
        for side, way in sides:

            @pl.when(has_origin(way, step))
            def _():
                line_landed(side, way, step).wait_recv()
                pl.when(has_next(way))(line_hop(side, way, step).start)

        if step == 1:
            loads[2].wait()

        def both(side, carry):
            block = here - step + 2 * step * side

            @pl.when(jnp.logical_and(block >= 0, block < size))
            def _():
                pull(block)
                push(block)

            return carry

        lax.fori_loop(0, 2, both, 0)
        pl.when(ending)(lambda: stage(step))
    saves = [
        pltpu.make_async_copy(source, target, save_sem.at[place])
        for place, (source, target) in enumerate(
            [(back, all_back), (d_up, all_up), (d_pre, all_pre)]
        )
    ]
    saves[0].start()
    saves[1].start()
    loads[3].wait()
    loads[4].wait()
    bias_grads[...] = jnp.zeros_like(bias_grads)
    half_rows = length // 2

    def turn_back(gradients, rows):
        return (
            gradients * rope[0, rows]
            - pltpu.roll(gradients, HD - ROT // 2, 1) * rope[1, rows]
            - pltpu.roll(gradients, ROT // 2, 1) * rope[2, rows]
        )

    for head in range(group_heads):
        lanes = pl.ds(head * HD, HD)
        d_keys = jnp.zeros((length, HD), single)
        d_values = jnp.zeros((length, HD), single)
        query_bias = jnp.zeros((1, HD), single)
        for half in range(2):
            rows = pl.ds(half * half_rows, half_rows)
            low = chances[head, rows]
            chance = low.astype(single)
            d_chance = contract_last(d_heads[rows, lanes], heads[2, :, lanes])
            centre = jnp.sum(d_chance * chance, axis=-1, keepdims=True)
            d_score = (chance * (d_chance - centre)).astype(bfloat)
            d_query = (
                jnp.dot(d_score, heads[1, :, lanes], preferred_element_type=single) * scale
            )
            d_query = turn_back(d_query, rows).astype(bfloat)
            d_pre[0, rows, lanes] = d_query
            query_bias = query_bias + jnp.sum(d_query.astype(single), axis=0, keepdims=True)
            d_keys = d_keys + contract_first(d_score, heads[0, rows, lanes])
            d_values = d_values + contract_first(low, d_heads[rows, lanes])
        whole = pl.ds(0, length)
        d_key = turn_back(d_keys * scale, whole).astype(bfloat)
        d_value = d_values.astype(bfloat)
        d_pre[1, :, lanes] = d_key
        d_pre[2, :, lanes] = d_value
        bias_grads[0:1, lanes] = query_bias
        bias_grads[1:2, lanes] = jnp.sum(d_key.astype(single), axis=0, keepdims=True)
        bias_grads[2:3, lanes] = jnp.sum(d_value.astype(single), axis=0, keepdims=True)
    saves[2].start()
    for step in range(1, size - 1):
        pl.when(jnp.logical_not(ending))(lambda: stage(step))
    for which in range(3):

        def one(index, carry):
            first = pl.multiple_of(index * tile, tile)
            d_normed[which, :, pl.ds(first, tile)] = contract_last(
                d_pre[which],
                jnp.concatenate(
                    [
                        w_in_low[pl.ds(first, tile), pl.ds((head * 3 + which) * HD, HD)]
                        for head in range(group_heads)
                    ],
                    axis=1,
                ),
            ).astype(bfloat)
            return carry

        lax.fori_loop(0, D // tile, one, 0)
        saves.append(
            pltpu.make_async_copy(
                d_normed.at[which], all_normed.at[which], save_sem.at[3 + which]
            )
        )
        saves[-1].start()
    push(here)
    def unit_sum(index, carry):
        lanes = pl.ds(pl.multiple_of(index * 256, 256), 256)
        bias_grads[3:4, lanes] = jnp.sum(d_up[:, lanes].astype(single), axis=0, keepdims=True)
        return carry

    lax.fori_loop(0, units // 256, unit_sum, 0)
    pl.when(jnp.logical_not(ending))(lambda: stage(size - 1))
    for place in range(CUT):
        chain.collect(place, d_residual)
    for step in range(size):
        for side, way in sides:

            @pl.when(jnp.logical_and(has_next(way), has_origin(way, step)))
            def _():
                line_hop(side, way, step).wait_send()

    chain.drain()
    for copy in saves:
        copy.wait()


def backward(d_branch, rope, all_in, all_out, slope, heads, chances, size, identity):
    own = d_branch.shape[0]
    length = own * size
    head_width = heads.shape[2]
    units = slope.shape[1]
    low = lambda *shape: jax.ShapeDtypeStruct(shape, bfloat)
    wide = lambda *shape: jax.ShapeDtypeStruct(shape, single)
    hbm = pl.BlockSpec(memory_space=pl.ANY)
    vmem = pl.BlockSpec(memory_space=pltpu.VMEM)
    return pl.pallas_call(
        lambda *refs: backward_kernel(size, *refs),
        out_shape=[
            low(length, D),
            low(length, units),
            low(3, length, head_width),
            low(3, length, D),
            wide(own, D),
            wide(8, D),
        ],
        in_specs=[vmem] * 2 + [hbm] * 5,
        out_specs=[hbm] * 4 + [vmem] * 2,
        scratch_shapes=[
            pltpu.VMEM(all_in.shape, bfloat),
            pltpu.VMEM(all_out.shape, bfloat),
            pltpu.VMEM(slope.shape, bfloat),
            pltpu.VMEM(heads.shape, bfloat),
            pltpu.VMEM(chances.shape, bfloat),
            pltpu.VMEM((length, D), bfloat),
            pltpu.VMEM((length, head_width), bfloat),
            pltpu.VMEM((length, units), bfloat),
            pltpu.VMEM((3, length, head_width), bfloat),
            pltpu.VMEM((length, D), bfloat),
            pltpu.VMEM((size + 1, own, D), bfloat),
            pltpu.VMEM((3, length, D), bfloat),
            pltpu.SemaphoreType.DMA((5,)),
            pltpu.SemaphoreType.DMA((2, size)),
            pltpu.SemaphoreType.DMA((2, size)),
            pltpu.SemaphoreType.DMA((2, size, CUT)),
            pltpu.SemaphoreType.DMA((2, size, CUT)),
            pltpu.SemaphoreType.DMA((6,)),
        ],
        compiler_params=pltpu.CompilerParams(
            collective_id=identity, has_side_effects=True, vmem_limit_bytes=60 * 2**20
        ),
        name="backward_%d" % identity,
    )(d_branch, rope, all_in, all_out, slope, heads, chances)


def scatter_kernel(
    size,
    count,
    all_normed,
    d_normed,
    back_in,
    joined_in,
    up_in,
    pre_in,
    flows_in,
    small,
    d_residual,
    d_newest,
    grad_in,
    grad_out,
    d_flows,
    norm_grads,
    squares,
    back,
    joined,
    d_up,
    d_pre,
    tiles,
    kept_in,
    kept_out,
    pair_in,
    pair_out,
    give_in,
    give_out,
    land_in,
    land_out,
    parts,
    terms,
    flows,
    total,
    sums,
    work,
    load_sem,
    tile_sem,
    flow_sem,
    give_sem,
    pair_sem,
    credit,
    cube_send,
    cube_recv,
    line_send,
    line_recv,
    save_sem,
):
    here = lax.axis_index("tensor")
    me = lax.axis_index("dp")
    bits = count.bit_length() - 1
    routes = cube_routes(bits)
    pieces = len(routes)
    subsets = sorted(routes[0][0], key=lambda held: -len(held))
    own = flows.shape[1]
    length = own * size
    rows = pair_in.shape[0]
    piece_rows = rows // pieces
    lane_rows = tiles.shape[3]
    head_width = d_pre.shape[2]
    group_heads = head_width // HD
    attn_width = 3 * head_width
    units = d_up.shape[1]
    tile = 512
    kept, pair, give, land = (
        (kept_out, kept_in),
        (pair_out, pair_in),
        (give_out, give_in),
        (land_out, land_in),
    )
    widths = (kept_out.shape[1], kept_in.shape[1])

    loads = [
        pltpu.make_async_copy(source, target, load_sem.at[place])
        for place, (source, target) in enumerate(
            [(d_normed.at[which], parts.at[which]) for which in range(3)]
            + [(back_in, back), (joined_in, joined), (up_in, d_up), (pre_in, d_pre)]
        )
    ]

    def first_lane(held):
        return pl.multiple_of(plus_flips(me, held) * rows // lane_rows * lane_rows, HD)

    def load_tile(slot, held):
        return pltpu.make_async_copy(
            all_normed.at[:, :, pl.ds(first_lane(held), lane_rows)],
            tiles.at[slot],
            tile_sem.at[slot],
        )

    def load_flow(flow):
        return pltpu.make_async_copy(
            flows_in.at[flow], flows.at[flow % 2], flow_sem.at[flow % 2]
        )

    for copy in loads:
        copy.start()
    load_tile(0, (0,) + subsets[0]).start()
    load_tile(1, subsets[0]).start()
    load_flow(3).start()
    load_flow(0).start()
    enter(
        [(here < size - 1, {"tensor": here + 1}), (here > 0, {"tensor": here - 1})]
        + [(jnp.bool_(True), {"dp": plus_flips(me, (bit,))}) for bit in range(bits)]
    )
    ending = jnp.logical_or(here == 0, here == size - 1)
    chains = [
        LineSum(size, parts.at[which], terms.at[which], line_send.at[which], line_recv.at[which], 1)
        for which in range(3)
    ]

    def relay(rank):
        for sign in (1, -1):
            for chain in chains:
                chain.relay(sign * chain.near, chain.far(rank, sign * chain.near))

    for which in range(3):
        loads[which].wait()
    for rank in range(size - 1):
        pl.when(ending)(lambda: relay(rank))

    def own_rows(value, held):
        if lane_rows == rows:
            return value
        work[:, 0 : value.shape[1]] = value
        first = lax.rem(plus_flips(me, held) * rows, lane_rows)
        return work[pl.ds(pl.multiple_of(first, 16), rows), 0 : value.shape[1]]

    def products(which, held, slot, emit):
        if which == 0:
            source = back[:, pl.ds(first_lane(held), lane_rows)]

            def one(index, carry):
                first = pl.multiple_of(index * tile, tile)
                emit(own_rows(contract_first(source, joined[:, pl.ds(first, tile)]), held), first)
                return carry

            lax.fori_loop(0, widths[0] // tile, one, 0)
            return
        for part in range(3):
            value = own_rows(contract_first(tiles[slot, part], d_pre[part]), held)
            for head in range(group_heads):
                emit(value[:, head * HD : (head + 1) * HD], (head * 3 + part) * HD)

        def one(index, carry):
            first = pl.multiple_of(index * tile, tile)
            value = contract_first(tiles[slot, 3], d_up[:, pl.ds(first, tile)])
            emit(own_rows(value, held), attn_width + first)
            return carry

        lax.fori_loop(0, units // tile, one, 0)

    def place_of(held):
        return sum(2 ** (bit - 1) for bit in held)

    def pass_pair(which):
        return pltpu.make_async_remote_copy(
            src_ref=give[which],
            dst_ref=pair[which],
            send_sem=give_sem.at[which],
            recv_sem=pair_sem.at[which],
            device_id={"dp": plus_flips(me, (0,))},
            device_id_type=MESH,
        )

    def kept_rows(piece, held):
        return pl.ds(place_of(held) * rows + piece * piece_rows, piece_rows)

    def land_rows(piece, landed):
        slot = piece * (len(subsets) - 1) + place_of(landed) - 1
        return pl.ds(slot * piece_rows, piece_rows)

    def cube_hop(which, piece, bit, landed):
        return pltpu.make_async_remote_copy(
            src_ref=kept[which].at[kept_rows(piece, landed)],
            dst_ref=land[which].at[land_rows(piece, landed)],
            send_sem=cube_send.at[which, piece, place_of(landed)],
            recv_sem=cube_recv.at[which, piece, place_of(landed)],
            device_id={"dp": plus_flips(me, (bit,))},
            device_id_type=MESH,
        )

    def needs(piece, held):
        return [
            (bit, landed)
            for step in routes[piece][1]
            for bit, source, landed in step
            if source == held
        ]

    def add_landed(which, piece, held):
        for bit, landed in needs(piece, held):
            cube_hop(which, piece, bit, landed).wait_recv()

        def one(index, carry):
            def column(at, inner):
                lanes = pl.ds(pl.multiple_of(at * tile, tile), tile)
                spot = pl.ds(
                    pl.multiple_of(kept_rows(piece, held).start + index * 16, 16), 16
                )
                value = kept[which][spot, lanes].astype(single)
                for _, landed in needs(piece, held):
                    arrived = pl.ds(
                        pl.multiple_of(land_rows(piece, landed).start + index * 16, 16), 16
                    )
                    value = value + land[which][arrived, lanes].astype(single)
                kept[which][spot, lanes] = value.astype(bfloat)
                if not held:
                    value = value * value
                    value = value[0:8] + value[8:16]
                    for group in range(tile // HD):
                        inner = inner + value[:, group * HD : (group + 1) * HD]
                return inner

            return lax.fori_loop(0, widths[which] // tile, column, carry)

        found = lax.fori_loop(0, piece_rows // 16, one, jnp.zeros((8, HD), single))
        if not held:
            squares[...] += found

    for copy in loads[3:]:
        copy.wait()
    last = len(subsets) - 1
    for index, held in enumerate(subsets):
        load_tile(0, (0,) + held).wait()
        for which in range(2):
            if index > 0:
                pass_pair(which).wait_send()

            def emit(value, first):
                give[which][:, pl.ds(first, value.shape[1])] = value.astype(bfloat)

            products(which, (0,) + held, 0, emit)
            if index > 0:
                pl.semaphore_wait(credit.at[which], 1)
            pass_pair(which).start()
        if index < last:
            load_tile(0, (0,) + subsets[index + 1]).start()
        load_tile(1, held).wait()
        for which in range(2):
            pass_pair(which).wait_recv()

            def emit(value, first):
                lanes = pl.ds(first, value.shape[1])
                kept[which][pl.ds(place_of(held) * rows, rows), lanes] = (
                    value + pair[which][:, lanes].astype(single)
                ).astype(bfloat)

            products(which, held, 1, emit)
            if index < last:
                pl.semaphore_signal(
                    credit.at[which],
                    inc=1,
                    device_id={"dp": plus_flips(me, (0,))},
                    device_id_type=MESH,
                )
            for piece, (_, steps) in enumerate(routes):
                for bit, _, landed in steps[-1]:
                    if landed == held:
                        cube_hop(which, piece, bit, landed).start()
        if index < last:
            load_tile(1, subsets[index + 1]).start()

    sums[...] = jnp.zeros_like(sums)

    def descend(flow, gradient):
        load_flow(flow).wait()
        gain = 2 if flow == 3 else 0

        def one(index, carry):
            spot = pl.ds(pl.multiple_of(index * 16, 16), 16)
            values = flows[flow % 2, spot].astype(single)
            centred = values - jnp.mean(values, axis=-1, keepdims=True)
            inverse = lax.rsqrt(jnp.mean(centred * centred, axis=-1, keepdims=True) + norm_eps)
            unit = centred * inverse
            incoming = gradient[spot]
            scaled = incoming * small[gain : gain + 1, :]
            result = inverse * (
                scaled
                - jnp.mean(scaled, axis=-1, keepdims=True)
                - unit * jnp.mean(scaled * unit, axis=-1, keepdims=True)
            )
            if flow == 3:
                result = result + d_newest[spot]
            d_flows[flow, spot] = result.astype(bfloat)
            unit = unit * incoming
            sums[gain] += unit[0:8] + unit[8:16]
            sums[gain + 1] += incoming[0:8] + incoming[8:16]
            return carry

        lax.fori_loop(0, own // 16, one, 0)

    descend(3, d_residual)
    load_flow(1).start()
    pl.when(jnp.logical_not(ending))(lambda: relay(0))
    for step in range(pieces - 2, -1, -1):
        for which in range(2):
            for piece, (_, steps) in enumerate(routes):
                for bit, _, landed in steps[step]:
                    add_landed(which, piece, landed)
                    cube_hop(which, piece, bit, landed).start()
    for rank in range(1, size - 1):
        pl.when(jnp.logical_not(ending))(lambda: relay(rank))
    for which in range(3):
        chains[which].collect(0, total)
        descend(which, total)
        if which == 0:
            load_flow(2).start()
    norm_grads[...] = jnp.zeros_like(norm_grads)
    for row in range(4):
        norm_grads[row : row + 1] = jnp.sum(sums[row], axis=0, keepdims=True)
    squares[...] = jnp.zeros_like(squares)
    saves = []
    for which, target in enumerate((grad_out, grad_in)):
        for piece in range(pieces):
            add_landed(which, piece, ())
        saves.append(
            pltpu.make_async_copy(kept[which].at[pl.ds(0, rows)], target, save_sem.at[which])
        )
        saves[-1].start()
    for which in range(2):
        pass_pair(which).wait_send()
        for piece, (_, steps) in enumerate(routes):
            for step in steps:
                for bit, _, landed in step:
                    cube_hop(which, piece, bit, landed).wait_send()
    for chain in chains:
        chain.drain()
    for copy in saves:
        copy.wait()


def scatter(
    all_normed, d_normed, back, joined, d_up, d_pre, flows, small, d_residual, d_newest,
    size, count, identity,
):
    own = flows.shape[1]
    length = own * size
    rows = D // count
    lane_rows = max(rows, HD)
    head_width = d_pre.shape[2]
    width_out = joined.shape[1]
    width_in = 3 * head_width + d_up.shape[1]
    pieces = count.bit_length() - 2
    held = 2**pieces
    low = lambda *shape: jax.ShapeDtypeStruct(shape, bfloat)
    wide = lambda *shape: jax.ShapeDtypeStruct(shape, single)
    hbm = pl.BlockSpec(memory_space=pl.ANY)
    vmem = pl.BlockSpec(memory_space=pltpu.VMEM)
    landed = pieces * (held - 1) * (rows // pieces)
    return pl.pallas_call(
        lambda *refs: scatter_kernel(size, count, *refs),
        out_shape=[
            low(rows, width_in),
            low(rows, width_out),
            low(STREAMS, own, D),
            wide(8, D),
            wide(8, HD),
        ],
        in_specs=[hbm] * 7 + [vmem] * 3,
        out_specs=[hbm] * 2 + [vmem] * 3,
        scratch_shapes=[
            pltpu.VMEM(back.shape, bfloat),
            pltpu.VMEM(joined.shape, bfloat),
            pltpu.VMEM(d_up.shape, bfloat),
            pltpu.VMEM(d_pre.shape, bfloat),
            pltpu.VMEM((2, STREAMS, length, lane_rows), bfloat),
            pltpu.VMEM((held * rows, width_in), bfloat),
            pltpu.VMEM((held * rows, width_out), bfloat),
            pltpu.VMEM((rows, width_in), bfloat),
            pltpu.VMEM((rows, width_out), bfloat),
            pltpu.VMEM((rows, width_in), bfloat),
            pltpu.VMEM((rows, width_out), bfloat),
            pltpu.VMEM((landed, width_in), bfloat),
            pltpu.VMEM((landed, width_out), bfloat),
            pltpu.VMEM((3, length, D), bfloat),
            pltpu.VMEM((3, size + 1, own, D), bfloat),
            pltpu.VMEM((2, own, D), bfloat),
            pltpu.VMEM((own, D), single),
            pltpu.VMEM((4, 8, D), single),
            pltpu.VMEM((lane_rows if lane_rows > rows else 8, 512), single),
            pltpu.SemaphoreType.DMA((7,)),
            pltpu.SemaphoreType.DMA((2,)),
            pltpu.SemaphoreType.DMA((2,)),
            pltpu.SemaphoreType.DMA((2,)),
            pltpu.SemaphoreType.DMA((2,)),
            pltpu.SemaphoreType.REGULAR((2,)),
            pltpu.SemaphoreType.DMA((2, pieces, held)),
            pltpu.SemaphoreType.DMA((2, pieces, held)),
            pltpu.SemaphoreType.DMA((3, 2, size, 1)),
            pltpu.SemaphoreType.DMA((3, 2, size, 1)),
            pltpu.SemaphoreType.DMA((2,)),
        ],
        compiler_params=pltpu.CompilerParams(
            collective_id=identity, has_side_effects=True, vmem_limit_bytes=63 * 2**20
        ),
        name="scatter_%d" % identity,
    )(all_normed, d_normed, back, joined, d_up, d_pre, flows, small, d_residual, d_newest)


def small_sum_kernel(
    bits,
    norm_grads,
    row_grads,
    bias_grads,
    mix_in_grad,
    mix_out_grad,
    squares,
    out,
    value,
    total,
    landing,
    send_a,
    recv_a,
    send_b,
    recv_b,
):
    here = lax.axis_index("tensor")
    value[...] = jnp.zeros_like(value)
    width = HEADS // lax.axis_size("tensor") * HD
    value[0:4] = norm_grads[0:4]
    value[4:5] = row_grads[0:1]
    lanes = pl.ds(pl.multiple_of(here * width, HD), width)
    value[5:8, lanes] = bias_grads[0:3, 0:width]
    value[8:9] = row_grads[1:2]
    value[9:10] = row_grads[1:2]
    value[pl.ds(10 + here, 1), :] = bias_grads[3:4]
    value[SMALL_MIX : SMALL_MIX + MIXH] = mix_in_grad[0:MIXH]
    for place in range(5):
        value[56:64, place * HD : (place + 1) * HD] = mix_out_grad[place * 8 : place * 8 + 8]
    value[56:64, 5 * HD : 6 * HD] = squares[...]
    cube_sum_steps(bits, value, out, total, landing, send_a, recv_a, send_b, recv_b)


def small_sum(parts, bits, identity):
    steps = len(bits)
    vmem = pl.BlockSpec(memory_space=pltpu.VMEM)
    return pl.pallas_call(
        lambda *refs: small_sum_kernel(bits, *refs),
        out_shape=jax.ShapeDtypeStruct((64, D), single),
        in_specs=[vmem] * 6,
        out_specs=vmem,
        scratch_shapes=[pltpu.VMEM((64, D), single)] * 2
        + [pltpu.VMEM((steps, 32, D), single)]
        + [pltpu.SemaphoreType.DMA((steps,))] * 4,
        compiler_params=pltpu.CompilerParams(
            collective_id=identity, has_side_effects=True, vmem_limit_bytes=8 * 2**20
        ),
        name="small_sum_%d" % identity,
    )(*parts)


def finish_kernel(grad_in, grad_out, sums, weights, newest, stored, cotangent, d_flows, *refs):
    states, refs = (refs[0:4], refs[4:8]), refs[8:]
    small, mix, refs = refs[0:4], refs[4:8], refs[8:]
    norm_out, refs = refs[0], refs[1:]
    new_states, refs = (refs[0:5], refs[5:10]), refs[10:]
    new_small, new_mix, refs = refs[0:4], refs[4:8], refs[8:]
    out_streams, grad_streams, grad_stored, refs = refs[0], refs[1], refs[2], refs[3:]
    held, refs = (refs[0:2], refs[2:4], refs[4:6]), refs[6:]
    tiles_in, tiles_out, spread, passed, grad_sem, load_sem, save_sem, tile_load, tile_save, pass_sem = refs
    grads = (grad_in, grad_out)
    parts = load_sem.shape[2]
    rows = grad_in.shape[0]
    step_rows = rows // parts

    def load_grad(which):
        return pltpu.make_async_copy(grads[which], held[0][which], grad_sem.at[which])

    def load(which, kind, place):
        spot = pl.ds(place * step_rows, step_rows)
        return pltpu.make_async_copy(
            states[which][kind].at[spot],
            held[1][which].at[kind, spot],
            load_sem.at[which, kind, place],
        )

    def save(which, kind, place):
        spot = pl.ds(place * step_rows, step_rows)
        source = held[1][which].at[kind, spot] if kind < 4 else held[2][which].at[spot]
        return pltpu.make_async_copy(
            source, new_states[which][kind].at[spot], save_sem.at[which, kind, place]
        )

    own = newest.shape[0]
    tile_rows = tiles_in.shape[2]
    tile_count = own // tile_rows
    mixes = STREAMS + LAYER

    def tile_copies(index, into):
        spot = pl.ds(index * tile_rows, tile_rows)
        first, second = (cotangent, stored) if into else (out_streams, grad_stored)
        held_tile = (tiles_in if into else tiles_out).at[index % 2]
        sem = (tile_load if into else tile_save).at[index % 2]
        pairs = [
            (first.at[:, spot], held_tile.at[0:STREAMS]),
            (second.at[:, spot], held_tile.at[STREAMS:mixes]),
        ]
        return [
            pltpu.make_async_copy(*(pair if into else pair[::-1]), sem.at[place])
            for place, pair in enumerate(pairs)
        ]

    def compose(index):
        for copy in tile_copies(index, True):
            copy.wait()
        if index > 1:
            for copy in tile_copies(index - 2, False):
                copy.wait()
        spot = pl.ds(index * tile_rows, tile_rows)
        mix_tile = weights[spot]
        slot = index % 2
        for column in range(MIXH):
            spread[column] = jnp.broadcast_to(mix_tile[:, column : column + 1], (tile_rows, HD))

        def columns(place, carry):
            lanes = pl.ds(pl.multiple_of(place * HD, HD), HD)
            value = newest[spot, lanes]
            flows = [tiles_in[slot, stream, :, lanes].astype(single) for stream in range(STREAMS)]
            results = [spread[stream * LAYERS + LAYER] * value for stream in range(STREAMS)]
            for layer in range(LAYER):
                earlier = tiles_in[slot, STREAMS + layer, :, lanes].astype(single)
                gradient = None
                for stream in range(STREAMS):
                    weight = spread[stream * LAYERS + layer]
                    results[stream] = results[stream] + weight * earlier
                    term = weight * flows[stream]
                    gradient = term if gradient is None else gradient + term
                tiles_out[slot, STREAMS + layer, :, lanes] = gradient.astype(bfloat)
            for stream in range(STREAMS):
                tiles_out[slot, stream, :, lanes] = results[stream].astype(bfloat)
            return carry

        lax.fori_loop(0, D // HD, columns, 0)
        for copy in tile_copies(index, False):
            copy.start()
        if index + 2 < tile_count:
            for copy in tile_copies(index + 2, True):
                copy.start()

    for index in range(2):
        for copy in tile_copies(index, True):
            copy.start()
    for which in range(2):
        load_grad(which).start()
        for place in range(parts):
            for kind in range(4):
                load(which, kind, place).start()
    take_flows = pltpu.make_async_copy(d_flows, passed, pass_sem.at[0])
    give_flows = pltpu.make_async_copy(passed, grad_streams, pass_sem.at[1])
    take_flows.start()
    small_total = sums[0 : small[0].shape[0]]
    mix_total = jnp.concatenate(
        [sums[56:64, place * HD : (place + 1) * HD] for place in range(5)], axis=0
    )[0 : mix[0].shape[0], 0 : mix[0].shape[1]]

    def whole_sum(values):
        return jnp.sum(jnp.sum(values, axis=1, keepdims=True), axis=0, keepdims=True)

    norm = jnp.sqrt(
        whole_sum(sums[56:64, 5 * HD : 6 * HD])
        + whole_sum(small_total * small_total)
        + whole_sum(mix_total * mix_total)
    )
    norm_out[...] = norm
    factor = clip_norm / jnp.maximum(norm, clip_norm)
    for target, result in zip(
        new_small, adamw_step(*(ref[...] for ref in small), small_total, factor, small_rate)
    ):
        target[...] = result
    for target, result in zip(
        new_mix, adamw_step(*(ref[...] for ref in mix), mix_total, factor, small_rate)
    ):
        target[...] = result
    take_flows.wait()
    give_flows.start()
    tiles_done = 0
    for which in range(2):
        columns = held[1][which].shape[2]
        load_grad(which).wait()
        for place in range(parts):
            for kind in range(4):
                load(which, kind, place).wait()

            def update(index, carry):
                spot = pl.ds(pl.multiple_of(place * step_rows + index * 16, 16), 16)

                def column(at, inner):
                    lanes = pl.ds(pl.multiple_of(at * 512, 512), 512)
                    results = adamw_step(
                        *(held[1][which][kind, spot, lanes] for kind in range(4)),
                        held[0][which][spot, lanes].astype(single),
                        factor,
                        learn_rate,
                    )
                    for kind in range(4):
                        held[1][which][kind, spot, lanes] = results[kind]
                    held[2][which][spot, lanes] = results[0].astype(bfloat)
                    return inner

                return lax.fori_loop(0, columns // 512, column, carry)

            lax.fori_loop(0, step_rows // 16, update, 0)
            for kind in range(5):
                save(which, kind, place).start()
            if tiles_done < tile_count:
                compose(tiles_done)
                tiles_done += 1
    while tiles_done < tile_count:
        compose(tiles_done)
        tiles_done += 1
    for index in range(tile_count - 2, tile_count):
        for copy in tile_copies(index, False):
            copy.wait()
    give_flows.wait()
    for which in range(2):
        for place in range(parts):
            for kind in range(5):
                save(which, kind, place).wait()


def finish(
    grads, sums, weights, newest, stored, cotangent, d_flows, in_states, out_states, small, mix
):
    wide = lambda shape: jax.ShapeDtypeStruct(shape, single)
    low = lambda shape: jax.ShapeDtypeStruct(shape, bfloat)
    hbm = pl.BlockSpec(memory_space=pl.ANY)
    vmem = pl.BlockSpec(memory_space=pltpu.VMEM)
    shapes = [in_states[0].shape, out_states[0].shape]
    parts = 4
    tile = (2, STREAMS + LAYER, 16, D)
    return pl.pallas_call(
        finish_kernel,
        out_shape=[wide((1, 1))]
        + [entry for shape in shapes for entry in [wide(shape)] * 4 + [low(shape)]]
        + [wide(small[0].shape)] * 4
        + [wide(mix[0].shape)] * 4
        + [low(cotangent.shape), low(d_flows.shape), low(stored.shape)],
        in_specs=[hbm] * 2 + [vmem] * 3 + [hbm] * 3 + [hbm] * 8 + [vmem] * 8,
        out_specs=[vmem] + [hbm] * 10 + [vmem] * 8 + [hbm] * 3,
        scratch_shapes=[pltpu.VMEM(shape, grads[0].dtype) for shape in shapes]
        + [pltpu.VMEM((4,) + shape, single) for shape in shapes]
        + [pltpu.VMEM(shape, bfloat) for shape in shapes]
        + [pltpu.VMEM(tile, bfloat)] * 2
        + [pltpu.VMEM((MIXH, tile[2], HD), single), pltpu.VMEM(d_flows.shape, bfloat)]
        + [
            pltpu.SemaphoreType.DMA((2,)),
            pltpu.SemaphoreType.DMA((2, 4, parts)),
            pltpu.SemaphoreType.DMA((2, 5, parts)),
            pltpu.SemaphoreType.DMA((2, 2)),
            pltpu.SemaphoreType.DMA((2, 2)),
            pltpu.SemaphoreType.DMA((2,)),
        ],
        compiler_params=pltpu.CompilerParams(vmem_limit_bytes=60 * 2**20),
        name="finish",
    )(
        *grads, sums, weights, newest, stored, cotangent, d_flows,
        *in_states, *out_states, *small, *mix,
    )


def shards(
    in_streams,
    stored,
    cotangent,
    in_weights,
    in_moment,
    in_second,
    in_average,
    out_weights,
    out_moment,
    output_second_moment,
    out_average,
    small_params,
    small_moment,
    small_second,
    small_average,
    mix_weights,
    mix_moment,
    mix_second,
    mix_average,
):
    groups, count = lax.axis_size("tensor"), lax.axis_size("dp")
    rope = jnp.asarray(rope_lanes(in_streams.shape[1] * groups))
    (
        full_in,
        full_out,
        normed,
        joined,
        slope,
        heads,
        chances,
        newest,
        d_newest,
        d_branch,
        weights,
        row_grads,
        mix_in_grad,
        mix_out_grad,
    ) = forward(
        in_streams,
        in_weights,
        out_weights,
        small_params,
        rope,
        stored,
        cotangent,
        mix_weights,
        groups,
        count,
        0,
    )
    branch_grads, d_up, d_pre, d_normed, d_residual, bias_grads = backward(
        d_branch, rope, full_in, full_out, slope, heads, chances, groups, 1
    )
    grad_in, grad_out, d_flows, norm_grads, squares = scatter(
        normed,
        d_normed,
        branch_grads,
        joined,
        d_up,
        d_pre,
        in_streams,
        small_params,
        d_residual,
        d_newest,
        groups,
        count,
        2,
    )
    sums = small_sum(
        (norm_grads, row_grads, bias_grads, mix_in_grad, mix_out_grad, squares),
        axis_bits("dp") + axis_bits("tensor"),
        3,
    )
    results = finish(
        (grad_in, grad_out),
        sums,
        weights,
        newest,
        stored,
        cotangent,
        d_flows,
        (in_weights, in_moment, in_second, in_average),
        (out_weights, out_moment, output_second_moment, out_average),
        (small_params, small_moment, small_second, small_average),
        (mix_weights, mix_moment, mix_second, mix_average),
    )
    out_streams, grad_streams, grad_stored = results[-3:]
    return (out_streams, grad_streams, grad_stored, results[0][0, 0], *results[1:-3])


def solution(mesh):
    in_specs = (
        P(None, ("dp", "tensor"), None),
        P(None, ("dp", "tensor"), None),
        P(None, ("dp", "tensor"), None),
        P("dp", "tensor"),
        P("dp", "tensor"),
        P("dp", "tensor"),
        P("dp", "tensor"),
        P("dp", "tensor"),
        P("dp", "tensor"),
        P("dp", "tensor"),
        P("dp", "tensor"),
        P(),
        P(),
        P(),
        P(),
        P(),
        P(),
        P(),
        P(),
    )
    out_specs = (
        P(None, ("dp", "tensor"), None),
        P(None, ("dp", "tensor"), None),
        P(None, ("dp", "tensor"), None),
        P(),
        P("dp", "tensor"),
        P("dp", "tensor"),
        P("dp", "tensor"),
        P("dp", "tensor"),
        P("dp", "tensor"),
        P("dp", "tensor"),
        P("dp", "tensor"),
        P("dp", "tensor"),
        P("dp", "tensor"),
        P("dp", "tensor"),
        P(),
        P(),
        P(),
        P(),
        P(),
        P(),
        P(),
        P(),
    )
    return jax.shard_map(shards, mesh=mesh, in_specs=in_specs, out_specs=out_specs, check_vma=False)
```

```python
import jax
import jax.numpy as jnp
import numpy as np
from jax import lax
from jax.experimental import pallas as pl
from jax.experimental.pallas import tpu as pltpu
from jax.sharding import PartitionSpec as P

D = 2048
HEADS = 16
HD = 128
ROT = 32
FF = 8192
STREAMS = 4
LAYER = 8
STEP = 10
LAYERS = 9
MIXH = 36


norm_eps = 1e-05
mix_eps = 1e-06
beta_first = 0.9
beta_second = 0.95
adam_eps = 1e-08
decay_rate = 0.01
learn_rate = 0.03
small_rate = 0.2
clip_norm = 1.0
average_keep = 0.5
masked_score = -1e30
highest_precision = lax.Precision.HIGHEST
bfloat = jnp.bfloat16
single = jnp.float32
MESH = pl.DeviceIdType.MESH


def contract_last(left_side, right_side):
    return lax.dot_general(
        left_side,
        right_side,
        (((left_side.ndim - 1,), (right_side.ndim - 1,)), ((), ())),
        preferred_element_type=single,
    )


def contract_first(left_side, right_side):
    return lax.dot_general(
        left_side, right_side, (((0,), (0,)), ((), ())), preferred_element_type=single
    )


def adamw_step(weight, moment, second, average, gradient, factor, rate):
    clipped = gradient * factor
    moment = beta_first * moment + (1.0 - beta_first) * clipped
    second = beta_second * second + (1.0 - beta_second) * clipped * clipped
    step_ratio = (
        moment
        / (1.0 - beta_first**STEP)
        / (jnp.sqrt(second / (1.0 - beta_second**STEP)) + adam_eps)
    )
    weight = weight - rate * (step_ratio + decay_rate * weight)
    average = average_keep * average + (1.0 - average_keep) * weight
    return (weight, moment, second, average)


def enter(partners):
    barrier = pltpu.get_barrier_semaphore()
    for present, device in partners:

        @pl.when(present)
        def _():
            pl.semaphore_signal(barrier, inc=1, device_id=device, device_id_type=MESH)

    pl.semaphore_wait(barrier, sum(present.astype(jnp.int32) for present, _ in partners))


class LineSum:
    def __init__(self, size, give, landing, send_sem, recv_sem, cut):
        self.size, self.give, self.landing = size, give, landing
        self.send_sem, self.recv_sem, self.cut = send_sem, recv_sem, cut
        self.here = lax.axis_index("tensor")
        self.own = landing.shape[1]
        self.rows = self.own // cut
        self.near = lax.select(2 * self.here < size, 1, -1)

    def has_next(self, way):
        return jnp.logical_and(self.here + way >= 0, self.here + way < self.size)

    def spot(self, dest, place):
        return pl.ds(pl.multiple_of(dest * self.own + place * self.rows, 16), self.rows)

    def landed(self, way, dest, place):
        rows = pl.ds(pl.multiple_of(place * self.rows, 16), self.rows)
        return self.landing.at[dest + (1 + way) // 2, rows]

    def hop(self, way, dest, place):
        return pltpu.make_async_remote_copy(
            src_ref=self.give.at[self.spot(dest, place)],
            dst_ref=self.landed(way, dest, place),
            send_sem=self.send_sem.at[(1 - way) // 2, dest, place],
            recv_sem=self.recv_sem.at[(1 - way) // 2, dest, place],
            device_id={"tensor": self.here + way},
            device_id_type=MESH,
        )

    def arrive(self, way, dest, place):
        block = self.landed(way, dest, place)
        pltpu.make_async_remote_copy(
            src_ref=block,
            dst_ref=block,
            send_sem=self.send_sem.at[(1 - way) // 2, dest, place],
            recv_sem=self.recv_sem.at[(1 - way) // 2, dest, place],
            device_id={"tensor": self.here - way},
            device_id_type=MESH,
        ).wait_recv()

    def relay(self, way, dest):
        @pl.when((dest - self.here) * way > 0)
        def _():
            def one(place, carry):
                @pl.when(self.has_next(-way))
                def _():
                    self.arrive(way, dest, place)
                    spot = self.spot(dest, place)
                    self.give[spot] = (
                        self.give[spot].astype(single)
                        + self.landed(way, dest, place)[...].astype(single)
                    ).astype(bfloat)

                self.hop(way, dest, place).start()
                return carry

            lax.fori_loop(0, self.cut, one, 0)

    def far(self, rank, way):
        return (self.size - 1) * ((1 + way) // 2) - rank * way

    def collect(self, place, into):
        rows = pl.ds(place * self.rows, self.rows)
        into[rows] = self.give[self.spot(self.here, place)].astype(single)
        for way in (1, -1):

            @pl.when(self.has_next(-way))
            def _():
                self.arrive(way, self.here, place)
                into[rows] += self.landed(way, self.here, place)[...].astype(single)

    def drain(self):
        for rank in range(self.size - 1):
            for way in (1, -1):
                dest = self.far(rank, way)

                @pl.when((dest - self.here) * way > 0)
                def _():
                    for place in range(self.cut):
                        self.hop(way, dest, place).wait_send()


class FlatSum:
    def __init__(self, count, size, value, out, landing, crossing, sems):
        self.count, self.size, self.value, self.out = count, size, value, out
        self.landing, self.crossing = landing, crossing
        self.send_a, self.recv_a, self.send_b, self.recv_b, self.send_c, self.recv_c = sems
        self.me = lax.axis_index("dp")
        self.here = lax.axis_index("tensor")
        self.across = min(count, D // HD)
        self.rows, self.lanes = landing.shape[1:]

    def part(self, ref, owner):
        row = pl.multiple_of(owner // self.across * self.rows, 8)
        lane = pl.multiple_of(lax.rem(owner, self.across) * self.lanes, HD)
        return ref.at[pl.ds(row, self.rows), pl.ds(lane, self.lanes)]

    def over(self, first, action):
        total, place = (self.count, self.me) if first else (self.size, self.here)

        def one(step, carry):
            action(lax.rem(place + step, total))
            return carry

        lax.fori_loop(1, total, one, 0)

    def to_owner(self, other):
        return pltpu.make_async_remote_copy(
            src_ref=self.part(self.value, other),
            dst_ref=self.landing.at[self.me],
            send_sem=self.send_a.at[other],
            recv_sem=self.recv_a.at[self.me],
            device_id={"dp": other},
            device_id_type=MESH,
        )

    def across_to(self, other):
        return pltpu.make_async_remote_copy(
            src_ref=self.crossing.at[self.here],
            dst_ref=self.crossing.at[self.here],
            send_sem=self.send_b.at[other],
            recv_sem=self.recv_b.at[self.here],
            device_id={"tensor": other},
            device_id_type=MESH,
        )

    def back_to(self, other):
        return pltpu.make_async_remote_copy(
            src_ref=self.part(self.out, self.me),
            dst_ref=self.part(self.out, self.me),
            send_sem=self.send_c.at[other],
            recv_sem=self.recv_c.at[self.me],
            device_id={"dp": other},
            device_id_type=MESH,
        )

    def arrive(self, block, send, recv, other, axis):
        pltpu.make_async_remote_copy(
            src_ref=block,
            dst_ref=block,
            send_sem=send.at[other],
            recv_sem=recv.at[other],
            device_id={axis: other},
            device_id_type=MESH,
        ).wait_recv()

    def first(self):
        self.over(True, lambda other: self.to_owner(other).start())

    def second(self):
        self.crossing[self.here] = self.part(self.value, self.me)[...]

        def add(other):
            self.arrive(self.landing.at[other], self.send_a, self.recv_a, other, "dp")
            self.crossing[self.here] += self.landing[other]

        self.over(True, add)
        self.over(False, lambda other: self.across_to(other).start())

    def third(self):
        self.over(
            False,
            lambda other: self.arrive(
                self.crossing.at[other], self.send_b, self.recv_b, other, "tensor"
            ),
        )
        result = self.crossing[0]
        for other in range(1, self.size):
            result = result + self.crossing[other]
        self.part(self.out, self.me)[...] = result
        self.over(True, lambda other: self.back_to(other).start())

    def last(self):
        self.over(
            True,
            lambda other: self.arrive(
                self.part(self.out, other), self.send_c, self.recv_c, other, "dp"
            ),
        )
        self.over(True, lambda other: self.to_owner(other).wait_send())
        self.over(False, lambda other: self.across_to(other).wait_send())
        self.over(True, lambda other: self.back_to(other).wait_send())

    def partners(self):
        def others(place, total):
            return [lax.rem(place + step, total) for step in range(1, total)]

        return [{"dp": other} for other in others(self.me, self.count)] + [
            {"tensor": other} for other in others(self.here, self.size)
        ]


def flat_scratch(rows, count, size):
    across = min(count, D // HD)
    part = (rows * across // count, D // across)
    return [
        pltpu.VMEM((count,) + part, single),
        pltpu.VMEM((size,) + part, single),
    ] + [pltpu.SemaphoreType.DMA((n,)) for n in (count, count, size, size, count, count)]


def plus_flips(place, bits):
    moved = place
    for bit in bits:
        moved = moved + (1 - 2 * lax.rem(place // 2**bit, 2)) * 2**bit
    return moved


def cube_routes(count):
    bits = list(range(1, count))
    pieces = []
    for turn in range(len(bits)):
        order = bits[turn:] + bits[:turn]
        arrivals = [()]
        steps = []
        for bit in order:
            fresh = [tuple(sorted(held + (bit,))) for held in arrivals]
            steps.append([(bit, held, whole) for held, whole in zip(arrivals, fresh)])
            arrivals = arrivals + fresh
        pieces.append((arrivals, steps))
    return pieces


class CubeGather:
    def __init__(self, whole, rows, count, sems):
        self.whole, self.rows, self.count = whole, rows, count
        self.send_sem, self.recv_sem, self.pair_send, self.pair_recv = sems
        self.routes = cube_routes(count.bit_length() - 1)
        self.me = lax.axis_index("dp")
        self.piece_rows = rows // len(self.routes)

    def region(self, piece, held):
        first = plus_flips(self.me, held) * self.rows + piece * self.piece_rows
        return self.whole.at[pl.ds(pl.multiple_of(first, 16), self.piece_rows)]

    def hop(self, piece, bit, held, slot, pair=False):
        block = self.region(piece, held)
        return pltpu.make_async_remote_copy(
            src_ref=block,
            dst_ref=block,
            send_sem=(self.pair_send if pair else self.send_sem).at[piece, slot],
            recv_sem=(self.pair_recv if pair else self.recv_sem).at[piece, slot],
            device_id={"dp": plus_flips(self.me, (bit,))},
            device_id_type=MESH,
        )

    def slot(self, piece, held):
        return self.routes[piece][0].index(held)

    def sends_of(self, piece, held):
        found = []
        for step in self.routes[piece][1]:
            for bit, source, landed in step:
                if source == held:
                    found.append(self.hop(piece, bit, held, self.slot(piece, landed)))
        found.append(self.hop(piece, 0, held, self.slot(piece, held), True))
        return found

    def start(self):
        for copies in zip(*(self.sends_of(piece, ()) for piece in range(len(self.routes)))):
            for copy in copies:
                copy.start()

    def step(self, index):
        for piece, (_, steps) in enumerate(self.routes):
            for bit, _, landed in steps[index]:
                self.hop(piece, bit, landed, self.slot(piece, landed)).wait_recv()
                for copy in self.sends_of(piece, landed):
                    copy.start()

    def steps(self):
        return len(self.routes)

    def finish(self):
        for piece, (arrivals, _) in enumerate(self.routes):
            for held in arrivals:
                self.hop(piece, 0, (0,) + held, self.slot(piece, held), True).wait_recv()

    def drain(self):
        for piece, (arrivals, _) in enumerate(self.routes):
            for held in arrivals:
                for copy in self.sends_of(piece, held):
                    copy.wait_send()


FLOW_ORDER = (1, 2, 3, 0)
CUT = 4
SMALL_MIX = 10 + FF // D


def rope_lanes(length):
    half = ROT // 2
    inverse = 10000.0 ** (-2.0 * np.arange(half) / ROT)
    angles = np.arange(length)[:, None] * inverse[None, :]
    tables = np.zeros((3, length, HD), np.float32)
    tables[0] = 1.0
    tables[0, :, :half] = tables[0, :, half:ROT] = np.cos(angles)
    tables[1, :, :half] = -np.sin(angles)
    tables[2, :, half:ROT] = np.sin(angles)
    return tables


def forward_kernel(
    size,
    count,
    flows,
    w_in,
    w_out,
    small,
    rope,
    stored,
    cotangent,
    mix,
    all_in,
    all_out,
    all_normed,
    joined_out,
    slope_out,
    heads_out,
    chances_out,
    newest,
    d_newest,
    d_branch,
    weights,
    early_grads,
    w_in_low,
    w_out_low,
    normed,
    heads,
    chances,
    joined,
    slope,
    total,
    give,
    terms,
    back,
    earlier,
    dots,
    scales,
    sums,
    mix_low,
    mix_table,
    stage_sem,
    back_sem,
    earlier_sem,
    line_send,
    line_recv,
    term_send,
    term_recv,
    save_sem,
    flow_sem,
    *cube_sems,
):
    here = lax.axis_index("tensor")
    me = lax.axis_index("dp")
    own = flows.shape[1]
    rows_in = w_in.shape[0]
    length = own * size
    width_in, width_out = w_in.shape[1], w_out.shape[1]
    head_width = heads.shape[2]
    group_heads = head_width // HD
    attn_width = 3 * head_width
    units = width_in - attn_width
    bits = count.bit_length() - 1
    sides = ((0, 1), (1, -1))
    tile = 512

    def rows_of(block):
        return pl.ds(pl.multiple_of(block * own, own), own)

    def stage(source, width):
        spans = [(0, min(width, D))] + ([(D, width - D)] if width > D else [])
        return [
            pltpu.make_async_copy(
                source.at[:, pl.ds(first, span)],
                total.at[pl.ds(place * rows_in, rows_in), pl.ds(0, span)],
                stage_sem.at[place],
            )
            for place, (first, span) in enumerate(spans)
        ]

    def settle(source, width, target):
        for place, copy in enumerate(stage(source, width)):
            copy.wait()
            span = min(D, width - place * D)

            def cast(index, carry):
                low = pl.multiple_of(index * 16, 16)
                into = pl.multiple_of(me * rows_in + index * 16, 16)
                target[pl.ds(into, 16), pl.ds(place * D, span)] = total[
                    pl.ds(place * rows_in + low, 16), pl.ds(0, span)
                ].astype(bfloat)
                return carry

            lax.fori_loop(0, rows_in // 16, cast, 0)

    for copy in stage(w_in, width_in):
        copy.start()
    load_back = pltpu.make_async_copy(cotangent, back, back_sem)
    load_back.start()

    def load_earlier(layer):
        return pltpu.make_async_copy(
            stored.at[layer], earlier.at[layer % 2], earlier_sem.at[layer % 2]
        )

    load_earlier(0).start()
    enter(
        [(here < size - 1, {"tensor": here + 1}), (here > 0, {"tensor": here - 1})]
        + [(jnp.bool_(True), {"dp": plus_flips(me, (bit,))}) for bit in range(bits)]
    )

    def line_hop(side, way, step, flow):
        block = normed.at[flow, rows_of(here - way * step)]
        return pltpu.make_async_remote_copy(
            src_ref=block,
            dst_ref=block,
            send_sem=line_send.at[side, step, flow],
            recv_sem=line_recv.at[side, step, flow],
            device_id={"tensor": here + way},
            device_id_type=MESH,
        )

    def line_landed(side, way, step, flow):
        block = normed.at[flow, rows_of(here - way * step)]
        return pltpu.make_async_remote_copy(
            src_ref=block,
            dst_ref=block,
            send_sem=line_send.at[side, step - 1, flow],
            recv_sem=line_recv.at[side, step - 1, flow],
            device_id={"tensor": here - way},
            device_id_type=MESH,
        )

    def has_next(way):
        return here < size - 1 if way > 0 else here > 0

    def has_origin(way, step):
        return here >= step if way > 0 else here < size - step

    def keep_flow(flow, block):
        return pltpu.make_async_copy(
            normed.at[flow, rows_of(block)],
            all_normed.at[flow, rows_of(block)],
            flow_sem.at[flow, block],
        )

    def send_normal(flow):
        which = 2 if flow == 3 else 0

        def normalize(index, carry):
            spot = pl.ds(pl.multiple_of(index * 16, 16), 16)
            values = flows[flow, spot].astype(single)
            centred = values - jnp.mean(values, axis=-1, keepdims=True)
            inverse = lax.rsqrt(jnp.mean(centred * centred, axis=-1, keepdims=True) + norm_eps)
            into = pl.ds(pl.multiple_of(here * own + index * 16, 16), 16)
            normed[flow, into] = (
                centred * inverse * small[which : which + 1, :] + small[which + 1 : which + 2, :]
            ).astype(bfloat)
            return carry

        lax.fori_loop(0, own // 16, normalize, 0)
        if flow:
            for side, way in sides:
                pl.when(has_next(way))(line_hop(side, way, 0, flow).start)
        keep_flow(flow, here).start()

    cube_in = CubeGather(w_in_low, rows_in, count, cube_sems[:4])
    cube_out = CubeGather(w_out_low, rows_in, count, cube_sems[4:])
    send_normal(FLOW_ORDER[0])
    settle(w_in, width_in, w_in_low)
    cube_in.start()
    for copy in stage(w_out, width_out):
        copy.start()
    for flow in FLOW_ORDER[1:]:
        send_normal(flow)
    settle(w_out, width_out, w_out_low)
    mix_low[...] = jnp.zeros_like(mix_low)
    mix_low[0:MIXH] = small[SMALL_MIX : SMALL_MIX + MIXH].astype(bfloat)
    mix_table[...] = jnp.zeros_like(mix_table)
    mix_table[0:MIXH, 0:MIXH] = mix[0:MIXH]
    mix_table[HD : HD + 1, 0:MIXH] = mix[MIXH : MIXH + 1]
    lane = lax.broadcasted_iota(jnp.int32, (16, HD), 1)
    load_back.wait()
    for layer in range(LAYER):
        if layer + 1 < LAYER:
            load_earlier(layer + 1).start()
        load_earlier(layer).wait()

        def correlate(index, carry):
            spot = pl.ds(pl.multiple_of(index * 16, 16), 16)
            held = earlier[layer % 2, spot].astype(single)
            found = jnp.zeros((16, HD), single) if layer == 0 else dots[spot]
            for stream in range(STREAMS):
                value = jnp.sum(back[stream, spot].astype(single) * held, axis=-1, keepdims=True)
                found = found + jnp.where(lane == stream * LAYERS + layer, value, 0.0)
            dots[spot] = found
            return carry

        lax.fori_loop(0, own // 16, correlate, 0)

    def line_step(step, flow_list):
        for flow in flow_list:
            for side, way in sides:

                @pl.when(has_origin(way, step))
                def _():
                    line_landed(side, way, step, flow).wait_recv()
                    pl.when(has_next(way))(line_hop(side, way, step, flow).start)
                    keep_flow(flow, here - way * step).start()

    def at_distance(step, action):
        if step == 0:
            action(here)
            return

        def one(side, carry):
            block = here - step + 2 * step * side

            @pl.when(jnp.logical_and(block >= 0, block < size))
            def _():
                action(block)

            return carry

        lax.fori_loop(0, 2, one, 0)

    def project(block, part):
        rows = rows_of(block)
        source = normed[part, rows]
        pre = jnp.dot(
            source,
            jnp.concatenate(
                [
                    w_in_low[:, pl.ds((head * 3 + part) * HD, HD)]
                    for head in range(group_heads)
                ],
                axis=1,
            ),
            preferred_element_type=single,
        )
        first = pl.multiple_of(here * head_width, HD)
        pre = pre + small[5 + part : 6 + part, pl.ds(first, head_width)]
        if part == 2:
            heads[part, rows] = pre.astype(bfloat)
            return
        cosine, sine_low, sine_high = rope[0, rows], rope[1, rows], rope[2, rows]
        for head in range(group_heads):
            values = pre[:, head * HD : (head + 1) * HD]
            turned = (
                values * cosine
                + pltpu.roll(values, HD - ROT // 2, 1) * sine_low
                + pltpu.roll(values, ROT // 2, 1) * sine_high
            )
            heads[part, rows, pl.ds(head * HD, HD)] = turned.astype(bfloat)

    def expand(block):
        rows = rows_of(block)

        def one(index, carry):
            first = pl.multiple_of(index * tile, tile)
            pre = jnp.dot(
                normed[3, rows],
                w_in_low[:, pl.ds(attn_width + first, tile)],
                preferred_element_type=single,
            )
            pre = pre + small[pl.ds(10 + here, 1), pl.ds(first, tile)]
            normal = 0.5 * (1.0 + lax.erf(pre * 0.7071067811865476))
            joined[rows, pl.ds(head_width + first, tile)] = (pre * normal).astype(bfloat)
            slope[rows, pl.ds(first, tile)] = (
                normal + pre * jnp.exp(-0.5 * pre * pre) * 0.3989422804014327
            ).astype(bfloat)
            return carry

        lax.fori_loop(0, units // tile, one, 0)

    def contract():
        def one(index, carry):
            first = pl.multiple_of(index * tile, tile)
            total[:, pl.ds(first, tile)] = contract_last(
                joined[:, pl.ds(head_width, units)],
                w_out_low[pl.ds(first, tile), pl.ds(head_width, units)],
            )
            return carry

        lax.fori_loop(0, D // tile, one, 0)

    def attend(block):
        rows = rows_of(block)
        places = block * own + lax.broadcasted_iota(jnp.int32, (own, length), 0)
        allowed = lax.broadcasted_iota(jnp.int32, (own, length), 1) <= places
        for head in range(group_heads):
            lanes = pl.ds(head * HD, HD)
            scores = contract_last(heads[0, rows, lanes], heads[1, :, lanes]) * HD ** (-0.5)
            scores = jnp.where(allowed, scores, masked_score)
            raised = jnp.exp(scores - jnp.max(scores, axis=-1, keepdims=True))
            low = (raised / jnp.sum(raised, axis=-1, keepdims=True)).astype(bfloat)
            chances[head, rows] = low
            joined[rows, lanes] = jnp.dot(
                low, heads[2, :, lanes], preferred_element_type=single
            ).astype(bfloat)

    def emit(block):
        rows = rows_of(block)

        def one(index, carry):
            first = pl.multiple_of(index * tile, tile)
            spot = (rows, pl.ds(first, tile))
            give[spot] = (
                total[spot]
                + contract_last(
                    joined[rows, pl.ds(0, head_width)],
                    w_out_low[pl.ds(first, tile), pl.ds(0, head_width)],
                )
            ).astype(bfloat)
            return carry

        lax.fori_loop(0, D // tile, one, 0)

    def save(place, source, target):
        return pltpu.make_async_copy(source, target, save_sem.at[place])

    chain = LineSum(size, give, terms, term_send, term_recv, CUT)
    ending = jnp.logical_or(here == 0, here == size - 1)

    def query_pass(side, way, step):
        @pl.when(has_origin(way, step))
        def _():
            line_landed(side, way, step, 0).wait_recv()
            pl.when(has_next(way))(line_hop(side, way, step, 0).start)
            keep_flow(0, here - way * step).start()

    def query_side(side, way):
        for step in range(size - 1, 0, -1):
            query_pass(side, way, step)
        pl.when(has_next(way))(line_hop(side, way, 0, 0).start)

    cube_in.step(0)
    cube_out.start()
    line_step(1, FLOW_ORDER[:3])
    lower = 2 * here < size
    pl.when(lower)(lambda: query_side(0, 1))
    pl.when(jnp.logical_not(lower))(lambda: query_side(1, -1))
    for index in range(1, cube_in.steps()):
        cube_in.step(index)
    cube_in.finish()
    save(0, w_in_low, all_in).start()

    def early(block):
        project(block, 1)
        project(block, 2)
        expand(block)

    at_distance(0, early)
    line_step(2, FLOW_ORDER[:3])
    at_distance(1, early)
    cube_out.step(0)
    at_distance(2, early)
    project(here, 0)

    @pl.when(jnp.logical_not(ending))
    def _():
        pl.when(lower)(lambda: query_side(1, -1))
        pl.when(jnp.logical_not(lower))(lambda: query_side(0, 1))

        def one(index, carry):
            project(lax.rem(here + 1 + index, size), 0)
            return carry

        lax.fori_loop(0, size - 1, one, 0)

        def two(block, carry):
            attend(block)
            return carry

        lax.fori_loop(0, size, two, 0)

    for step in range(3, size):
        line_step(step, FLOW_ORDER[:3])
        at_distance(step, early)
    pl.when(ending)(lambda: attend(here))
    for index in range(1, cube_out.steps()):
        cube_out.step(index)
    cube_out.finish()
    save(1, w_out_low, all_out).start()
    contract()

    @pl.when(jnp.logical_not(ending))
    def _():
        def one(index, carry):
            emit(lax.rem(here + 1 + index, size))
            return carry

        lax.fori_loop(0, size - 1, one, 0)

    for rank in range(size - 1):
        step = size - 1 - rank

        @pl.when(ending)
        def _():
            dest = lax.select(here == 0, size - 1 - rank, rank)
            side = lax.select(here == 0, 1, 0)
            block = normed.at[0, rows_of(dest)]
            pltpu.make_async_remote_copy(
                src_ref=block,
                dst_ref=block,
                send_sem=line_send.at[side, step - 1, 0],
                recv_sem=line_recv.at[side, step - 1, 0],
                device_id={"tensor": lax.select(here == 0, 1, size - 2)},
                device_id_type=MESH,
            ).wait_recv()
            keep_flow(0, dest).start()
            project(dest, 0)
            attend(dest)
            emit(dest)

        for way in (chain.near, -chain.near):
            chain.relay(way, chain.far(rank, way))

    emit(here)
    saves = [
        save(2, joined, joined_out),
        save(3, slope, slope_out),
        save(4, heads, heads_out),
        save(5, chances, chances_out),
    ]
    for copy in saves:
        copy.start()
    for place in range(CUT):
        chain.collect(place, newest)

    def sixteen(index):
        spot = pl.ds(pl.multiple_of(index * 16, 16), 16)
        return spot, pl.ds(pl.multiple_of(here * own + index * 16, 16), 16)

    def compose(index, carry):
        spot, inner = sixteen(index)
        value = flows[3, spot].astype(single) + newest[spot] + small[8:9, :] + small[9:10, :]
        newest[spot] = value
        inverse = lax.rsqrt(jnp.mean(value * value, axis=-1, keepdims=True) + mix_eps)
        scales[spot] = jnp.broadcast_to(inverse, (16, HD))
        give[inner] = (value * inverse * small[4:5, :]).astype(bfloat)
        found = dots[spot]
        for stream in range(STREAMS):
            dot = jnp.sum(back[stream, spot].astype(single) * value, axis=-1, keepdims=True)
            found = found + jnp.where(lane == stream * LAYERS + LAYER, dot, 0.0)
        dots[spot] = found
        return carry

    lax.fori_loop(0, own // 16, compose, 0)
    mix_normed = give[rows_of(here)]
    mix_pre = contract_last(mix_normed, mix_low[...])
    normal = 0.5 * (1.0 + lax.erf(mix_pre * 0.7071067811865476))
    act = mix_pre * normal
    act_slope = normal + mix_pre * jnp.exp(-0.5 * mix_pre * mix_pre) * 0.3989422804014327
    table = mix_table[0:HD]
    weights[...] = (
        jnp.dot(act, table, precision=highest_precision, preferred_element_type=single)
        + mix_table[HD : HD + 1]
    )
    d_mixing = dots[...]
    d_act = lax.dot_general(
        d_mixing,
        table,
        (((1,), (1,)), ((), ())),
        precision=highest_precision,
        preferred_element_type=single,
    )
    d_mix_pre = (d_act * act_slope).astype(bfloat)
    out_grad = lax.dot_general(
        act,
        d_mixing,
        (((0,), (0,)), ((), ())),
        precision=highest_precision,
        preferred_element_type=single,
    )
    scales_sum = jnp.sum(d_mixing, axis=0, keepdims=True)
    early_grads[MIXH:] = jnp.zeros((early_grads.shape[0] - MIXH, D), single)
    for place in range((MIXH + 7) // 8):
        rows_left = min(8, MIXH - place * 8)
        early_grads[40 : 40 + rows_left, place * HD : (place + 1) * HD] = out_grad[
            place * 8 : place * 8 + rows_left
        ]
    early_grads[40 + MIXH % 8 : 41 + MIXH % 8, MIXH // 8 * HD : MIXH // 8 * HD + HD] = scales_sum

    def spread(index, carry):
        lanes = pl.ds(pl.multiple_of(index * tile, tile), tile)
        total[0:own, lanes] = jnp.dot(
            d_mix_pre, mix_low[:, lanes], preferred_element_type=single
        )
        early_grads[0:MIXH, lanes] = contract_first(d_mix_pre, give[rows_of(here), lanes])[0:MIXH]
        return carry

    lax.fori_loop(0, D // tile, spread, 0)
    sums[...] = jnp.zeros_like(sums)

    def descend(index, carry):
        spot, inner = sixteen(index)
        value, inverse = newest[spot], scales[spot][:, 0:1]
        d_normed = total[spot]
        scaled = d_normed * small[4:5, :]
        middle = jnp.mean(scaled * value, axis=-1, keepdims=True)
        result = inverse * scaled - value * (inverse * inverse * inverse * middle)
        for stream in range(STREAMS):
            column = stream * LAYERS + LAYER
            result = result + weights[spot][:, column : column + 1] * back[stream, spot].astype(
                single
            )
        d_newest[spot] = result
        d_branch[spot] = result.astype(bfloat)
        gain = d_normed * value * inverse
        sums[0] += gain[0:8] + gain[8:16]
        sums[1] += result[0:8] + result[8:16]
        return carry

    lax.fori_loop(0, own // 16, descend, 0)
    early_grads[MIXH : MIXH + 1] = jnp.sum(sums[0], axis=0, keepdims=True)
    early_grads[MIXH + 1 : MIXH + 2] = jnp.sum(sums[1], axis=0, keepdims=True)
    for step in range(size):
        for flow in FLOW_ORDER:
            for side, way in sides:

                @pl.when(jnp.logical_and(has_next(way), has_origin(way, step)))
                def _():
                    line_hop(side, way, step, flow).wait_send()

    cube_in.drain()
    cube_out.drain()
    chain.drain()
    for flow in FLOW_ORDER:
        for block in range(size):
            keep_flow(flow, block).wait()
    save(0, w_in_low, all_in).wait()
    save(1, w_out_low, all_out).wait()
    for copy in saves:
        copy.wait()


def forward(flows, w_in, w_out, small, rope, stored, cotangent, mix_weights, size, count, identity):
    own = flows.shape[1]
    length = own * size
    rows, width_in = w_in.shape
    width_out = w_out.shape[1]
    head_width = HEADS // size * HD
    units = FF // size
    pieces = count.bit_length() - 2
    cube = [pltpu.SemaphoreType.DMA((pieces, 2**pieces))] * 8
    low = lambda *shape: jax.ShapeDtypeStruct(shape, bfloat)
    hbm = pl.BlockSpec(memory_space=pl.ANY)
    vmem = pl.BlockSpec(memory_space=pltpu.VMEM)
    return pl.pallas_call(
        lambda *refs: forward_kernel(size, count, *refs),
        out_shape=[
            low(D, width_in),
            low(D, width_out),
            low(STREAMS, length, D),
            low(length, width_out),
            low(length, units),
            low(3, length, head_width),
            low(HEADS // size, length, length),
            jax.ShapeDtypeStruct((own, D), single),
            jax.ShapeDtypeStruct((own, D), single),
            low(own, D),
            jax.ShapeDtypeStruct((own, HD), single),
            jax.ShapeDtypeStruct((48, D), single),
        ],
        in_specs=[vmem, hbm, hbm, vmem, vmem, hbm, hbm, vmem],
        out_specs=[hbm] * 7 + [vmem] * 5,
        scratch_shapes=[
            pltpu.VMEM((D, width_in), bfloat),
            pltpu.VMEM((D, width_out), bfloat),
            pltpu.VMEM((STREAMS, length, D), bfloat),
            pltpu.VMEM((3, length, head_width), bfloat),
            pltpu.VMEM((HEADS // size, length, length), bfloat),
            pltpu.VMEM((length, width_out), bfloat),
            pltpu.VMEM((length, units), bfloat),
            pltpu.VMEM((length, D), single),
            pltpu.VMEM((length, D), bfloat),
            pltpu.VMEM((size + 1, own, D), bfloat),
            pltpu.VMEM((STREAMS, own, D), bfloat),
            pltpu.VMEM((2, own, D), bfloat),
            pltpu.VMEM((own, HD), single),
            pltpu.VMEM((own, HD), single),
            pltpu.VMEM((2, 8, D), single),
            pltpu.VMEM((HD, D), bfloat),
            pltpu.VMEM((HD + 8, HD), single),
            pltpu.SemaphoreType.DMA((2,)),
            pltpu.SemaphoreType.DMA,
            pltpu.SemaphoreType.DMA((2,)),
            pltpu.SemaphoreType.DMA((2, size, STREAMS)),
            pltpu.SemaphoreType.DMA((2, size, STREAMS)),
            pltpu.SemaphoreType.DMA((2, size, CUT)),
            pltpu.SemaphoreType.DMA((2, size, CUT)),
            pltpu.SemaphoreType.DMA((6,)),
            pltpu.SemaphoreType.DMA((STREAMS, size)),
        ]
        + cube,
        compiler_params=pltpu.CompilerParams(
            collective_id=identity, has_side_effects=True, vmem_limit_bytes=60 * 2**20
        ),
        name="forward_%d" % identity,
    )(flows, w_in, w_out, small, jnp.asarray(rope), stored, cotangent, mix_weights)


def backward_kernel(
    size,
    count,
    d_branch,
    early_grads,
    rope,
    all_in,
    all_out,
    slope_in,
    heads_in,
    chances_in,
    joined_in,
    all_normed,
    flows_in,
    small,
    grad_in,
    grad_out,
    d_flows,
    early_sums,
    late_sums,
    arena,
    give,
    wide,
    heads,
    chances,
    back,
    d_up,
    d_pre,
    parts,
    terms,
    flows,
    total,
    sums,
    work,
    late,
    squares,
    arena_sem,
    load_sem,
    tile_sem,
    flow_sem,
    keep_sem,
    save_sem,
    line_send,
    line_recv,
    term_send,
    term_recv,
    give_sem,
    pair_sem,
    credit,
    ready,
    cube_send,
    cube_recv,
    *flat_refs,
):
    here = lax.axis_index("tensor")
    me = lax.axis_index("dp")
    bits = count.bit_length() - 1
    routes = cube_routes(bits)
    pieces = len(routes)
    subsets = sorted(routes[0][0], key=lambda held: -len(held))
    last = len(subsets) - 1
    own = flows.shape[1]
    length = own * size
    tile = arena.shape[2]
    head_width = heads.shape[2]
    group_heads = head_width // HD
    units = d_up.shape[1]
    tiles_out = (head_width + units) // tile
    tiles_in = (3 * head_width + units) // tile
    first_up = tiles_out + 3 * head_width // tile
    groups = (
        (0, tiles_out),
        (tiles_out, first_up - tiles_out),
        (first_up, tiles_out + tiles_in - first_up),
    )
    give_first = (0, tiles_out, 0)
    rows = D // count
    piece_rows = rows // pieces
    lane_rows = max(rows, HD)
    kept_first, land_first, pair_first = 0, D // 2, D - rows
    sides = ((0, 1), (1, -1))
    scale = HD ** (-0.5)
    ending = jnp.logical_or(here == 0, here == size - 1)

    def rows_of(block):
        return pl.ds(pl.multiple_of(block * own, own), own)

    def load_arena(index):
        source, place = (all_out, index) if index < tiles_out else (all_in, index - tiles_out)
        return pltpu.make_async_copy(
            source.at[:, pl.ds(place * tile, tile)], arena.at[index], arena_sem.at[index]
        )

    load_branch = pltpu.make_async_copy(d_branch, back.at[rows_of(here)], load_sem.at[0])
    load_slope = pltpu.make_async_copy(slope_in, wide.at[:, pl.ds(0, units)], load_sem.at[1])
    load_heads = pltpu.make_async_copy(heads_in, heads, load_sem.at[2])
    load_chances = pltpu.make_async_copy(chances_in, chances, load_sem.at[3])
    load_joined = pltpu.make_async_copy(joined_in, wide, load_sem.at[4])

    def load_flow(flow):
        return pltpu.make_async_copy(
            flows_in.at[flow], flows.at[flow % 2], flow_sem.at[flow % 2]
        )

    def keep_flow(flow):
        return pltpu.make_async_copy(
            flows.at[flow % 2], d_flows.at[flow], keep_sem.at[flow % 2]
        )

    load_rope = pltpu.make_async_copy(
        rope, total.at[:, pl.ds(0, rope.shape[1])], load_sem.at[5]
    )
    load_branch.start()
    load_rope.start()
    for index in range(tiles_out):
        load_arena(index).start()
    load_slope.start()
    for index in range(first_up, tiles_out + tiles_in):
        load_arena(index).start()
    load_heads.start()
    load_chances.start()
    for index in range(tiles_out, first_up):
        load_arena(index).start()
    load_flow(3).start()
    load_flow(0).start()
    half = len(flat_refs) // 2
    early = FlatSum(count, size, early_grads, early_sums, *flat_refs[:2], flat_refs[2:half])
    final = FlatSum(
        count, size, late, late_sums, *flat_refs[half : half + 2], flat_refs[half + 2 :]
    )
    enter([(jnp.bool_(True), partner) for partner in early.partners()])

    def has_next(way):
        return here < size - 1 if way > 0 else here > 0

    def has_origin(way, step):
        return here >= step if way > 0 else here < size - step

    def line_hop(side, way, step):
        block = back.at[rows_of(here - way * step)]
        return pltpu.make_async_remote_copy(
            src_ref=block,
            dst_ref=block,
            send_sem=line_send.at[side, step],
            recv_sem=line_recv.at[side, step],
            device_id={"tensor": here + way},
            device_id_type=MESH,
        )

    def line_landed(side, way, step):
        block = back.at[rows_of(here - way * step)]
        return pltpu.make_async_remote_copy(
            src_ref=block,
            dst_ref=block,
            send_sem=line_send.at[side, step - 1],
            recv_sem=line_recv.at[side, step - 1],
            device_id={"tensor": here - way},
            device_id_type=MESH,
        )

    load_branch.wait()
    for side, way in sides:
        pl.when(has_next(way))(line_hop(side, way, 0).start)
    early.first()

    def pull(block):
        spot = rows_of(block)
        wide[spot, pl.ds(units, head_width)] = jnp.dot(
            back[spot], arena[0], preferred_element_type=single
        ).astype(bfloat)

        def one(index, carry):
            lanes = pl.ds(pl.multiple_of(index * tile, tile), tile)
            d_hidden = jnp.dot(
                back[spot], arena[head_width // tile + index], preferred_element_type=single
            )
            d_up[spot, lanes] = (d_hidden * wide[spot, lanes].astype(single)).astype(bfloat)
            return carry

        lax.fori_loop(0, units // tile, one, 0)

    def push(block):
        spot = rows_of(block)

        def one(index, carry):
            lanes = pl.ds(pl.multiple_of(index * tile, tile), tile)
            value = None
            for place in range(units // tile):
                term = contract_last(
                    d_up[spot, pl.ds(place * tile, tile)], arena[first_up + place, lanes]
                )
                value = term if value is None else value + term
            parts[3, spot, lanes] = value.astype(bfloat)
            return carry

        lax.fori_loop(0, D // tile, one, 0)

    chains = [
        LineSum(
            size,
            parts.at[flow],
            terms.at[flow],
            term_send.at[flow],
            term_recv.at[flow],
            CUT if flow == 3 else 1,
        )
        for flow in range(STREAMS)
    ]

    def relay(flow, rank):
        for sign in (1, -1):
            way = sign * chains[flow].near
            chains[flow].relay(way, chains[flow].far(rank, way))

    def middle(action):
        pl.when(jnp.logical_not(ending))(action)

    for index in range(tiles_out):
        load_arena(index).wait()
    load_slope.wait()
    pull(here)
    early.second()
    for step in range(1, size):
        for side, way in sides:

            @pl.when(has_origin(way, step))
            def _():
                line_landed(side, way, step).wait_recv()
                pl.when(has_next(way))(line_hop(side, way, step).start)

        if step == 1:
            for index in range(first_up, tiles_out + tiles_in):
                load_arena(index).wait()

        def both(side, carry):
            block = here - step + 2 * step * side

            @pl.when(jnp.logical_and(block >= 0, block < size))
            def _():
                pull(block)
                push(block)

            return carry

        lax.fori_loop(0, 2, both, 0)
        pl.when(ending)(lambda: relay(3, size - 1 - step))
        if step == min(2, size - 1):
            early.third()

    def tell(which):
        for bit in range(bits):
            pl.semaphore_signal(
                ready.at[which, bit],
                inc=1,
                device_id={"dp": plus_flips(me, (bit,))},
                device_id_type=MESH,
            )

    tell(0)
    load_heads.wait()
    load_chances.wait()
    half_rows = length // 2
    late[...] = jnp.zeros_like(late)

    load_rope.wait()

    def turn_back(gradients, first, blocks):
        def table(kind):
            return jnp.concatenate(
                [
                    total[:, (kind * size + block) * HD : (kind * size + block + 1) * HD]
                    for block in range(first, first + blocks)
                ],
                axis=0,
            )

        return (
            gradients * table(0)
            - pltpu.roll(gradients, HD - ROT // 2, 1) * table(1)
            - pltpu.roll(gradients, ROT // 2, 1) * table(2)
        )

    for head in range(group_heads):
        lanes = pl.ds(head * HD, HD)
        d_lanes = pl.ds(units + head * HD, HD)
        d_keys = jnp.zeros((length, HD), single)
        d_values = jnp.zeros((length, HD), single)
        query_bias = jnp.zeros((1, HD), single)
        for place in range(2):
            spot = pl.ds(place * half_rows, half_rows)
            low = chances[head, spot]
            chance = low.astype(single)
            d_chance = contract_last(wide[spot, d_lanes], heads[2, :, lanes])
            centre = jnp.sum(d_chance * chance, axis=-1, keepdims=True)
            d_score = (chance * (d_chance - centre)).astype(bfloat)
            d_query = jnp.dot(d_score, heads[1, :, lanes], preferred_element_type=single) * scale
            d_query = turn_back(d_query, place * size // 2, size // 2).astype(bfloat)
            d_pre[0, spot, lanes] = d_query
            query_bias = query_bias + jnp.sum(d_query.astype(single), axis=0, keepdims=True)
            d_keys = d_keys + contract_first(d_score, heads[0, spot, lanes])
            d_values = d_values + contract_first(low, wide[spot, d_lanes])
        d_key = turn_back(d_keys * scale, 0, size).astype(bfloat)
        d_value = d_values.astype(bfloat)
        d_pre[1, :, lanes] = d_key
        d_pre[2, :, lanes] = d_value
        bias_lanes = pl.ds(pl.multiple_of(here * head_width + head * HD, HD), HD)
        late[4:5, bias_lanes] = query_bias
        late[5:6, bias_lanes] = jnp.sum(d_key.astype(single), axis=0, keepdims=True)
        late[6:7, bias_lanes] = jnp.sum(d_value.astype(single), axis=0, keepdims=True)

    def first_lane(held):
        return pl.multiple_of(plus_flips(me, held) * rows // lane_rows * lane_rows, HD)

    def normal_lanes(slot):
        return pl.ds(slot * lane_rows, lane_rows)

    def load_tile(slot, held):
        return pltpu.make_async_copy(
            all_normed.at[:, :, pl.ds(first_lane(held), lane_rows)],
            chances.at[:, :, normal_lanes(slot)],
            tile_sem.at[slot],
        )

    load_joined.start()
    load_tile(0, (0,) + subsets[0]).start()
    load_tile(1, subsets[0]).start()
    for step in range(1, size - 1):
        middle(lambda: relay(3, size - 1 - step))

    def spread(flow):
        def one(index, carry):
            lanes = pl.ds(pl.multiple_of(index * tile, tile), tile)
            columns = []
            for head in range(group_heads):
                place, lane = divmod((head * 3 + flow) * HD, tile)
                columns.append(arena[tiles_out + place, lanes, pl.ds(lane, HD)])
            parts[flow, :, lanes] = contract_last(
                d_pre[flow], jnp.concatenate(columns, axis=1)
            ).astype(bfloat)
            return carry

        lax.fori_loop(0, D // tile, one, 0)

        @pl.when(ending)
        def _():
            for rank in range(size - 1):
                relay(flow, rank)

    for index in range(tiles_out, first_up):
        load_arena(index).wait()
    spread(0)

    def own_rows(value, held):
        if lane_rows == rows:
            return value
        work[...] = value
        first = lax.rem(plus_flips(me, held) * rows, lane_rows)
        return work[pl.ds(pl.multiple_of(first, 16), rows)]

    def products(which, held, slot, emit):
        if which == 0:
            source = back[:, pl.ds(first_lane(held), lane_rows)]

            def one(index, carry):
                lanes = pl.ds(pl.multiple_of(index * tile, tile), tile)
                emit(own_rows(contract_first(source, wide[:, lanes]), held), index, 0)
                return carry

            lax.fori_loop(0, tiles_out, one, 0)
            return
        if which == 1:
            for part in range(3):
                value = own_rows(
                    contract_first(chances[part, :, normal_lanes(slot)], d_pre[part]), held
                )
                for head in range(group_heads):
                    place, lane = divmod((head * 3 + part) * HD, tile)
                    emit(value[:, head * HD : (head + 1) * HD], place, lane)
            return

        def one(index, carry):
            lanes = pl.ds(pl.multiple_of(index * tile, tile), tile)
            value = contract_first(chances[3, :, normal_lanes(slot)], d_up[:, lanes])
            emit(own_rows(value, held), index, 0)
            return carry

        lax.fori_loop(0, units // tile, one, 0)

    def place_of(held):
        return sum(2 ** (bit - 1) for bit in held)

    def pass_pair(which):
        first, span = groups[which]
        return pltpu.make_async_remote_copy(
            src_ref=give.at[pl.ds(give_first[which], span)],
            dst_ref=arena.at[pl.ds(first, span), pl.ds(pair_first, rows)],
            send_sem=give_sem.at[which],
            recv_sem=pair_sem.at[which],
            device_id={"dp": plus_flips(me, (0,))},
            device_id_type=MESH,
        )

    def kept_row(piece, held):
        return kept_first + place_of(held) * rows + piece * piece_rows

    def land_row(piece, landed):
        return land_first + (piece * last + place_of(landed) - 1) * piece_rows

    def cube_hop(which, piece, bit, landed):
        tiles = pl.ds(*groups[which])
        return pltpu.make_async_remote_copy(
            src_ref=arena.at[tiles, pl.ds(kept_row(piece, landed), piece_rows)],
            dst_ref=arena.at[tiles, pl.ds(land_row(piece, landed), piece_rows)],
            send_sem=cube_send.at[which, piece, place_of(landed)],
            recv_sem=cube_recv.at[which, piece, place_of(landed)],
            device_id={"dp": plus_flips(me, (bit,))},
            device_id_type=MESH,
        )

    def needs(piece, held):
        return [
            (bit, landed)
            for step in routes[piece][1]
            for bit, source, landed in step
            if source == held
        ]

    def add_landed(which, piece, held):
        for bit, landed in needs(piece, held):
            cube_hop(which, piece, bit, landed).wait_recv()
        first, span = groups[which]

        def one(index, carry):
            def column(at, inner):
                spot = pl.ds(pl.multiple_of(kept_row(piece, held) + index * 16, 16), 16)
                value = arena[first + at, spot].astype(single)
                for _, landed in needs(piece, held):
                    arrived = pl.ds(pl.multiple_of(land_row(piece, landed) + index * 16, 16), 16)
                    value = value + arena[first + at, arrived].astype(single)
                arena[first + at, spot] = value.astype(bfloat)
                if not held:
                    value = value * value
                    value = value[0:8] + value[8:16]
                    for group in range(tile // HD):
                        inner = inner + value[:, group * HD : (group + 1) * HD]
                return inner

            return lax.fori_loop(0, span, column, carry)

        found = lax.fori_loop(0, piece_rows // 16, one, jnp.zeros((8, HD), single))
        if not held:
            squares[...] += found

    def offer(which, index):
        held = subsets[index]
        if index > 0:
            pass_pair(which).wait_send()
        else:
            for bit in range(bits):
                pl.semaphore_wait(ready.at[which, bit], 1)
        if which == 1:
            load_tile(0, (0,) + held).wait()

        def emit(value, place, lane):
            give[give_first[which] + place, :, pl.ds(lane, value.shape[1])] = value.astype(bfloat)

        products(which, (0,) + held, 0, emit)
        if index > 0:
            pl.semaphore_wait(credit.at[which], 1)
        pass_pair(which).start()
        if which == 2 and index < last:
            load_tile(0, (0,) + subsets[index + 1]).start()

    def keep(which, index):
        held = subsets[index]
        first, _ = groups[which]
        if which == 1:
            load_tile(1, held).wait()
        pass_pair(which).wait_recv()

        def emit(value, place, lane):
            lanes = pl.ds(lane, value.shape[1])
            arena[first + place, pl.ds(kept_first + place_of(held) * rows, rows), lanes] = (
                value + arena[first + place, pl.ds(pair_first, rows), lanes].astype(single)
            ).astype(bfloat)

        products(which, held, 1, emit)
        if index < last:
            pl.semaphore_signal(
                credit.at[which],
                inc=1,
                device_id={"dp": plus_flips(me, (0,))},
                device_id_type=MESH,
            )
        else:
            pass_pair(which).wait_send()
        for piece, (_, steps) in enumerate(routes):
            for bit, _, landed in steps[-1]:
                if landed == held:
                    cube_hop(which, piece, bit, landed).start()
        if which == 2 and index < last:
            load_tile(1, subsets[index + 1]).start()

    def pass_on(which):
        for step in range(pieces - 2, -1, -1):
            for piece, (_, steps) in enumerate(routes):
                for bit, _, landed in steps[step]:
                    add_landed(which, piece, landed)
                    cube_hop(which, piece, bit, landed).start()

    def descend(flow):
        for place in range(chains[flow].cut):
            chains[flow].collect(place, total)
        load_flow(flow).wait()
        gain = 2 if flow == 3 else 0
        slot = flow % 2

        def one(index, carry):
            spot = pl.ds(pl.multiple_of(index * 16, 16), 16)
            values = flows[slot, spot].astype(single)
            centred = values - jnp.mean(values, axis=-1, keepdims=True)
            inverse = lax.rsqrt(jnp.mean(centred * centred, axis=-1, keepdims=True) + norm_eps)
            unit = centred * inverse
            incoming = total[spot]
            scaled = incoming * small[gain : gain + 1, :]
            result = inverse * (
                scaled
                - jnp.mean(scaled, axis=-1, keepdims=True)
                - unit * jnp.mean(scaled * unit, axis=-1, keepdims=True)
            )
            flows[slot, spot] = result.astype(bfloat)
            unit = unit * incoming
            sums[gain] += unit[0:8] + unit[8:16]
            sums[gain + 1] += incoming[0:8] + incoming[8:16]
            return carry

        lax.fori_loop(0, own // 16, one, 0)
        keep_flow(flow).start()

    def near(flow, rank):
        way = chains[flow].near
        middle(lambda: chains[flow].relay(way, chains[flow].far(rank, way)))

    def beyond(flow, rank):
        way = -chains[flow].near
        middle(lambda: chains[flow].relay(way, chains[flow].far(rank, way)))

    def unit_sum(index, carry):
        lanes = pl.ds(pl.multiple_of(index * 256, 256), 256)
        late[pl.ds(8 + here, 1), lanes] = jnp.sum(
            d_up[:, lanes].astype(single), axis=0, keepdims=True
        )
        return carry

    def release():
        push(here)
        tell(2)
        middle(lambda: relay(3, 0))

    def closing():
        spread(2)
        tell(1)

    between = [lambda: spread(1), closing, release]
    load_joined.wait()
    for index in range(last + 1):
        offer(0, index)
        if between:
            between.pop(0)()
        if index == last:
            for action in between:
                action()
            offer(1, 0)
        keep(0, index)
        if index == 2:
            near(0, 0)
    offer(2, 0)
    lax.fori_loop(0, units // 256, unit_sum, 0)
    between = [lambda: near(0, 1), lambda: beyond(0, 0), lambda: pass_on(0)]
    for index in range(last + 1):
        keep(1, index)
        if index < last:
            offer(1, index + 1)
        keep(2, index)
        if index < last:
            offer(2, index + 1)
        if between:
            between.pop(0)()
    for action in between:
        action()
    sums[...] = jnp.zeros_like(sums)
    for rank in range(1, size - 1):
        if rank > 1:
            near(0, rank)
        beyond(0, rank)
    near(1, 0)
    descend(3)
    descend(0)
    keep_flow(3).wait()
    load_flow(1).start()
    near(1, 1)
    beyond(1, 0)
    pass_on(1)
    pass_on(2)
    for rank in range(1, size - 1):
        if rank > 1:
            near(1, rank)
        beyond(1, rank)
    keep_flow(0).wait()
    load_flow(2).start()
    descend(1)
    near(2, 0)
    near(2, 1)
    beyond(2, 0)
    for rank in range(1, size - 1):
        if rank > 1:
            near(2, rank)
        beyond(2, rank)
    descend(2)
    squares[...] = jnp.zeros_like(squares)
    saves = []
    for which in range(3):
        for piece in range(pieces):
            add_landed(which, piece, ())
        first, span = groups[which]
        target, offset = (grad_out, 0) if which == 0 else (grad_in, first - tiles_out)
        for place in range(span):
            saves.append(
                pltpu.make_async_copy(
                    arena.at[first + place, pl.ds(kept_first, rows)],
                    target.at[:, pl.ds((offset + place) * tile, tile)],
                    save_sem.at[first + place],
                )
            )
            saves[-1].start()
    for row in range(4):
        late[row : row + 1] = jnp.sum(sums[row], axis=0, keepdims=True)
    late[7:8, 0:HD] = jnp.sum(squares[...], axis=0, keepdims=True)
    final.first()
    final.second()
    final.third()
    final.last()
    early.last()
    for step in range(size):
        for side, way in sides:

            @pl.when(jnp.logical_and(has_next(way), has_origin(way, step)))
            def _():
                line_hop(side, way, step).wait_send()

    for which in range(3):
        for piece, (_, steps) in enumerate(routes):
            for step in steps:
                for bit, _, landed in step:
                    cube_hop(which, piece, bit, landed).wait_send()
    for chain in chains:
        chain.drain()
    keep_flow(1).wait()
    keep_flow(2).wait()
    for copy in saves:
        copy.wait()


def backward(
    d_branch, early_grads, rope, all_in, all_out, slope, heads, chances, joined, all_normed,
    flows, small, size, count, identity,
):
    own = d_branch.shape[0]
    length = own * size
    rows = D // count
    lane_rows = max(rows, HD)
    tile = 512
    head_width, units = heads.shape[2], slope.shape[1]
    width_in, width_out = all_in.shape[1], all_out.shape[1]
    tiles = (width_in + width_out) // tile
    pieces = count.bit_length() - 2
    held = 2**pieces
    bits = pieces + 1
    late_rows = 16
    low = lambda *shape: jax.ShapeDtypeStruct(shape, bfloat)
    wide = lambda *shape: jax.ShapeDtypeStruct(shape, single)
    hbm = pl.BlockSpec(memory_space=pl.ANY)
    vmem = pl.BlockSpec(memory_space=pltpu.VMEM)
    dma = pltpu.SemaphoreType.DMA
    rope = rope.reshape(3, size, own, HD).transpose(2, 0, 1, 3).reshape(own, -1)
    return pl.pallas_call(
        lambda *refs: backward_kernel(size, count, *refs),
        out_shape=[
            low(rows, width_in),
            low(rows, width_out),
            low(STREAMS, own, D),
            wide(*early_grads.shape),
            wide(late_rows, D),
        ],
        in_specs=[hbm, vmem] + [hbm] * 9 + [vmem],
        out_specs=[hbm] * 3 + [vmem] * 2,
        scratch_shapes=[
            pltpu.VMEM((tiles, D, tile), bfloat),
            pltpu.VMEM(((width_out + 3 * head_width) // tile, rows, tile), bfloat),
            pltpu.VMEM((length, width_out), bfloat),
            pltpu.VMEM(heads.shape, bfloat),
            pltpu.VMEM(chances.shape, bfloat),
            pltpu.VMEM((length, D), bfloat),
            pltpu.VMEM((length, units), bfloat),
            pltpu.VMEM((3, length, head_width), bfloat),
            pltpu.VMEM((STREAMS, length, D), bfloat),
            pltpu.VMEM((STREAMS, size + 1, own, D), bfloat),
            pltpu.VMEM((2, own, D), bfloat),
            pltpu.VMEM((own, D), single),
            pltpu.VMEM((4, 8, D), single),
            pltpu.VMEM((lane_rows, tile) if lane_rows > rows else (8, HD), single),
            pltpu.VMEM((late_rows, D), single),
            pltpu.VMEM((8, HD), single),
            dma((tiles,)),
            dma((6,)),
            dma((2,)),
            dma((2,)),
            dma((2,)),
            dma((tiles,)),
            dma((2, size)),
            dma((2, size)),
            dma((STREAMS, 2, size, CUT)),
            dma((STREAMS, 2, size, CUT)),
            dma((3,)),
            dma((3,)),
            pltpu.SemaphoreType.REGULAR((3,)),
            pltpu.SemaphoreType.REGULAR((3, bits)),
            dma((3, pieces, held)),
            dma((3, pieces, held)),
        ]
        + flat_scratch(early_grads.shape[0], count, size)
        + flat_scratch(late_rows, count, size),
        compiler_params=pltpu.CompilerParams(
            collective_id=identity, has_side_effects=True, vmem_limit_bytes=64 * 2**20 - 2**19
        ),
        name="backward_%d" % identity,
    )(
        d_branch, early_grads, jnp.asarray(rope), all_in, all_out, slope, heads, chances, joined,
        all_normed, flows, small,
    )


def finish_kernel(grad_in, grad_out, sums, early_sums, weights, newest, d_newest, stored, cotangent, d_flows, *refs):
    states, refs = (refs[0:4], refs[4:8]), refs[8:]
    small, mix, refs = refs[0:4], refs[4:8], refs[8:]
    norm_out, refs = refs[0], refs[1:]
    new_states, refs = (refs[0:5], refs[5:10]), refs[10:]
    new_small, new_mix, refs = refs[0:4], refs[4:8], refs[8:]
    out_streams, grad_streams, grad_stored, refs = refs[0], refs[1], refs[2], refs[3:]
    held, refs = (refs[0:2], refs[2:4], refs[4:6]), refs[6:]
    tiles_in, tiles_out, spread, passed, small_sums, grad_sem, load_sem, save_sem, tile_load, tile_save, pass_sem = refs
    grads = (grad_in, grad_out)
    parts = load_sem.shape[2]
    rows = grad_in.shape[0]
    step_rows = rows // parts

    def load_grad(which):
        return pltpu.make_async_copy(grads[which], held[0][which], grad_sem.at[which])

    def load(which, kind, place):
        spot = pl.ds(place * step_rows, step_rows)
        return pltpu.make_async_copy(
            states[which][kind].at[spot],
            held[1][which].at[kind, spot],
            load_sem.at[which, kind, place],
        )

    def save(which, kind, place):
        spot = pl.ds(place * step_rows, step_rows)
        source = held[1][which].at[kind, spot] if kind < 4 else held[2][which].at[spot]
        return pltpu.make_async_copy(
            source, new_states[which][kind].at[spot], save_sem.at[which, kind, place]
        )

    own = newest.shape[0]
    tile_rows = tiles_in.shape[2]
    tile_count = own // tile_rows
    mixes = STREAMS + LAYER

    def tile_copies(index, into):
        spot = pl.ds(index * tile_rows, tile_rows)
        first, second = (cotangent, stored) if into else (out_streams, grad_stored)
        held_tile = (tiles_in if into else tiles_out).at[index % 2]
        sem = (tile_load if into else tile_save).at[index % 2]
        pairs = [
            (first.at[:, spot], held_tile.at[0:STREAMS]),
            (second.at[:, spot], held_tile.at[STREAMS:mixes]),
        ]
        return [
            pltpu.make_async_copy(*(pair if into else pair[::-1]), sem.at[place])
            for place, pair in enumerate(pairs)
        ]

    def compose(index):
        for copy in tile_copies(index, True):
            copy.wait()
        if index > 1:
            for copy in tile_copies(index - 2, False):
                copy.wait()
        spot = pl.ds(index * tile_rows, tile_rows)
        mix_tile = weights[spot]
        slot = index % 2
        for column in range(MIXH):
            spread[column] = jnp.broadcast_to(mix_tile[:, column : column + 1], (tile_rows, HD))

        def columns(place, carry):
            lanes = pl.ds(pl.multiple_of(place * HD, HD), HD)
            value = newest[spot, lanes]
            flows = [tiles_in[slot, stream, :, lanes].astype(single) for stream in range(STREAMS)]
            results = [spread[stream * LAYERS + LAYER] * value for stream in range(STREAMS)]
            for layer in range(LAYER):
                earlier = tiles_in[slot, STREAMS + layer, :, lanes].astype(single)
                gradient = None
                for stream in range(STREAMS):
                    weight = spread[stream * LAYERS + layer]
                    results[stream] = results[stream] + weight * earlier
                    term = weight * flows[stream]
                    gradient = term if gradient is None else gradient + term
                tiles_out[slot, STREAMS + layer, :, lanes] = gradient.astype(bfloat)
            for stream in range(STREAMS):
                tiles_out[slot, stream, :, lanes] = results[stream].astype(bfloat)
            return carry

        lax.fori_loop(0, D // HD, columns, 0)
        for copy in tile_copies(index, False):
            copy.start()
        if index + 2 < tile_count:
            for copy in tile_copies(index + 2, True):
                copy.start()

    for index in range(2):
        for copy in tile_copies(index, True):
            copy.start()
    for which in range(2):
        load_grad(which).start()
        for place in range(parts):
            for kind in range(4):
                load(which, kind, place).start()
    take_flows = pltpu.make_async_copy(d_flows, passed, pass_sem.at[0])
    give_flows = pltpu.make_async_copy(passed, grad_streams, pass_sem.at[1])
    take_flows.start()
    small_sums[0:4] = sums[0:4]
    small_sums[4:5] = early_sums[MIXH : MIXH + 1]
    small_sums[5:8] = sums[4:7]
    small_sums[8:9] = early_sums[MIXH + 1 : MIXH + 2]
    small_sums[9:10] = early_sums[MIXH + 1 : MIXH + 2]
    small_sums[10:SMALL_MIX] = sums[8 : 8 + SMALL_MIX - 10]
    small_sums[SMALL_MIX : SMALL_MIX + MIXH] = early_sums[0:MIXH]
    small_total = small_sums[...]
    mix_total = jnp.concatenate(
        [early_sums[40:48, place * HD : (place + 1) * HD] for place in range(5)], axis=0
    )[0 : mix[0].shape[0], 0 : mix[0].shape[1]]

    def whole_sum(values):
        return jnp.sum(jnp.sum(values, axis=1, keepdims=True), axis=0, keepdims=True)

    norm = jnp.sqrt(
        whole_sum(sums[7:8, 0:HD])
        + whole_sum(small_total * small_total)
        + whole_sum(mix_total * mix_total)
    )
    norm_out[...] = norm
    factor = clip_norm / jnp.maximum(norm, clip_norm)
    for target, result in zip(
        new_small, adamw_step(*(ref[...] for ref in small), small_total, factor, small_rate)
    ):
        target[...] = result
    for target, result in zip(
        new_mix, adamw_step(*(ref[...] for ref in mix), mix_total, factor, small_rate)
    ):
        target[...] = result
    take_flows.wait()

    def add_residual(index, carry):
        spot = pl.ds(pl.multiple_of(index * 16, 16), 16)
        passed[3, spot] = (passed[3, spot].astype(single) + d_newest[spot]).astype(bfloat)
        return carry

    lax.fori_loop(0, own // 16, add_residual, 0)
    give_flows.start()
    tiles_done = 0
    for which in range(2):
        columns = held[1][which].shape[2]
        load_grad(which).wait()
        for place in range(parts):
            for kind in range(4):
                load(which, kind, place).wait()

            def update(index, carry):
                spot = pl.ds(pl.multiple_of(place * step_rows + index * 16, 16), 16)

                def column(at, inner):
                    lanes = pl.ds(pl.multiple_of(at * 512, 512), 512)
                    results = adamw_step(
                        *(held[1][which][kind, spot, lanes] for kind in range(4)),
                        held[0][which][spot, lanes].astype(single),
                        factor,
                        learn_rate,
                    )
                    for kind in range(4):
                        held[1][which][kind, spot, lanes] = results[kind]
                    held[2][which][spot, lanes] = results[0].astype(bfloat)
                    return inner

                return lax.fori_loop(0, columns // 512, column, carry)

            lax.fori_loop(0, step_rows // 16, update, 0)
            for kind in range(5):
                save(which, kind, place).start()
            if tiles_done < tile_count:
                compose(tiles_done)
                tiles_done += 1
    while tiles_done < tile_count:
        compose(tiles_done)
        tiles_done += 1
    for index in range(tile_count - 2, tile_count):
        for copy in tile_copies(index, False):
            copy.wait()
    give_flows.wait()
    for which in range(2):
        for place in range(parts):
            for kind in range(5):
                save(which, kind, place).wait()


def finish(
    grads, sums, early_sums, weights, newest, d_newest, stored, cotangent, d_flows, in_states, out_states, small, mix
):
    wide = lambda shape: jax.ShapeDtypeStruct(shape, single)
    low = lambda shape: jax.ShapeDtypeStruct(shape, bfloat)
    hbm = pl.BlockSpec(memory_space=pl.ANY)
    vmem = pl.BlockSpec(memory_space=pltpu.VMEM)
    shapes = [in_states[0].shape, out_states[0].shape]
    parts = 4
    tile = (2, STREAMS + LAYER, 16, D)
    return pl.pallas_call(
        finish_kernel,
        out_shape=[wide((1, 1))]
        + [entry for shape in shapes for entry in [wide(shape)] * 4 + [low(shape)]]
        + [wide(small[0].shape)] * 4
        + [wide(mix[0].shape)] * 4
        + [low(cotangent.shape), low(d_flows.shape), low(stored.shape)],
        in_specs=[hbm] * 2 + [vmem] * 5 + [hbm] * 3 + [hbm] * 8 + [vmem] * 8,
        out_specs=[vmem] + [hbm] * 10 + [vmem] * 8 + [hbm] * 3,
        scratch_shapes=[pltpu.VMEM(shape, grads[0].dtype) for shape in shapes]
        + [pltpu.VMEM((4,) + shape, single) for shape in shapes]
        + [pltpu.VMEM(shape, bfloat) for shape in shapes]
        + [pltpu.VMEM(tile, bfloat)] * 2
        + [pltpu.VMEM((MIXH, tile[2], HD), single), pltpu.VMEM(d_flows.shape, bfloat)]
        + [pltpu.VMEM(small[0].shape, single)]
        + [
            pltpu.SemaphoreType.DMA((2,)),
            pltpu.SemaphoreType.DMA((2, 4, parts)),
            pltpu.SemaphoreType.DMA((2, 5, parts)),
            pltpu.SemaphoreType.DMA((2, 2)),
            pltpu.SemaphoreType.DMA((2, 2)),
            pltpu.SemaphoreType.DMA((2,)),
        ],
        compiler_params=pltpu.CompilerParams(vmem_limit_bytes=60 * 2**20),
        name="finish",
    )(
        *grads, sums, early_sums, weights, newest, d_newest, stored, cotangent, d_flows,
        *in_states, *out_states, *small, *mix,
    )


def shards(
    in_streams,
    stored,
    cotangent,
    in_weights,
    in_moment,
    in_second,
    in_average,
    out_weights,
    out_moment,
    output_second_moment,
    out_average,
    small_params,
    small_moment,
    small_second,
    small_average,
    mix_weights,
    mix_moment,
    mix_second,
    mix_average,
):
    groups, count = lax.axis_size("tensor"), lax.axis_size("dp")
    rope = rope_lanes(in_streams.shape[1] * groups)
    (
        full_in,
        full_out,
        normed,
        joined,
        slope,
        heads,
        chances,
        newest,
        d_newest,
        d_branch,
        weights,
        early_grads,
    ) = forward(
        in_streams,
        in_weights,
        out_weights,
        small_params,
        rope,
        stored,
        cotangent,
        mix_weights,
        groups,
        count,
        0,
    )
    grad_in, grad_out, d_flows, early_sums, sums = backward(
        d_branch,
        early_grads,
        rope,
        full_in,
        full_out,
        slope,
        heads,
        chances,
        joined,
        normed,
        in_streams,
        small_params,
        groups,
        count,
        1,
    )
    results = finish(
        (grad_in, grad_out),
        sums,
        early_sums,
        weights,
        newest,
        d_newest,
        stored,
        cotangent,
        d_flows,
        (in_weights, in_moment, in_second, in_average),
        (out_weights, out_moment, output_second_moment, out_average),
        (small_params, small_moment, small_second, small_average),
        (mix_weights, mix_moment, mix_second, mix_average),
    )
    out_streams, grad_streams, grad_stored = results[-3:]
    return (out_streams, grad_streams, grad_stored, results[0][0, 0], *results[1:-3])


def solution(mesh):
    in_specs = (
        P(None, ("dp", "tensor"), None),
        P(None, ("dp", "tensor"), None),
        P(None, ("dp", "tensor"), None),
        P("dp", "tensor"),
        P("dp", "tensor"),
        P("dp", "tensor"),
        P("dp", "tensor"),
        P("dp", "tensor"),
        P("dp", "tensor"),
        P("dp", "tensor"),
        P("dp", "tensor"),
        P(),
        P(),
        P(),
        P(),
        P(),
        P(),
        P(),
        P(),
    )
    out_specs = (
        P(None, ("dp", "tensor"), None),
        P(None, ("dp", "tensor"), None),
        P(None, ("dp", "tensor"), None),
        P(),
        P("dp", "tensor"),
        P("dp", "tensor"),
        P("dp", "tensor"),
        P("dp", "tensor"),
        P("dp", "tensor"),
        P("dp", "tensor"),
        P("dp", "tensor"),
        P("dp", "tensor"),
        P("dp", "tensor"),
        P("dp", "tensor"),
        P(),
        P(),
        P(),
        P(),
        P(),
        P(),
        P(),
        P(),
    )
    return jax.shard_map(shards, mesh=mesh, in_specs=in_specs, out_specs=out_specs, check_vma=False)
```

```python
import jax
import jax.numpy as jnp
import numpy as np
from jax import lax
from jax.experimental import pallas as pl
from jax.experimental.pallas import tpu as pltpu
from jax.sharding import PartitionSpec as P

D = 2048
HEADS = 16
HD = 128
ROT = 32
FF = 8192
STREAMS = 4
LAYER = 8
STEP = 10
LAYERS = 9
MIXH = 36


norm_eps = 1e-05
mix_eps = 1e-06
beta_first = 0.9
beta_second = 0.95
adam_eps = 1e-08
decay_rate = 0.01
learn_rate = 0.03
small_rate = 0.2
clip_norm = 1.0
average_keep = 0.5
masked_score = -1e30
highest_precision = lax.Precision.HIGHEST
bfloat = jnp.bfloat16
single = jnp.float32
MESH = pl.DeviceIdType.MESH


def contract_last(left_side, right_side):
    return lax.dot_general(
        left_side,
        right_side,
        (((left_side.ndim - 1,), (right_side.ndim - 1,)), ((), ())),
        preferred_element_type=single,
    )


def contract_first(left_side, right_side):
    return lax.dot_general(
        left_side, right_side, (((0,), (0,)), ((), ())), preferred_element_type=single
    )


def adamw_step(weight, moment, second, average, gradient, factor, rate):
    clipped = gradient * factor
    moment = beta_first * moment + (1.0 - beta_first) * clipped
    second = beta_second * second + (1.0 - beta_second) * clipped * clipped
    step_ratio = (moment * (1.0 / (1.0 - beta_first**STEP))) / (
        jnp.sqrt(second * (1.0 / (1.0 - beta_second**STEP))) + adam_eps
    )
    weight = weight - rate * (step_ratio + decay_rate * weight)
    average = average_keep * average + (1.0 - average_keep) * weight
    return (weight, moment, second, average)


def enter(partners):
    barrier = pltpu.get_barrier_semaphore()
    for present, device in partners:

        @pl.when(present)
        def _():
            pl.semaphore_signal(barrier, inc=1, device_id=device, device_id_type=MESH)

    pl.semaphore_wait(barrier, sum(present.astype(jnp.int32) for present, _ in partners))


class LineSum:
    def __init__(self, size, give, landing, send_sem, recv_sem, cut):
        self.size, self.give, self.landing = size, give, landing
        self.send_sem, self.recv_sem, self.cut = send_sem, recv_sem, cut
        self.here = lax.axis_index("tensor")
        self.own = landing.shape[1]
        self.rows = self.own // cut
        self.near = lax.select(2 * self.here < size, 1, -1)

    def has_next(self, way):
        return jnp.logical_and(self.here + way >= 0, self.here + way < self.size)

    def spot(self, dest, place):
        return pl.ds(pl.multiple_of(dest * self.own + place * self.rows, 16), self.rows)

    def landed(self, way, dest, place):
        rows = pl.ds(pl.multiple_of(place * self.rows, 16), self.rows)
        return self.landing.at[dest + (1 + way) // 2, rows]

    def hop(self, way, dest, place):
        return pltpu.make_async_remote_copy(
            src_ref=self.give.at[self.spot(dest, place)],
            dst_ref=self.landed(way, dest, place),
            send_sem=self.send_sem.at[(1 - way) // 2, dest, place],
            recv_sem=self.recv_sem.at[(1 - way) // 2, dest, place],
            device_id={"tensor": self.here + way},
            device_id_type=MESH,
        )

    def arrive(self, way, dest, place):
        block = self.landed(way, dest, place)
        pltpu.make_async_remote_copy(
            src_ref=block,
            dst_ref=block,
            send_sem=self.send_sem.at[(1 - way) // 2, dest, place],
            recv_sem=self.recv_sem.at[(1 - way) // 2, dest, place],
            device_id={"tensor": self.here - way},
            device_id_type=MESH,
        ).wait_recv()

    def relay(self, way, dest, first=0, many=None):
        @pl.when((dest - self.here) * way > 0)
        def _():
            def one(place, carry):
                @pl.when(self.has_next(-way))
                def _():
                    self.arrive(way, dest, place)
                    spot = self.spot(dest, place)
                    self.give[spot] = (
                        self.give[spot].astype(single)
                        + self.landed(way, dest, place)[...].astype(single)
                    ).astype(bfloat)

                self.hop(way, dest, place).start()
                return carry

            lax.fori_loop(first, first + (many or self.cut), one, 0)

    def far(self, rank, way):
        return (self.size - 1) * ((1 + way) // 2) - rank * way

    def collect(self, place, into):
        rows = pl.ds(place * self.rows, self.rows)
        into[rows] = self.give[self.spot(self.here, place)].astype(single)
        for way in (1, -1):

            @pl.when(self.has_next(-way))
            def _():
                self.arrive(way, self.here, place)
                into[rows] += self.landed(way, self.here, place)[...].astype(single)

    def drain(self):
        for rank in range(self.size - 1):
            for way in (1, -1):
                dest = self.far(rank, way)

                @pl.when((dest - self.here) * way > 0)
                def _():
                    for place in range(self.cut):
                        self.hop(way, dest, place).wait_send()


class FlatSum:
    def __init__(self, count, size, value, out, landing, crossing, sems):
        self.count, self.size, self.value, self.out = count, size, value, out
        self.landing, self.crossing = landing, crossing
        self.send_a, self.recv_a, self.send_b, self.recv_b, self.send_c, self.recv_c = sems
        self.me = lax.axis_index("dp")
        self.here = lax.axis_index("tensor")
        self.across = min(count, D // HD)
        self.rows, self.lanes = landing.shape[1:]

    def part(self, ref, owner):
        row = pl.multiple_of(owner // self.across * self.rows, 8)
        lane = pl.multiple_of(lax.rem(owner, self.across) * self.lanes, HD)
        return ref.at[pl.ds(row, self.rows), pl.ds(lane, self.lanes)]

    def over(self, first, action):
        total, place = (self.count, self.me) if first else (self.size, self.here)

        def one(step, carry):
            action(lax.rem(place + step, total))
            return carry

        lax.fori_loop(1, total, one, 0)

    def to_owner(self, other):
        return pltpu.make_async_remote_copy(
            src_ref=self.part(self.value, other),
            dst_ref=self.landing.at[self.me],
            send_sem=self.send_a.at[other],
            recv_sem=self.recv_a.at[self.me],
            device_id={"dp": other},
            device_id_type=MESH,
        )

    def across_to(self, other):
        return pltpu.make_async_remote_copy(
            src_ref=self.crossing.at[self.here],
            dst_ref=self.crossing.at[self.here],
            send_sem=self.send_b.at[other],
            recv_sem=self.recv_b.at[self.here],
            device_id={"tensor": other},
            device_id_type=MESH,
        )

    def back_to(self, other):
        return pltpu.make_async_remote_copy(
            src_ref=self.part(self.out, self.me),
            dst_ref=self.part(self.out, self.me),
            send_sem=self.send_c.at[other],
            recv_sem=self.recv_c.at[self.me],
            device_id={"dp": other},
            device_id_type=MESH,
        )

    def arrive(self, block, send, recv, other, axis):
        pltpu.make_async_remote_copy(
            src_ref=block,
            dst_ref=block,
            send_sem=send.at[other],
            recv_sem=recv.at[other],
            device_id={axis: other},
            device_id_type=MESH,
        ).wait_recv()

    def first(self):
        self.over(True, lambda other: self.to_owner(other).start())

    def second(self):
        self.crossing[self.here] = self.part(self.value, self.me)[...]

        def add(other):
            self.arrive(self.landing.at[other], self.send_a, self.recv_a, other, "dp")
            self.crossing[self.here] += self.landing[other]

        self.over(True, add)
        self.over(False, lambda other: self.across_to(other).start())

    def third(self):
        self.over(
            False,
            lambda other: self.arrive(
                self.crossing.at[other], self.send_b, self.recv_b, other, "tensor"
            ),
        )
        result = self.crossing[0]
        for other in range(1, self.size):
            result = result + self.crossing[other]
        self.part(self.out, self.me)[...] = result
        self.over(True, lambda other: self.back_to(other).start())

    def last(self):
        self.over(
            True,
            lambda other: self.arrive(
                self.part(self.out, other), self.send_c, self.recv_c, other, "dp"
            ),
        )
        self.over(True, lambda other: self.to_owner(other).wait_send())
        self.over(False, lambda other: self.across_to(other).wait_send())
        self.over(True, lambda other: self.back_to(other).wait_send())

    def partners(self):
        def others(place, total):
            return [lax.rem(place + step, total) for step in range(1, total)]

        return [{"dp": other} for other in others(self.me, self.count)] + [
            {"tensor": other} for other in others(self.here, self.size)
        ]


def flat_scratch(rows, count, size):
    across = min(count, D // HD)
    part = (rows * across // count, D // across)
    return [
        pltpu.VMEM((count,) + part, single),
        pltpu.VMEM((size,) + part, single),
    ] + [pltpu.SemaphoreType.DMA((n,)) for n in (count, count, size, size, count, count)]


def plus_flips(place, bits):
    moved = place
    for bit in bits:
        moved = moved + (1 - 2 * lax.rem(place // 2**bit, 2)) * 2**bit
    return moved


def cube_routes(count):
    bits = list(range(1, count))
    pieces = []
    for turn in range(len(bits)):
        order = bits[turn:] + bits[:turn]
        arrivals = [()]
        steps = []
        for bit in order:
            fresh = [tuple(sorted(held + (bit,))) for held in arrivals]
            steps.append([(bit, held, whole) for held, whole in zip(arrivals, fresh)])
            arrivals = arrivals + fresh
        pieces.append((arrivals, steps))
    return pieces


class CubeGather:
    def __init__(self, whole, rows, count, sems):
        self.whole, self.rows, self.count = whole, rows, count
        self.send_sem, self.recv_sem, self.pair_send, self.pair_recv = sems
        self.routes = cube_routes(count.bit_length() - 1)
        self.me = lax.axis_index("dp")
        self.piece_rows = rows // len(self.routes)

    def region(self, piece, held):
        first = plus_flips(self.me, held) * self.rows + piece * self.piece_rows
        return self.whole.at[pl.ds(pl.multiple_of(first, 16), self.piece_rows)]

    def hop(self, piece, bit, held, slot, pair=False):
        block = self.region(piece, held)
        return pltpu.make_async_remote_copy(
            src_ref=block,
            dst_ref=block,
            send_sem=(self.pair_send if pair else self.send_sem).at[piece, slot],
            recv_sem=(self.pair_recv if pair else self.recv_sem).at[piece, slot],
            device_id={"dp": plus_flips(self.me, (bit,))},
            device_id_type=MESH,
        )

    def slot(self, piece, held):
        return self.routes[piece][0].index(held)

    def sends_of(self, piece, held):
        found = []
        for step in self.routes[piece][1]:
            for bit, source, landed in step:
                if source == held:
                    found.append(self.hop(piece, bit, held, self.slot(piece, landed)))
        found.append(self.hop(piece, 0, held, self.slot(piece, held), True))
        return found

    def start(self):
        for copies in zip(*(self.sends_of(piece, ()) for piece in range(len(self.routes)))):
            for copy in copies:
                copy.start()

    def step(self, index, which=lambda held: True):
        for piece, (_, steps) in enumerate(self.routes):
            for bit, _, landed in steps[index]:
                if not which(landed):
                    continue
                self.hop(piece, bit, landed, self.slot(piece, landed)).wait_recv()
                for copy in self.sends_of(piece, landed):
                    copy.start()

    def steps(self):
        return len(self.routes)

    def finish(self, which=lambda held: True):
        for piece, (arrivals, _) in enumerate(self.routes):
            for held in filter(which, arrivals):
                self.hop(piece, 0, (0,) + held, self.slot(piece, held), True).wait_recv()

    def drain(self):
        for piece, (arrivals, _) in enumerate(self.routes):
            for held in arrivals:
                for copy in self.sends_of(piece, held):
                    copy.wait_send()


FLOW_ORDER = (3, 1, 2, 0)
CUT = 4
SMALL_MIX = 10 + FF // D


def rope_lanes(length):
    half = ROT // 2
    inverse = 10000.0 ** (-2.0 * np.arange(half) / ROT)
    angles = np.arange(length)[:, None] * inverse[None, :]
    tables = np.zeros((3, length, HD), np.float32)
    tables[0] = 1.0
    tables[0, :, :half] = tables[0, :, half:ROT] = np.cos(angles)
    tables[1, :, :half] = -np.sin(angles)
    tables[2, :, half:ROT] = np.sin(angles)
    return tables


def forward_kernel(
    size,
    count,
    flows,
    w_in,
    w_out,
    small,
    rope,
    stored,
    cotangent,
    mix,
    all_in,
    all_out,
    all_normed,
    joined_out,
    slope_out,
    heads_out,
    chances_out,
    newest,
    d_newest,
    d_branch,
    weights,
    early_grads,
    w_in_low,
    w_out_low,
    normed,
    heads,
    chances,
    joined,
    slope,
    total,
    give,
    terms,
    back,
    earlier,
    dots,
    scales,
    sums,
    mix_low,
    mix_table,
    stage_sem,
    back_sem,
    earlier_sem,
    line_send,
    line_recv,
    term_send,
    term_recv,
    save_sem,
    flow_sem,
    *cube_sems,
):
    here = lax.axis_index("tensor")
    me = lax.axis_index("dp")
    own = flows.shape[1]
    rows_in = w_in.shape[0]
    length = own * size
    width_in, width_out = w_in.shape[1], w_out.shape[1]
    head_width = heads.shape[2]
    group_heads = head_width // HD
    attn_width = 3 * head_width
    units = width_in - attn_width
    bits = count.bit_length() - 1
    sides = ((0, 1), (1, -1))
    tile = 512

    def rows_of(block):
        return pl.ds(pl.multiple_of(block * own, own), own)

    def stage(source, width):
        spans = [(0, min(width, D))] + ([(D, width - D)] if width > D else [])
        return [
            pltpu.make_async_copy(
                source.at[:, pl.ds(first, span)],
                total.at[pl.ds(place * rows_in, rows_in), pl.ds(0, span)],
                stage_sem.at[place],
            )
            for place, (first, span) in enumerate(spans)
        ]

    def settle(source, width, target):
        for place, copy in enumerate(stage(source, width)):
            copy.wait()
            span = min(D, width - place * D)

            def cast(index, carry):
                low = pl.multiple_of(index * 16, 16)
                into = pl.multiple_of(me * rows_in + index * 16, 16)
                target[pl.ds(into, 16), pl.ds(place * D, span)] = total[
                    pl.ds(place * rows_in + low, 16), pl.ds(0, span)
                ].astype(bfloat)
                return carry

            lax.fori_loop(0, rows_in // 16, cast, 0)

    for copy in stage(w_in, width_in):
        copy.start()
    load_back = pltpu.make_async_copy(cotangent, back, back_sem)
    load_back.start()

    def load_earlier(layer):
        return pltpu.make_async_copy(
            stored.at[layer], earlier.at[layer % 2], earlier_sem.at[layer % 2]
        )

    load_earlier(0).start()
    enter(
        [(here < size - 1, {"tensor": here + 1}), (here > 0, {"tensor": here - 1})]
        + [(jnp.bool_(True), {"dp": plus_flips(me, (bit,))}) for bit in range(bits)]
    )

    def line_rows(block, half):
        if half is None:
            return rows_of(block)
        return pl.ds(pl.multiple_of(block * own + half * (own // 2), 16), own // 2)

    def line_hop(side, way, step, flow, half=None):
        block = normed.at[flow, line_rows(here - way * step, half)]
        return pltpu.make_async_remote_copy(
            src_ref=block,
            dst_ref=block,
            send_sem=line_send.at[side, step, flow if half is None else half * STREAMS],
            recv_sem=line_recv.at[side, step, flow if half is None else half * STREAMS],
            device_id={"tensor": here + way},
            device_id_type=MESH,
        )

    def line_landed(side, way, step, flow, half=None):
        block = normed.at[flow, line_rows(here - way * step, half)]
        return pltpu.make_async_remote_copy(
            src_ref=block,
            dst_ref=block,
            send_sem=line_send.at[side, step - 1, flow if half is None else half * STREAMS],
            recv_sem=line_recv.at[side, step - 1, flow if half is None else half * STREAMS],
            device_id={"tensor": here - way},
            device_id_type=MESH,
        )

    def has_next(way):
        return here < size - 1 if way > 0 else here > 0

    def has_origin(way, step):
        return here >= step if way > 0 else here < size - step

    def keep_flow(flow, block):
        return pltpu.make_async_copy(
            normed.at[flow, rows_of(block)],
            all_normed.at[flow, rows_of(block)],
            flow_sem.at[flow, block],
        )

    def send_normal(flow):
        which = 2 if flow == 3 else 0

        def normalize(index, carry):
            spot = pl.ds(pl.multiple_of(index * 16, 16), 16)
            values = flows[flow, spot].astype(single)
            centred = values - jnp.mean(values, axis=-1, keepdims=True)
            inverse = lax.rsqrt(jnp.mean(centred * centred, axis=-1, keepdims=True) + norm_eps)
            into = pl.ds(pl.multiple_of(here * own + index * 16, 16), 16)
            normed[flow, into] = (
                centred * inverse * small[which : which + 1, :] + small[which + 1 : which + 2, :]
            ).astype(bfloat)
            return carry

        lax.fori_loop(0, own // 16, normalize, 0)
        if flow:
            for side, way in sides:
                pl.when(has_next(way))(line_hop(side, way, 0, flow).start)
        keep_flow(flow, here).start()

    cube_in = CubeGather(w_in_low, rows_in, count, cube_sems[:4])
    cube_out = CubeGather(w_out_low, rows_in, count, cube_sems[4:])
    send_normal(FLOW_ORDER[0])
    settle(w_in, width_in, w_in_low)
    cube_in.start()
    for copy in stage(w_out, width_out):
        copy.start()
    for flow in FLOW_ORDER[1:]:
        send_normal(flow)
    settle(w_out, width_out, w_out_low)
    mix_low[...] = jnp.zeros_like(mix_low)
    mix_low[0:MIXH] = small[SMALL_MIX : SMALL_MIX + MIXH].astype(bfloat)
    mix_table[...] = jnp.zeros_like(mix_table)
    mix_table[0:MIXH, 0:MIXH] = mix[0:MIXH]
    mix_table[HD : HD + 1, 0:MIXH] = mix[MIXH : MIXH + 1]
    lane = lax.broadcasted_iota(jnp.int32, (16, HD), 1)
    load_back.wait()
    for layer in range(LAYER):
        if layer + 1 < LAYER:
            load_earlier(layer + 1).start()
        load_earlier(layer).wait()

        def correlate(index, carry):
            spot = pl.ds(pl.multiple_of(index * 16, 16), 16)
            held = earlier[layer % 2, spot].astype(single)
            found = jnp.zeros((16, HD), single) if layer == 0 else dots[spot]
            for stream in range(STREAMS):
                value = jnp.sum(back[stream, spot].astype(single) * held, axis=-1, keepdims=True)
                found = found + jnp.where(lane == stream * LAYERS + layer, value, 0.0)
            dots[spot] = found
            return carry

        lax.fori_loop(0, own // 16, correlate, 0)

    def line_step(step, flow_list):
        for flow in flow_list:
            for side, way in sides:

                @pl.when(has_origin(way, step))
                def _():
                    line_landed(side, way, step, flow).wait_recv()
                    pl.when(has_next(way))(line_hop(side, way, step, flow).start)
                    keep_flow(flow, here - way * step).start()

    def at_distance(step, action):
        if step == 0:
            action(here)
            return

        def one(side, carry):
            block = here - step + 2 * step * side

            @pl.when(jnp.logical_and(block >= 0, block < size))
            def _():
                action(block)

            return carry

        lax.fori_loop(0, 2, one, 0)

    def project(block, part, half=None):
        rows = line_rows(block, half)
        source = normed[part, rows]
        pre = jnp.dot(
            source,
            jnp.concatenate(
                [
                    w_in_low[:, pl.ds((head * 3 + part) * HD, HD)]
                    for head in range(group_heads)
                ],
                axis=1,
            ),
            preferred_element_type=single,
        )
        first = pl.multiple_of(here * head_width, HD)
        pre = pre + small[5 + part : 6 + part, pl.ds(first, head_width)]
        if part == 2:
            heads[part, rows] = pre.astype(bfloat)
            return
        cosine, sine_low, sine_high = rope[0, rows], rope[1, rows], rope[2, rows]
        for head in range(group_heads):
            values = pre[:, head * HD : (head + 1) * HD]
            turned = (
                values * cosine
                + pltpu.roll(values, HD - ROT // 2, 1) * sine_low
                + pltpu.roll(values, ROT // 2, 1) * sine_high
            )
            heads[part, rows, pl.ds(head * HD, HD)] = turned.astype(bfloat)

    def expand(block):
        rows = rows_of(block)

        def one(index, carry):
            first = pl.multiple_of(index * tile, tile)
            pre = jnp.dot(
                normed[3, rows],
                w_in_low[:, pl.ds(attn_width + first, tile)],
                preferred_element_type=single,
            )
            pre = pre + small[pl.ds(10 + here, 1), pl.ds(first, tile)]
            normal = 0.5 * (1.0 + lax.erf(pre * 0.7071067811865476))
            joined[rows, pl.ds(head_width + first, tile)] = (pre * normal).astype(bfloat)
            slope[rows, pl.ds(first, tile)] = (
                normal + pre * jnp.exp(-0.5 * pre * pre) * 0.3989422804014327
            ).astype(bfloat)
            return carry

        lax.fori_loop(0, units // tile, one, 0)

    def contract(which):
        if rows_in % HD:
            return
        for held in filter(which, cube_out.routes[0][0]):
            for pair in ((), (0,)):
                first = pl.multiple_of(plus_flips(me, pair + held) * rows_in, HD)
                total[:, pl.ds(first, rows_in)] = contract_last(
                    joined[:, pl.ds(head_width, units)],
                    w_out_low[pl.ds(first, rows_in), pl.ds(head_width, units)],
                )

    def contract_whole():
        def one(index, carry):
            first = pl.multiple_of(index * tile, tile)
            total[:, pl.ds(first, tile)] = contract_last(
                joined[:, pl.ds(head_width, units)],
                w_out_low[pl.ds(first, tile), pl.ds(head_width, units)],
            )
            return carry

        lax.fori_loop(0, D // tile, one, 0)

    def direct(held):
        return len(held) <= 1

    def indirect(held):
        return len(held) > 1

    def attend(block, half=None):
        rows = line_rows(block, half)
        shape = (rows.size, length)
        places = rows.start + lax.broadcasted_iota(jnp.int32, shape, 0)
        allowed = lax.broadcasted_iota(jnp.int32, shape, 1) <= places
        for head in range(group_heads):
            lanes = pl.ds(head * HD, HD)
            scores = contract_last(heads[0, rows, lanes], heads[1, :, lanes]) * HD ** (-0.5)
            scores = jnp.where(allowed, scores, masked_score)
            raised = jnp.exp(scores - jnp.max(scores, axis=-1, keepdims=True))
            low = (raised / jnp.sum(raised, axis=-1, keepdims=True)).astype(bfloat)
            chances[head, rows] = low
            joined[rows, lanes] = jnp.dot(
                low, heads[2, :, lanes], preferred_element_type=single
            ).astype(bfloat)

    def emit(block, half=None):
        rows = line_rows(block, half)

        def one(index, carry):
            first = pl.multiple_of(index * tile, tile)
            spot = (rows, pl.ds(first, tile))
            give[spot] = (
                total[spot]
                + contract_last(
                    joined[rows, pl.ds(0, head_width)],
                    w_out_low[pl.ds(first, tile), pl.ds(0, head_width)],
                )
            ).astype(bfloat)
            return carry

        lax.fori_loop(0, D // tile, one, 0)

    def save(place, source, target):
        return pltpu.make_async_copy(source, target, save_sem.at[place])

    chain = LineSum(size, give, terms, term_send, term_recv, CUT)
    ending = jnp.logical_or(here == 0, here == size - 1)

    def query_pass(side, way, step):
        @pl.when(has_origin(way, step))
        def _():
            for half in range(2):
                line_landed(side, way, step, 0, half).wait_recv()
                pl.when(has_next(way))(line_hop(side, way, step, 0, half).start)
            keep_flow(0, here - way * step).start()

    def query_side(side, way):
        for step in range(size - 1, 0, -1):
            query_pass(side, way, step)
        for half in range(2):
            pl.when(has_next(way))(line_hop(side, way, 0, 0, half).start)

    cube_in.step(0)
    cube_out.start()
    line_step(1, FLOW_ORDER[:3])
    lower = 2 * here < size
    pl.when(lower)(lambda: query_side(0, 1))
    pl.when(jnp.logical_not(lower))(lambda: query_side(1, -1))
    line_step(2, FLOW_ORDER[:1])
    for index in range(1, cube_in.steps()):
        cube_in.step(index)
    line_step(2, FLOW_ORDER[1:3])
    cube_in.finish()
    save(0, w_in_low, all_in).start()

    def early(block):
        project(block, 1)
        project(block, 2)
        expand(block)

    at_distance(0, early)
    at_distance(1, early)
    cube_out.step(0)
    at_distance(2, early)
    project(here, 0)

    @pl.when(jnp.logical_not(ending))
    def _():
        pl.when(lower)(lambda: query_side(1, -1))
        pl.when(jnp.logical_not(lower))(lambda: query_side(0, 1))

        def one(index, carry):
            project(lax.rem(here + 1 + index, size), 0)
            return carry

        lax.fori_loop(0, size - 1, one, 0)

        def two(block, carry):
            attend(block)
            return carry

        lax.fori_loop(0, size, two, 0)

    for step in range(3, size):
        line_step(step, FLOW_ORDER[:1])
        at_distance(step, expand)
    for index in range(1, cube_out.steps()):
        cube_out.step(index, direct)
    cube_out.finish(direct)
    contract(direct)

    def keys_values(block):
        project(block, 1)
        project(block, 2)

    for step in range(3, size):
        line_step(step, FLOW_ORDER[1:3])
        at_distance(step, keys_values)
    pl.when(ending)(lambda: attend(here))
    for index in range(1, cube_out.steps()):
        cube_out.step(index, indirect)
    cube_out.finish(indirect)
    save(1, w_out_low, all_out).start()
    if rows_in % HD:
        contract_whole()
    else:
        contract(indirect)

    @pl.when(jnp.logical_not(ending))
    def _():
        def one(index, carry):
            emit(lax.rem(here + 1 + index, size))
            return carry

        lax.fori_loop(0, size - 1, one, 0)

    for rank in range(size - 1):
        step = size - 1 - rank

        @pl.when(ending)
        def _():
            dest = lax.select(here == 0, size - 1 - rank, rank)
            side = lax.select(here == 0, 1, 0)

            def one(half, carry):
                block = normed.at[0, line_rows(dest, half)]
                pltpu.make_async_remote_copy(
                    src_ref=block,
                    dst_ref=block,
                    send_sem=line_send.at[side, step - 1, half * STREAMS],
                    recv_sem=line_recv.at[side, step - 1, half * STREAMS],
                    device_id={"tensor": lax.select(here == 0, 1, size - 2)},
                    device_id_type=MESH,
                ).wait_recv()
                project(dest, 0, half)
                attend(dest, half)
                emit(dest, half)
                chain.relay(chain.near, dest, half * (CUT // 2), CUT // 2)
                return carry

            lax.fori_loop(0, 2, one, 0)
            keep_flow(0, dest).start()

        @pl.when(jnp.logical_not(ending))
        def _():
            for way in (chain.near, -chain.near):
                chain.relay(way, chain.far(rank, way))

    emit(here)
    saves = [
        save(2, joined, joined_out),
        save(3, slope, slope_out),
        save(4, heads, heads_out),
        save(5, chances, chances_out),
    ]
    for copy in saves:
        copy.start()
    for place in range(CUT):
        chain.collect(place, newest)

    def sixteen(index):
        spot = pl.ds(pl.multiple_of(index * 16, 16), 16)
        return spot, pl.ds(pl.multiple_of(here * own + index * 16, 16), 16)

    def compose(index, carry):
        spot, inner = sixteen(index)
        value = flows[3, spot].astype(single) + newest[spot] + small[8:9, :] + small[9:10, :]
        newest[spot] = value
        inverse = lax.rsqrt(jnp.mean(value * value, axis=-1, keepdims=True) + mix_eps)
        scales[spot] = jnp.broadcast_to(inverse, (16, HD))
        give[inner] = (value * inverse * small[4:5, :]).astype(bfloat)
        found = dots[spot]
        for stream in range(STREAMS):
            dot = jnp.sum(back[stream, spot].astype(single) * value, axis=-1, keepdims=True)
            found = found + jnp.where(lane == stream * LAYERS + LAYER, dot, 0.0)
        dots[spot] = found
        return carry

    lax.fori_loop(0, own // 16, compose, 0)
    mix_normed = give[rows_of(here)]
    mix_pre = contract_last(mix_normed, mix_low[...])
    normal = 0.5 * (1.0 + lax.erf(mix_pre * 0.7071067811865476))
    act = mix_pre * normal
    act_slope = normal + mix_pre * jnp.exp(-0.5 * mix_pre * mix_pre) * 0.3989422804014327
    table = mix_table[0:HD]
    weights[...] = (
        jnp.dot(act, table, precision=highest_precision, preferred_element_type=single)
        + mix_table[HD : HD + 1]
    )
    d_mixing = dots[...]
    d_act = lax.dot_general(
        d_mixing,
        table,
        (((1,), (1,)), ((), ())),
        precision=highest_precision,
        preferred_element_type=single,
    )
    d_mix_pre = (d_act * act_slope).astype(bfloat)
    out_grad = lax.dot_general(
        act,
        d_mixing,
        (((0,), (0,)), ((), ())),
        precision=highest_precision,
        preferred_element_type=single,
    )
    scales_sum = jnp.sum(d_mixing, axis=0, keepdims=True)
    early_grads[MIXH:] = jnp.zeros((early_grads.shape[0] - MIXH, D), single)
    for place in range((MIXH + 7) // 8):
        rows_left = min(8, MIXH - place * 8)
        early_grads[40 : 40 + rows_left, place * HD : (place + 1) * HD] = out_grad[
            place * 8 : place * 8 + rows_left
        ]
    early_grads[40 + MIXH % 8 : 41 + MIXH % 8, MIXH // 8 * HD : MIXH // 8 * HD + HD] = scales_sum

    def spread(index, carry):
        lanes = pl.ds(pl.multiple_of(index * tile, tile), tile)
        total[0:own, lanes] = jnp.dot(
            d_mix_pre, mix_low[:, lanes], preferred_element_type=single
        )
        early_grads[0:MIXH, lanes] = contract_first(d_mix_pre, give[rows_of(here), lanes])[0:MIXH]
        return carry

    lax.fori_loop(0, D // tile, spread, 0)
    sums[...] = jnp.zeros_like(sums)

    def descend(index, carry):
        spot, inner = sixteen(index)
        value, inverse = newest[spot], scales[spot][:, 0:1]
        d_normed = total[spot]
        scaled = d_normed * small[4:5, :]
        middle = jnp.mean(scaled * value, axis=-1, keepdims=True)
        result = inverse * scaled - value * (inverse * inverse * inverse * middle)
        for stream in range(STREAMS):
            column = stream * LAYERS + LAYER
            result = result + weights[spot][:, column : column + 1] * back[stream, spot].astype(
                single
            )
        d_newest[spot] = result
        d_branch[spot] = result.astype(bfloat)
        gain = d_normed * value * inverse
        sums[0] += gain[0:8] + gain[8:16]
        sums[1] += result[0:8] + result[8:16]
        return carry

    lax.fori_loop(0, own // 16, descend, 0)
    early_grads[MIXH : MIXH + 1] = jnp.sum(sums[0], axis=0, keepdims=True)
    early_grads[MIXH + 1 : MIXH + 2] = jnp.sum(sums[1], axis=0, keepdims=True)
    for step in range(size):
        for flow in FLOW_ORDER:
            for side, way in sides:

                @pl.when(jnp.logical_and(has_next(way), has_origin(way, step)))
                def _():
                    for half in range(2) if flow == 0 else [None]:
                        line_hop(side, way, step, flow, half).wait_send()

    cube_in.drain()
    cube_out.drain()
    chain.drain()
    for flow in FLOW_ORDER:
        for block in range(size):
            keep_flow(flow, block).wait()
    save(0, w_in_low, all_in).wait()
    save(1, w_out_low, all_out).wait()
    for copy in saves:
        copy.wait()


def forward(flows, w_in, w_out, small, rope, stored, cotangent, mix_weights, size, count, identity):
    own = flows.shape[1]
    length = own * size
    rows, width_in = w_in.shape
    width_out = w_out.shape[1]
    head_width = HEADS // size * HD
    units = FF // size
    pieces = count.bit_length() - 2
    cube = [pltpu.SemaphoreType.DMA((pieces, 2**pieces))] * 8
    low = lambda *shape: jax.ShapeDtypeStruct(shape, bfloat)
    hbm = pl.BlockSpec(memory_space=pl.ANY)
    vmem = pl.BlockSpec(memory_space=pltpu.VMEM)
    return pl.pallas_call(
        lambda *refs: forward_kernel(size, count, *refs),
        out_shape=[
            low(D, width_in),
            low(D, width_out),
            low(STREAMS, length, D),
            low(length, width_out),
            low(length, units),
            low(3, length, head_width),
            low(HEADS // size, length, length),
            jax.ShapeDtypeStruct((own, D), single),
            jax.ShapeDtypeStruct((own, D), single),
            low(own, D),
            jax.ShapeDtypeStruct((own, HD), single),
            jax.ShapeDtypeStruct((48, D), single),
        ],
        in_specs=[vmem, hbm, hbm, vmem, vmem, hbm, hbm, vmem],
        out_specs=[hbm] * 7 + [vmem] * 5,
        scratch_shapes=[
            pltpu.VMEM((D, width_in), bfloat),
            pltpu.VMEM((D, width_out), bfloat),
            pltpu.VMEM((STREAMS, length, D), bfloat),
            pltpu.VMEM((3, length, head_width), bfloat),
            pltpu.VMEM((HEADS // size, length, length), bfloat),
            pltpu.VMEM((length, width_out), bfloat),
            pltpu.VMEM((length, units), bfloat),
            pltpu.VMEM((length, D), single),
            pltpu.VMEM((length, D), bfloat),
            pltpu.VMEM((size + 1, own, D), bfloat),
            pltpu.VMEM((STREAMS, own, D), bfloat),
            pltpu.VMEM((2, own, D), bfloat),
            pltpu.VMEM((own, HD), single),
            pltpu.VMEM((own, HD), single),
            pltpu.VMEM((2, 8, D), single),
            pltpu.VMEM((HD, D), bfloat),
            pltpu.VMEM((HD + 8, HD), single),
            pltpu.SemaphoreType.DMA((2,)),
            pltpu.SemaphoreType.DMA,
            pltpu.SemaphoreType.DMA((2,)),
            pltpu.SemaphoreType.DMA((2, size, STREAMS + 1)),
            pltpu.SemaphoreType.DMA((2, size, STREAMS + 1)),
            pltpu.SemaphoreType.DMA((2, size, CUT)),
            pltpu.SemaphoreType.DMA((2, size, CUT)),
            pltpu.SemaphoreType.DMA((6,)),
            pltpu.SemaphoreType.DMA((STREAMS, size)),
        ]
        + cube,
        compiler_params=pltpu.CompilerParams(
            collective_id=identity, has_side_effects=True, vmem_limit_bytes=60 * 2**20
        ),
        name="forward_%d" % identity,
    )(flows, w_in, w_out, small, jnp.asarray(rope), stored, cotangent, mix_weights)


def backward_kernel(
    size,
    count,
    d_branch,
    early_grads,
    rope,
    all_in,
    all_out,
    slope_in,
    heads_in,
    chances_in,
    joined_in,
    all_normed,
    flows_in,
    small,
    grad_in,
    grad_out,
    d_flows,
    early_sums,
    late_sums,
    arena,
    give,
    wide,
    heads,
    chances,
    back,
    d_up,
    d_pre,
    parts,
    terms,
    flows,
    total,
    sums,
    work,
    late,
    squares,
    arena_sem,
    load_sem,
    tile_sem,
    flow_sem,
    keep_sem,
    save_sem,
    line_send,
    line_recv,
    term_send,
    term_recv,
    give_sem,
    pair_sem,
    credit,
    ready,
    cube_send,
    cube_recv,
    *flat_refs,
):
    here = lax.axis_index("tensor")
    me = lax.axis_index("dp")
    bits = count.bit_length() - 1
    routes = cube_routes(bits)
    pieces = len(routes)
    subsets = sorted(routes[0][0], key=lambda held: -len(held))
    last = len(subsets) - 1
    own = flows.shape[1]
    length = own * size
    tile = arena.shape[2]
    head_width = heads.shape[2]
    group_heads = head_width // HD
    units = d_up.shape[1]
    tiles_out = (head_width + units) // tile
    tiles_in = (3 * head_width + units) // tile
    first_up = tiles_out + 3 * head_width // tile
    groups = (
        (0, tiles_out),
        (tiles_out, first_up - tiles_out),
        (first_up, tiles_out + tiles_in - first_up),
    )
    give_first = (0, tiles_out, 0)
    rows = D // count
    piece_rows = rows // pieces
    lane_rows = max(rows, HD)
    kept_first, land_first, pair_first = 0, D // 2, D - rows
    sides = ((0, 1), (1, -1))
    scale = HD ** (-0.5)
    ending = jnp.logical_or(here == 0, here == size - 1)

    def rows_of(block):
        return pl.ds(pl.multiple_of(block * own, own), own)

    def load_arena(index):
        source, place = (all_out, index) if index < tiles_out else (all_in, index - tiles_out)
        return pltpu.make_async_copy(
            source.at[:, pl.ds(place * tile, tile)], arena.at[index], arena_sem.at[index]
        )

    load_branch = pltpu.make_async_copy(d_branch, back.at[rows_of(here)], load_sem.at[0])
    load_slope = pltpu.make_async_copy(slope_in, wide.at[:, pl.ds(0, units)], load_sem.at[1])
    load_heads = pltpu.make_async_copy(heads_in, heads, load_sem.at[2])
    load_chances = pltpu.make_async_copy(chances_in, chances, load_sem.at[3])
    load_joined = pltpu.make_async_copy(joined_in, wide, load_sem.at[4])

    def load_flow(flow):
        return pltpu.make_async_copy(
            flows_in.at[flow], flows.at[flow % 2], flow_sem.at[flow % 2]
        )

    def keep_flow(flow):
        return pltpu.make_async_copy(
            flows.at[flow % 2], d_flows.at[flow], keep_sem.at[flow % 2]
        )

    load_rope = pltpu.make_async_copy(
        rope, total.at[:, pl.ds(0, rope.shape[1])], load_sem.at[5]
    )
    load_branch.start()
    half = len(flat_refs) // 2
    early = FlatSum(count, size, early_grads, early_sums, *flat_refs[:2], flat_refs[2:half])
    final = FlatSum(
        count, size, late, late_sums, *flat_refs[half : half + 2], flat_refs[half + 2 :]
    )
    enter([(jnp.bool_(True), partner) for partner in early.partners()])

    def has_next(way):
        return here < size - 1 if way > 0 else here > 0

    def has_origin(way, step):
        return here >= step if way > 0 else here < size - step

    def line_hop(side, way, step):
        block = back.at[rows_of(here - way * step)]
        return pltpu.make_async_remote_copy(
            src_ref=block,
            dst_ref=block,
            send_sem=line_send.at[side, step],
            recv_sem=line_recv.at[side, step],
            device_id={"tensor": here + way},
            device_id_type=MESH,
        )

    def line_landed(side, way, step):
        block = back.at[rows_of(here - way * step)]
        return pltpu.make_async_remote_copy(
            src_ref=block,
            dst_ref=block,
            send_sem=line_send.at[side, step - 1],
            recv_sem=line_recv.at[side, step - 1],
            device_id={"tensor": here - way},
            device_id_type=MESH,
        )

    load_branch.wait()
    for side, way in sides:
        pl.when(has_next(way))(line_hop(side, way, 0).start)
    load_rope.start()
    for index in range(tiles_out):
        load_arena(index).start()
    load_slope.start()
    for index in range(first_up, tiles_out + tiles_in):
        load_arena(index).start()
    load_heads.start()
    load_chances.start()
    for index in range(tiles_out, first_up):
        load_arena(index).start()
    load_flow(3).start()
    load_flow(0).start()
    early.first()

    def pull(block):
        spot = rows_of(block)
        wide[spot, pl.ds(units, head_width)] = jnp.dot(
            back[spot], arena[0], preferred_element_type=single
        ).astype(bfloat)

        def one(index, carry):
            lanes = pl.ds(pl.multiple_of(index * tile, tile), tile)
            d_hidden = jnp.dot(
                back[spot], arena[head_width // tile + index], preferred_element_type=single
            )
            d_up[spot, lanes] = (d_hidden * wide[spot, lanes].astype(single)).astype(bfloat)
            return carry

        lax.fori_loop(0, units // tile, one, 0)

    def push(block):
        spot = rows_of(block)

        def one(index, carry):
            lanes = pl.ds(pl.multiple_of(index * tile, tile), tile)
            value = None
            for place in range(units // tile):
                term = contract_last(
                    d_up[spot, pl.ds(place * tile, tile)], arena[first_up + place, lanes]
                )
                value = term if value is None else value + term
            parts[3, spot, lanes] = value.astype(bfloat)
            return carry

        lax.fori_loop(0, D // tile, one, 0)

    late[...] = jnp.zeros_like(late)

    def turn_back(gradients, first, blocks):
        def table(kind):
            lanes = [
                pl.ds(pl.multiple_of((kind * size + first + block) * HD, HD), HD)
                for block in range(blocks)
            ]
            return jnp.concatenate([total[:, lane] for lane in lanes], axis=0)

        return (
            gradients * table(0)
            - pltpu.roll(gradients, HD - ROT // 2, 1) * table(1)
            - pltpu.roll(gradients, ROT // 2, 1) * table(2)
        )

    def attend_back(block):
        spot = rows_of(block)
        for head in range(group_heads):
            lanes = pl.ds(head * HD, HD)
            chance = chances[head, spot].astype(single)
            d_chance = contract_last(
                wide[spot, pl.ds(units + head * HD, HD)], heads[2, :, lanes]
            )
            centre = jnp.sum(d_chance * chance, axis=-1, keepdims=True)
            d_score = (chance * (d_chance - centre)).astype(bfloat)
            parts[1, spot, pl.ds(head * length, length)] = d_score
            d_query = jnp.dot(d_score, heads[1, :, lanes], preferred_element_type=single) * scale
            d_query = turn_back(d_query, block, 1).astype(bfloat)
            d_pre[0, spot, lanes] = d_query
            bias_lanes = pl.ds(pl.multiple_of(here * head_width + head * HD, HD), HD)
            late[4:5, bias_lanes] += jnp.sum(d_query.astype(single), axis=0, keepdims=True)

    chains = [
        LineSum(
            size,
            parts.at[flow],
            terms.at[flow],
            term_send.at[flow],
            term_recv.at[flow],
            CUT if flow == 3 else 1,
        )
        for flow in range(STREAMS)
    ]

    def relay(flow, rank):
        for sign in (1, -1):
            way = sign * chains[flow].near
            chains[flow].relay(way, chains[flow].far(rank, way))

    def middle(action):
        pl.when(jnp.logical_not(ending))(action)

    def spread_rows(flow, spot):
        def one(index, carry):
            lanes = pl.ds(pl.multiple_of(index * tile, tile), tile)
            columns = []
            for head in range(group_heads):
                place, lane = divmod((head * 3 + flow) * HD, tile)
                columns.append(arena[tiles_out + place, lanes, pl.ds(lane, HD)])
            parts[flow, spot, lanes] = contract_last(
                d_pre[flow, spot], jnp.concatenate(columns, axis=1)
            ).astype(bfloat)
            return carry

        lax.fori_loop(0, D // tile, one, 0)

    def spread(flow):
        spread_rows(flow, pl.ds(0, length))

        @pl.when(ending)
        def _():
            for rank in range(size - 1):
                relay(flow, rank)

    for index in range(tiles_out):
        load_arena(index).wait()
    load_slope.wait()
    pull(here)
    load_heads.wait()
    load_chances.wait()
    load_rope.wait()
    attend_back(here)
    early.second()
    for step in range(1, size):
        for side, way in sides:

            @pl.when(has_origin(way, step))
            def _():
                line_landed(side, way, step).wait_recv()
                pl.when(has_next(way))(line_hop(side, way, step).start)

        if step == 1:
            for index in range(tiles_out, tiles_out + tiles_in):
                load_arena(index).wait()
            spread_rows(0, rows_of(here))

        def both(side, carry):
            block = here - step + 2 * step * side

            @pl.when(jnp.logical_and(block >= 0, block < size))
            def _():
                pull(block)
                push(block)
                attend_back(block)
                spread_rows(0, rows_of(block))

            return carry

        lax.fori_loop(0, 2, both, 0)
        for flow in (3, 0):
            pl.when(ending)(lambda: relay(flow, size - 1 - step))
        if step == min(2, size - 1):
            early.third()

    def tell(which):
        for bit in range(bits):
            pl.semaphore_signal(
                ready.at[which, bit],
                inc=1,
                device_id={"dp": plus_flips(me, (bit,))},
                device_id_type=MESH,
            )

    tell(0)
    for head in range(group_heads):
        lanes = pl.ds(head * HD, HD)
        wide_lanes = pl.ds(head * length, length)
        d_key = contract_first(parts[1, :, wide_lanes], heads[0, :, lanes]) * scale
        d_key = turn_back(d_key, 0, size).astype(bfloat)
        d_value = contract_first(
            chances[head], wide[:, pl.ds(units + head * HD, HD)]
        ).astype(bfloat)
        d_pre[1, :, lanes] = d_key
        d_pre[2, :, lanes] = d_value
        bias_lanes = pl.ds(pl.multiple_of(here * head_width + head * HD, HD), HD)
        late[5:6, bias_lanes] = jnp.sum(d_key.astype(single), axis=0, keepdims=True)
        late[6:7, bias_lanes] = jnp.sum(d_value.astype(single), axis=0, keepdims=True)

    def first_lane(held):
        return pl.multiple_of(plus_flips(me, held) * rows // lane_rows * lane_rows, HD)

    def normal_lanes(slot):
        return pl.ds(slot * lane_rows, lane_rows)

    def load_tile(slot, held):
        return pltpu.make_async_copy(
            all_normed.at[:, :, pl.ds(first_lane(held), lane_rows)],
            chances.at[:, :, normal_lanes(slot)],
            tile_sem.at[slot],
        )

    load_joined.start()
    load_tile(0, (0,) + subsets[0]).start()
    load_tile(1, subsets[0]).start()


    def own_rows(value, held):
        if lane_rows == rows:
            return value
        work[...] = value
        first = lax.rem(plus_flips(me, held) * rows, lane_rows)
        return work[pl.ds(pl.multiple_of(first, 16), rows)]

    def products(which, held, slot, emit):
        if which == 0:
            source = back[:, pl.ds(first_lane(held), lane_rows)]

            def one(index, carry):
                lanes = pl.ds(pl.multiple_of(index * tile, tile), tile)
                emit(own_rows(contract_first(source, wide[:, lanes]), held), index, 0)
                return carry

            lax.fori_loop(0, tiles_out, one, 0)
            return
        if which == 1:
            for part in range(3):
                value = own_rows(
                    contract_first(chances[part, :, normal_lanes(slot)], d_pre[part]), held
                )
                for head in range(group_heads):
                    place, lane = divmod((head * 3 + part) * HD, tile)
                    emit(value[:, head * HD : (head + 1) * HD], place, lane)
            return

        def one(index, carry):
            lanes = pl.ds(pl.multiple_of(index * tile, tile), tile)
            value = contract_first(chances[3, :, normal_lanes(slot)], d_up[:, lanes])
            emit(own_rows(value, held), index, 0)
            return carry

        lax.fori_loop(0, units // tile, one, 0)

    def place_of(held):
        return sum(2 ** (bit - 1) for bit in held)

    def pass_pair(which):
        first, span = groups[which]
        return pltpu.make_async_remote_copy(
            src_ref=give.at[pl.ds(give_first[which], span)],
            dst_ref=arena.at[pl.ds(first, span), pl.ds(pair_first, rows)],
            send_sem=give_sem.at[which],
            recv_sem=pair_sem.at[which],
            device_id={"dp": plus_flips(me, (0,))},
            device_id_type=MESH,
        )

    def kept_row(piece, held):
        return kept_first + place_of(held) * rows + piece * piece_rows

    def land_row(piece, landed):
        return land_first + (piece * last + place_of(landed) - 1) * piece_rows

    def cube_hop(which, piece, bit, landed):
        tiles = pl.ds(*groups[which])
        return pltpu.make_async_remote_copy(
            src_ref=arena.at[tiles, pl.ds(kept_row(piece, landed), piece_rows)],
            dst_ref=arena.at[tiles, pl.ds(land_row(piece, landed), piece_rows)],
            send_sem=cube_send.at[which, piece, place_of(landed)],
            recv_sem=cube_recv.at[which, piece, place_of(landed)],
            device_id={"dp": plus_flips(me, (bit,))},
            device_id_type=MESH,
        )

    def needs(piece, held):
        return [
            (bit, landed)
            for step in routes[piece][1]
            for bit, source, landed in step
            if source == held
        ]

    def add_landed(which, piece, held):
        for bit, landed in needs(piece, held):
            cube_hop(which, piece, bit, landed).wait_recv()
        first, span = groups[which]

        def one(index, carry):
            def column(at, inner):
                spot = pl.ds(pl.multiple_of(kept_row(piece, held) + index * 16, 16), 16)
                value = arena[first + at, spot].astype(single)
                for _, landed in needs(piece, held):
                    arrived = pl.ds(pl.multiple_of(land_row(piece, landed) + index * 16, 16), 16)
                    value = value + arena[first + at, arrived].astype(single)
                arena[first + at, spot] = value.astype(bfloat)
                if not held:
                    value = value * value
                    value = value[0:8] + value[8:16]
                    for group in range(tile // HD):
                        inner = inner + value[:, group * HD : (group + 1) * HD]
                return inner

            return lax.fori_loop(0, span, column, carry)

        found = lax.fori_loop(0, piece_rows // 16, one, jnp.zeros((8, HD), single))
        if not held:
            squares[...] += found

    def offer(which, index):
        held = subsets[index]
        if index > 0:
            pass_pair(which).wait_send()
        else:
            for bit in range(bits):
                pl.semaphore_wait(ready.at[which, bit], 1)
        if which == 1:
            load_tile(0, (0,) + held).wait()

        def emit(value, place, lane):
            give[give_first[which] + place, :, pl.ds(lane, value.shape[1])] = value.astype(bfloat)

        products(which, (0,) + held, 0, emit)
        if index > 0:
            pl.semaphore_wait(credit.at[which], 1)
        pass_pair(which).start()
        if which == 2 and index < last:
            load_tile(0, (0,) + subsets[index + 1]).start()

    def keep(which, index):
        held = subsets[index]
        first, _ = groups[which]
        if which == 1:
            load_tile(1, held).wait()
        pass_pair(which).wait_recv()

        def emit(value, place, lane):
            lanes = pl.ds(lane, value.shape[1])
            arena[first + place, pl.ds(kept_first + place_of(held) * rows, rows), lanes] = (
                value + arena[first + place, pl.ds(pair_first, rows), lanes].astype(single)
            ).astype(bfloat)

        products(which, held, 1, emit)
        if index < last:
            pl.semaphore_signal(
                credit.at[which],
                inc=1,
                device_id={"dp": plus_flips(me, (0,))},
                device_id_type=MESH,
            )
        else:
            pass_pair(which).wait_send()
        for piece, (_, steps) in enumerate(routes):
            for bit, _, landed in steps[-1]:
                if landed == held:
                    cube_hop(which, piece, bit, landed).start()
        if which == 2 and index < last:
            load_tile(1, subsets[index + 1]).start()

    def pass_on(which):
        for step in range(pieces - 2, -1, -1):
            for piece, (_, steps) in enumerate(routes):
                for bit, _, landed in steps[step]:
                    add_landed(which, piece, landed)
                    cube_hop(which, piece, bit, landed).start()

    def descend(flow):
        for place in range(chains[flow].cut):
            chains[flow].collect(place, total)
        load_flow(flow).wait()
        gain = 2 if flow == 3 else 0
        slot = flow % 2

        def one(index, carry):
            spot = pl.ds(pl.multiple_of(index * 16, 16), 16)
            values = flows[slot, spot].astype(single)
            centred = values - jnp.mean(values, axis=-1, keepdims=True)
            inverse = lax.rsqrt(jnp.mean(centred * centred, axis=-1, keepdims=True) + norm_eps)
            unit = centred * inverse
            incoming = total[spot]
            scaled = incoming * small[gain : gain + 1, :]
            result = inverse * (
                scaled
                - jnp.mean(scaled, axis=-1, keepdims=True)
                - unit * jnp.mean(scaled * unit, axis=-1, keepdims=True)
            )
            flows[slot, spot] = result.astype(bfloat)
            unit = unit * incoming
            sums[gain] += unit[0:8] + unit[8:16]
            sums[gain + 1] += incoming[0:8] + incoming[8:16]
            return carry

        lax.fori_loop(0, own // 16, one, 0)
        keep_flow(flow).start()

    def near(flow, rank):
        way = chains[flow].near
        middle(lambda: chains[flow].relay(way, chains[flow].far(rank, way)))

    def beyond(flow, rank):
        way = -chains[flow].near
        middle(lambda: chains[flow].relay(way, chains[flow].far(rank, way)))

    def unit_sum(index, carry):
        lanes = pl.ds(pl.multiple_of(index * 256, 256), 256)
        late[pl.ds(8 + here, 1), lanes] = jnp.sum(
            d_up[:, lanes].astype(single), axis=0, keepdims=True
        )
        return carry

    def release():
        push(here)
        tell(2)

    def closing():
        spread(2)
        tell(1)

    between = [lambda: spread(1), closing, release]
    load_joined.wait()
    for index in range(last + 1):
        offer(0, index)
        if between:
            between.pop(0)()
        if index == last:
            for action in between:
                action()
            offer(1, 0)
        keep(0, index)
        if index < 2:
            for rank in range(size - 2, 0, -1):
                middle(lambda: relay((3, 0)[index], rank))
    near(3, 0)
    offer(2, 0)
    lax.fori_loop(0, units // 256, unit_sum, 0)
    between = [lambda: near(0, 0), lambda: pass_on(0), lambda: beyond(3, 0)]
    for index in range(last + 1):
        keep(1, index)
        if index < last:
            offer(1, index + 1)
        keep(2, index)
        if index < last:
            offer(2, index + 1)
        if between:
            between.pop(0)()
    for action in between:
        action()
    sums[...] = jnp.zeros_like(sums)
    beyond(0, 0)
    near(1, 0)
    descend(3)
    descend(0)
    keep_flow(3).wait()
    load_flow(1).start()
    near(1, 1)
    beyond(1, 0)
    pass_on(1)
    pass_on(2)
    for rank in range(1, size - 1):
        if rank > 1:
            near(1, rank)
        beyond(1, rank)
    keep_flow(0).wait()
    load_flow(2).start()
    descend(1)
    near(2, 0)
    near(2, 1)
    beyond(2, 0)
    for rank in range(1, size - 1):
        if rank > 1:
            near(2, rank)
        beyond(2, rank)
    descend(2)
    squares[...] = jnp.zeros_like(squares)
    saves = []
    for which in range(3):
        for piece in range(pieces):
            add_landed(which, piece, ())
        first, span = groups[which]
        target, offset = (grad_out, 0) if which == 0 else (grad_in, first - tiles_out)
        for place in range(span):
            saves.append(
                pltpu.make_async_copy(
                    arena.at[first + place, pl.ds(kept_first, rows)],
                    target.at[:, pl.ds((offset + place) * tile, tile)],
                    save_sem.at[first + place],
                )
            )
            saves[-1].start()
    for row in range(4):
        late[row : row + 1] = jnp.sum(sums[row], axis=0, keepdims=True)
    late[7:8, 0:HD] = jnp.sum(squares[...], axis=0, keepdims=True)
    final.first()
    final.second()
    final.third()
    final.last()
    early.last()
    for step in range(size):
        for side, way in sides:

            @pl.when(jnp.logical_and(has_next(way), has_origin(way, step)))
            def _():
                line_hop(side, way, step).wait_send()

    for which in range(3):
        for piece, (_, steps) in enumerate(routes):
            for step in steps:
                for bit, _, landed in step:
                    cube_hop(which, piece, bit, landed).wait_send()
    for chain in chains:
        chain.drain()
    keep_flow(1).wait()
    keep_flow(2).wait()
    for copy in saves:
        copy.wait()


def backward(
    d_branch, early_grads, rope, all_in, all_out, slope, heads, chances, joined, all_normed,
    flows, small, size, count, identity,
):
    own = d_branch.shape[0]
    length = own * size
    rows = D // count
    lane_rows = max(rows, HD)
    tile = 512
    head_width, units = heads.shape[2], slope.shape[1]
    width_in, width_out = all_in.shape[1], all_out.shape[1]
    tiles = (width_in + width_out) // tile
    pieces = count.bit_length() - 2
    held = 2**pieces
    bits = pieces + 1
    late_rows = 16
    low = lambda *shape: jax.ShapeDtypeStruct(shape, bfloat)
    wide = lambda *shape: jax.ShapeDtypeStruct(shape, single)
    hbm = pl.BlockSpec(memory_space=pl.ANY)
    vmem = pl.BlockSpec(memory_space=pltpu.VMEM)
    dma = pltpu.SemaphoreType.DMA
    rope = rope.reshape(3, size, own, HD).transpose(2, 0, 1, 3).reshape(own, -1)
    return pl.pallas_call(
        lambda *refs: backward_kernel(size, count, *refs),
        out_shape=[
            low(rows, width_in),
            low(rows, width_out),
            low(STREAMS, own, D),
            wide(*early_grads.shape),
            wide(late_rows, D),
        ],
        in_specs=[hbm, vmem] + [hbm] * 9 + [vmem],
        out_specs=[hbm] * 3 + [vmem] * 2,
        scratch_shapes=[
            pltpu.VMEM((tiles, D, tile), bfloat),
            pltpu.VMEM(((width_out + 3 * head_width) // tile, rows, tile), bfloat),
            pltpu.VMEM((length, width_out), bfloat),
            pltpu.VMEM(heads.shape, bfloat),
            pltpu.VMEM(chances.shape, bfloat),
            pltpu.VMEM((length, D), bfloat),
            pltpu.VMEM((length, units), bfloat),
            pltpu.VMEM((3, length, head_width), bfloat),
            pltpu.VMEM((STREAMS, length, D), bfloat),
            pltpu.VMEM((STREAMS, size + 1, own, D), bfloat),
            pltpu.VMEM((2, own, D), bfloat),
            pltpu.VMEM((own, D), single),
            pltpu.VMEM((4, 8, D), single),
            pltpu.VMEM((lane_rows, tile) if lane_rows > rows else (8, HD), single),
            pltpu.VMEM((late_rows, D), single),
            pltpu.VMEM((8, HD), single),
            dma((tiles,)),
            dma((6,)),
            dma((2,)),
            dma((2,)),
            dma((2,)),
            dma((tiles,)),
            dma((2, size)),
            dma((2, size)),
            dma((STREAMS, 2, size, CUT)),
            dma((STREAMS, 2, size, CUT)),
            dma((3,)),
            dma((3,)),
            pltpu.SemaphoreType.REGULAR((3,)),
            pltpu.SemaphoreType.REGULAR((3, bits)),
            dma((3, pieces, held)),
            dma((3, pieces, held)),
        ]
        + flat_scratch(early_grads.shape[0], count, size)
        + flat_scratch(late_rows, count, size),
        compiler_params=pltpu.CompilerParams(
            collective_id=identity, has_side_effects=True, vmem_limit_bytes=64 * 2**20 - 2**19
        ),
        name="backward_%d" % identity,
    )(
        d_branch, early_grads, jnp.asarray(rope), all_in, all_out, slope, heads, chances, joined,
        all_normed, flows, small,
    )


def finish_kernel(grad_in, grad_out, sums, early_sums, weights, newest_in, d_newest_in, stored, cotangent, d_flows, *refs):
    states, refs = (refs[0:4], refs[4:8]), refs[8:]
    small_in, mix, refs = refs[0:4], refs[4:8], refs[8:]
    norm_out, refs = refs[0], refs[1:]
    new_states, refs = (refs[0:5], refs[5:10]), refs[10:]
    new_small, new_mix, refs = refs[0:4], refs[4:8], refs[8:]
    out_streams, grad_streams, grad_stored, refs = refs[0], refs[1], refs[2], refs[3:]
    held, refs = (refs[0:2], refs[2:4], refs[4:6]), refs[6:]
    tiles_in, tiles_out, spread, passed, small_sums, newest, d_newest, small, refs = (
        *refs[0:8],
        refs[8:],
    )
    row_sem, small_load, small_save, grad_sem, load_sem, save_sem, tile_load, tile_save, pass_sem = refs
    grads = (grad_in, grad_out)
    parts = load_sem.shape[2]
    rows = grad_in.shape[0]
    step_rows = rows // parts

    def load_grad(which):
        return pltpu.make_async_copy(grads[which], held[0][which], grad_sem.at[which])

    def load(which, kind, place):
        spot = pl.ds(place * step_rows, step_rows)
        return pltpu.make_async_copy(
            states[which][kind].at[spot],
            held[1][which].at[kind, spot],
            load_sem.at[which, kind, place],
        )

    def save(which, kind, place):
        spot = pl.ds(place * step_rows, step_rows)
        source = held[1][which].at[kind, spot] if kind < 4 else held[2][which].at[spot]
        return pltpu.make_async_copy(
            source, new_states[which][kind].at[spot], save_sem.at[which, kind, place]
        )

    own = newest_in.shape[0]
    tile_rows = tiles_in.shape[2]
    tile_count = own // tile_rows
    mixes = STREAMS + LAYER

    def tile_copies(index, into):
        spot = pl.ds(index * tile_rows, tile_rows)
        first, second = (cotangent, stored) if into else (out_streams, grad_stored)
        held_tile = (tiles_in if into else tiles_out).at[index % 2]
        sem = (tile_load if into else tile_save).at[index % 2]
        pairs = [
            (first.at[:, spot], held_tile.at[0:STREAMS]),
            (second.at[:, spot], held_tile.at[STREAMS:mixes]),
        ]
        return [
            pltpu.make_async_copy(*(pair if into else pair[::-1]), sem.at[place])
            for place, pair in enumerate(pairs)
        ]

    def compose(index):
        for copy in tile_copies(index, True):
            copy.wait()
        if index > 1:
            for copy in tile_copies(index - 2, False):
                copy.wait()
        spot = pl.ds(index * tile_rows, tile_rows)
        mix_tile = weights[spot]
        slot = index % 2
        for column in range(MIXH):
            spread[column] = jnp.broadcast_to(mix_tile[:, column : column + 1], (tile_rows, HD))

        def columns(place, carry):
            lanes = pl.ds(pl.multiple_of(place * HD, HD), HD)
            value = newest[spot, lanes]
            flows = [tiles_in[slot, stream, :, lanes].astype(single) for stream in range(STREAMS)]
            results = [spread[stream * LAYERS + LAYER] * value for stream in range(STREAMS)]
            for layer in range(LAYER):
                earlier = tiles_in[slot, STREAMS + layer, :, lanes].astype(single)
                gradient = None
                for stream in range(STREAMS):
                    weight = spread[stream * LAYERS + layer]
                    results[stream] = results[stream] + weight * earlier
                    term = weight * flows[stream]
                    gradient = term if gradient is None else gradient + term
                tiles_out[slot, STREAMS + layer, :, lanes] = gradient.astype(bfloat)
            for stream in range(STREAMS):
                tiles_out[slot, stream, :, lanes] = results[stream].astype(bfloat)
            return carry

        lax.fori_loop(0, D // HD, columns, 0)
        for copy in tile_copies(index, False):
            copy.start()
        if index + 2 < tile_count:
            for copy in tile_copies(index + 2, True):
                copy.start()

    load_rows = [
        pltpu.make_async_copy(newest_in, newest, row_sem.at[0]),
        pltpu.make_async_copy(d_newest_in, d_newest, row_sem.at[1]),
    ]
    load_small = [
        pltpu.make_async_copy(small_in[kind], small.at[kind], small_load.at[kind])
        for kind in range(4)
    ]
    save_small = [
        pltpu.make_async_copy(small.at[kind], new_small[kind], small_save.at[kind])
        for kind in range(4)
    ]
    for copy in load_small:
        copy.start()
    for index in range(2):
        for copy in tile_copies(index, True):
            copy.start()
    for copy in load_rows:
        copy.start()
    for which in range(2):
        load_grad(which).start()
        for place in range(parts):
            for kind in range(4):
                load(which, kind, place).start()
    take_flows = pltpu.make_async_copy(d_flows, passed, pass_sem.at[0])
    give_flows = pltpu.make_async_copy(passed, grad_streams, pass_sem.at[1])
    take_flows.start()
    small_sums[0:4] = sums[0:4]
    small_sums[4:5] = early_sums[MIXH : MIXH + 1]
    small_sums[5:8] = sums[4:7]
    small_sums[8:9] = early_sums[MIXH + 1 : MIXH + 2]
    small_sums[9:10] = early_sums[MIXH + 1 : MIXH + 2]
    small_sums[10:SMALL_MIX] = sums[8 : 8 + SMALL_MIX - 10]
    small_sums[SMALL_MIX : SMALL_MIX + MIXH] = early_sums[0:MIXH]
    small_total = small_sums[...]
    mix_total = jnp.concatenate(
        [early_sums[40:48, place * HD : (place + 1) * HD] for place in range(5)], axis=0
    )[0 : mix[0].shape[0], 0 : mix[0].shape[1]]

    def whole_sum(values):
        return jnp.sum(jnp.sum(values, axis=1, keepdims=True), axis=0, keepdims=True)

    norm = jnp.sqrt(
        whole_sum(sums[7:8, 0:HD])
        + whole_sum(small_total * small_total)
        + whole_sum(mix_total * mix_total)
    )
    norm_out[...] = norm
    factor = clip_norm / jnp.maximum(norm, clip_norm)
    for copy in load_small:
        copy.wait()
    results = adamw_step(*(small[kind] for kind in range(4)), small_total, factor, small_rate)
    for kind in range(4):
        small[kind] = results[kind]
        save_small[kind].start()
    for target, result in zip(
        new_mix, adamw_step(*(ref[...] for ref in mix), mix_total, factor, small_rate)
    ):
        target[...] = result
    take_flows.wait()
    for copy in load_rows:
        copy.wait()

    def add_residual(index, carry):
        spot = pl.ds(pl.multiple_of(index * 16, 16), 16)
        passed[3, spot] = (passed[3, spot].astype(single) + d_newest[spot]).astype(bfloat)
        return carry

    lax.fori_loop(0, own // 16, add_residual, 0)
    give_flows.start()
    tiles_done = 0
    for which in range(2):
        columns = held[1][which].shape[2]
        load_grad(which).wait()
        for place in range(parts):
            for kind in range(4):
                load(which, kind, place).wait()

            def update(index, carry):
                spot = pl.ds(pl.multiple_of(place * step_rows + index * 16, 16), 16)

                def column(at, inner):
                    lanes = pl.ds(pl.multiple_of(at * 512, 512), 512)
                    results = adamw_step(
                        *(held[1][which][kind, spot, lanes] for kind in range(4)),
                        held[0][which][spot, lanes].astype(single),
                        factor,
                        learn_rate,
                    )
                    for kind in range(4):
                        held[1][which][kind, spot, lanes] = results[kind]
                    held[2][which][spot, lanes] = results[0].astype(bfloat)
                    return inner

                return lax.fori_loop(0, columns // 512, column, carry, unroll=True)

            lax.fori_loop(0, step_rows // 16, update, 0)
            for kind in range(5):
                save(which, kind, place).start()
            if tiles_done < tile_count:
                compose(tiles_done)
                tiles_done += 1
    while tiles_done < tile_count:
        compose(tiles_done)
        tiles_done += 1
    for index in range(tile_count - 2, tile_count):
        for copy in tile_copies(index, False):
            copy.wait()
    give_flows.wait()
    for copy in save_small:
        copy.wait()
    for which in range(2):
        for place in range(parts):
            for kind in range(5):
                save(which, kind, place).wait()


def finish(
    grads, sums, early_sums, weights, newest, d_newest, stored, cotangent, d_flows, in_states, out_states, small, mix
):
    wide = lambda shape: jax.ShapeDtypeStruct(shape, single)
    low = lambda shape: jax.ShapeDtypeStruct(shape, bfloat)
    hbm = pl.BlockSpec(memory_space=pl.ANY)
    vmem = pl.BlockSpec(memory_space=pltpu.VMEM)
    shapes = [in_states[0].shape, out_states[0].shape]
    parts = 4
    tile = (2, STREAMS + LAYER, 16, D)
    return pl.pallas_call(
        finish_kernel,
        out_shape=[wide((1, 1))]
        + [entry for shape in shapes for entry in [wide(shape)] * 4 + [low(shape)]]
        + [wide(small[0].shape)] * 4
        + [wide(mix[0].shape)] * 4
        + [low(cotangent.shape), low(d_flows.shape), low(stored.shape)],
        in_specs=[hbm] * 2 + [vmem] * 3 + [hbm] * 17 + [vmem] * 4,
        out_specs=[vmem] + [hbm] * 14 + [vmem] * 4 + [hbm] * 3,
        scratch_shapes=[pltpu.VMEM(shape, grads[0].dtype) for shape in shapes]
        + [pltpu.VMEM((4,) + shape, single) for shape in shapes]
        + [pltpu.VMEM(shape, bfloat) for shape in shapes]
        + [pltpu.VMEM(tile, bfloat)] * 2
        + [pltpu.VMEM((MIXH, tile[2], HD), single), pltpu.VMEM(d_flows.shape, bfloat)]
        + [pltpu.VMEM(small[0].shape, single)]
        + [pltpu.VMEM(newest.shape, single)] * 2
        + [pltpu.VMEM((4,) + small[0].shape, single)]
        + [pltpu.SemaphoreType.DMA((n,)) for n in (2, 4, 4)]
        + [
            pltpu.SemaphoreType.DMA((2,)),
            pltpu.SemaphoreType.DMA((2, 4, parts)),
            pltpu.SemaphoreType.DMA((2, 5, parts)),
            pltpu.SemaphoreType.DMA((2, 2)),
            pltpu.SemaphoreType.DMA((2, 2)),
            pltpu.SemaphoreType.DMA((2,)),
        ],
        compiler_params=pltpu.CompilerParams(vmem_limit_bytes=60 * 2**20),
        name="finish",
    )(
        *grads, sums, early_sums, weights, newest, d_newest, stored, cotangent, d_flows,
        *in_states, *out_states, *small, *mix,
    )


def shards(
    in_streams,
    stored,
    cotangent,
    in_weights,
    in_moment,
    in_second,
    in_average,
    out_weights,
    out_moment,
    output_second_moment,
    out_average,
    small_params,
    small_moment,
    small_second,
    small_average,
    mix_weights,
    mix_moment,
    mix_second,
    mix_average,
):
    groups, count = lax.axis_size("tensor"), lax.axis_size("dp")
    rope = rope_lanes(in_streams.shape[1] * groups)
    (
        full_in,
        full_out,
        normed,
        joined,
        slope,
        heads,
        chances,
        newest,
        d_newest,
        d_branch,
        weights,
        early_grads,
    ) = forward(
        in_streams,
        in_weights,
        out_weights,
        small_params,
        rope,
        stored,
        cotangent,
        mix_weights,
        groups,
        count,
        0,
    )
    grad_in, grad_out, d_flows, early_sums, sums = backward(
        d_branch,
        early_grads,
        rope,
        full_in,
        full_out,
        slope,
        heads,
        chances,
        joined,
        normed,
        in_streams,
        small_params,
        groups,
        count,
        1,
    )
    results = finish(
        (grad_in, grad_out),
        sums,
        early_sums,
        weights,
        newest,
        d_newest,
        stored,
        cotangent,
        d_flows,
        (in_weights, in_moment, in_second, in_average),
        (out_weights, out_moment, output_second_moment, out_average),
        (small_params, small_moment, small_second, small_average),
        (mix_weights, mix_moment, mix_second, mix_average),
    )
    out_streams, grad_streams, grad_stored = results[-3:]
    return (out_streams, grad_streams, grad_stored, results[0][0, 0], *results[1:-3])


def solution(mesh):
    in_specs = (
        P(None, ("dp", "tensor"), None),
        P(None, ("dp", "tensor"), None),
        P(None, ("dp", "tensor"), None),
        P("dp", "tensor"),
        P("dp", "tensor"),
        P("dp", "tensor"),
        P("dp", "tensor"),
        P("dp", "tensor"),
        P("dp", "tensor"),
        P("dp", "tensor"),
        P("dp", "tensor"),
        P(),
        P(),
        P(),
        P(),
        P(),
        P(),
        P(),
        P(),
    )
    out_specs = (
        P(None, ("dp", "tensor"), None),
        P(None, ("dp", "tensor"), None),
        P(None, ("dp", "tensor"), None),
        P(),
        P("dp", "tensor"),
        P("dp", "tensor"),
        P("dp", "tensor"),
        P("dp", "tensor"),
        P("dp", "tensor"),
        P("dp", "tensor"),
        P("dp", "tensor"),
        P("dp", "tensor"),
        P("dp", "tensor"),
        P("dp", "tensor"),
        P(),
        P(),
        P(),
        P(),
        P(),
        P(),
        P(),
        P(),
    )
    return jax.shard_map(shards, mesh=mesh, in_specs=in_specs, out_specs=out_specs, check_vma=False)
```

```python
import jax
import jax.numpy as jnp
import numpy as np
from jax import lax
from jax.experimental import pallas as pl
from jax.experimental.pallas import tpu as pltpu
from jax.sharding import PartitionSpec as P

D = 2048
HEADS = 16
HD = 128
ROT = 32
FF = 8192
STREAMS = 4
LAYER = 8
STEP = 10
LAYERS = 9
MIXH = 36


norm_eps = 1e-05
mix_eps = 1e-06
beta_first = 0.9
beta_second = 0.95
adam_eps = 1e-08
decay_rate = 0.01
learn_rate = 0.03
small_rate = 0.2
clip_norm = 1.0
average_keep = 0.5
masked_score = -1e30
highest_precision = lax.Precision.HIGHEST
bfloat = jnp.bfloat16
single = jnp.float32
MESH = pl.DeviceIdType.MESH


def contract_last(left_side, right_side):
    return lax.dot_general(
        left_side,
        right_side,
        (((left_side.ndim - 1,), (right_side.ndim - 1,)), ((), ())),
        preferred_element_type=single,
    )


def contract_first(left_side, right_side):
    return lax.dot_general(
        left_side, right_side, (((0,), (0,)), ((), ())), preferred_element_type=single
    )


def adamw_step(weight, moment, second, average, gradient, factor, rate):
    clipped = gradient * factor
    moment = beta_first * moment + (1.0 - beta_first) * clipped
    second = beta_second * second + (1.0 - beta_second) * clipped * clipped
    step_ratio = (moment * (1.0 / (1.0 - beta_first**STEP))) / (
        jnp.sqrt(second * (1.0 / (1.0 - beta_second**STEP))) + adam_eps
    )
    weight = weight - rate * (step_ratio + decay_rate * weight)
    average = average_keep * average + (1.0 - average_keep) * weight
    return (weight, moment, second, average)


def enter(partners):
    barrier = pltpu.get_barrier_semaphore()
    for present, device in partners:

        @pl.when(present)
        def _():
            pl.semaphore_signal(barrier, inc=1, device_id=device, device_id_type=MESH)

    pl.semaphore_wait(barrier, sum(present.astype(jnp.int32) for present, _ in partners))


class LineSum:
    def __init__(self, size, give, landing, send_sem, recv_sem, cut):
        self.size, self.give, self.landing = size, give, landing
        self.send_sem, self.recv_sem, self.cut = send_sem, recv_sem, cut
        self.here = lax.axis_index("tensor")
        self.own = landing.shape[1]
        self.rows = self.own // cut
        self.near = lax.select(2 * self.here < size, 1, -1)

    def has_next(self, way):
        return jnp.logical_and(self.here + way >= 0, self.here + way < self.size)

    def spot(self, dest, place):
        return pl.ds(pl.multiple_of(dest * self.own + place * self.rows, 16), self.rows)

    def landed(self, way, dest, place):
        rows = pl.ds(pl.multiple_of(place * self.rows, 16), self.rows)
        return self.landing.at[dest + (1 + way) // 2, rows]

    def hop(self, way, dest, place):
        return pltpu.make_async_remote_copy(
            src_ref=self.give.at[self.spot(dest, place)],
            dst_ref=self.landed(way, dest, place),
            send_sem=self.send_sem.at[(1 - way) // 2, dest, place],
            recv_sem=self.recv_sem.at[(1 - way) // 2, dest, place],
            device_id={"tensor": self.here + way},
            device_id_type=MESH,
        )

    def arrive(self, way, dest, place):
        block = self.landed(way, dest, place)
        pltpu.make_async_remote_copy(
            src_ref=block,
            dst_ref=block,
            send_sem=self.send_sem.at[(1 - way) // 2, dest, place],
            recv_sem=self.recv_sem.at[(1 - way) // 2, dest, place],
            device_id={"tensor": self.here - way},
            device_id_type=MESH,
        ).wait_recv()

    def relay(self, way, dest, first=0, many=None):
        @pl.when((dest - self.here) * way > 0)
        def _():
            def one(place, carry):
                @pl.when(self.has_next(-way))
                def _():
                    self.arrive(way, dest, place)
                    spot = self.spot(dest, place)
                    self.give[spot] = (
                        self.give[spot].astype(single)
                        + self.landed(way, dest, place)[...].astype(single)
                    ).astype(bfloat)

                self.hop(way, dest, place).start()
                return carry

            lax.fori_loop(first, first + (many or self.cut), one, 0)

    def far(self, rank, way):
        return (self.size - 1) * ((1 + way) // 2) - rank * way

    def collect(self, place, into):
        rows = pl.ds(place * self.rows, self.rows)
        into[rows] = self.give[self.spot(self.here, place)].astype(single)
        for way in (1, -1):

            @pl.when(self.has_next(-way))
            def _():
                self.arrive(way, self.here, place)
                into[rows] += self.landed(way, self.here, place)[...].astype(single)

    def drain(self):
        for rank in range(self.size - 1):
            for way in (1, -1):
                dest = self.far(rank, way)

                @pl.when((dest - self.here) * way > 0)
                def _():
                    for place in range(self.cut):
                        self.hop(way, dest, place).wait_send()


class FlatSum:
    def __init__(self, count, size, value, out, landing, crossing, sems):
        self.count, self.size, self.value, self.out = count, size, value, out
        self.landing, self.crossing = landing, crossing
        self.send_a, self.recv_a, self.send_b, self.recv_b, self.send_c, self.recv_c = sems
        self.me = lax.axis_index("dp")
        self.here = lax.axis_index("tensor")
        self.across = min(count, D // HD)
        self.rows, self.lanes = landing.shape[1:]

    def part(self, ref, owner):
        row = pl.multiple_of(owner // self.across * self.rows, 8)
        lane = pl.multiple_of(lax.rem(owner, self.across) * self.lanes, HD)
        return ref.at[pl.ds(row, self.rows), pl.ds(lane, self.lanes)]

    def over(self, first, action):
        total, place = (self.count, self.me) if first else (self.size, self.here)

        def one(step, carry):
            action(lax.rem(place + step, total))
            return carry

        lax.fori_loop(1, total, one, 0)

    def to_owner(self, other):
        return pltpu.make_async_remote_copy(
            src_ref=self.part(self.value, other),
            dst_ref=self.landing.at[self.me],
            send_sem=self.send_a.at[other],
            recv_sem=self.recv_a.at[self.me],
            device_id={"dp": other},
            device_id_type=MESH,
        )

    def across_to(self, other):
        return pltpu.make_async_remote_copy(
            src_ref=self.crossing.at[self.here],
            dst_ref=self.crossing.at[self.here],
            send_sem=self.send_b.at[other],
            recv_sem=self.recv_b.at[self.here],
            device_id={"tensor": other},
            device_id_type=MESH,
        )

    def back_to(self, other):
        return pltpu.make_async_remote_copy(
            src_ref=self.part(self.out, self.me),
            dst_ref=self.part(self.out, self.me),
            send_sem=self.send_c.at[other],
            recv_sem=self.recv_c.at[self.me],
            device_id={"dp": other},
            device_id_type=MESH,
        )

    def arrive(self, block, send, recv, other, axis):
        pltpu.make_async_remote_copy(
            src_ref=block,
            dst_ref=block,
            send_sem=send.at[other],
            recv_sem=recv.at[other],
            device_id={axis: other},
            device_id_type=MESH,
        ).wait_recv()

    def first(self):
        self.over(True, lambda other: self.to_owner(other).start())

    def second(self, extra=None):
        self.crossing[self.here] = self.part(self.value, self.me)[...]

        def add(other):
            self.arrive(self.landing.at[other], self.send_a, self.recv_a, other, "dp")
            self.crossing[self.here] += self.landing[other]

        self.over(True, add)
        if extra is not None:
            self.crossing[self.here, 7:8, 0:HD] += extra
        self.over(False, lambda other: self.across_to(other).start())

    def third(self):
        self.over(
            False,
            lambda other: self.arrive(
                self.crossing.at[other], self.send_b, self.recv_b, other, "tensor"
            ),
        )
        result = self.crossing[0]
        for other in range(1, self.size):
            result = result + self.crossing[other]
        self.part(self.out, self.me)[...] = result
        self.over(True, lambda other: self.back_to(other).start())

    def last(self):
        self.over(
            True,
            lambda other: self.arrive(
                self.part(self.out, other), self.send_c, self.recv_c, other, "dp"
            ),
        )
        self.over(True, lambda other: self.to_owner(other).wait_send())
        self.over(False, lambda other: self.across_to(other).wait_send())
        self.over(True, lambda other: self.back_to(other).wait_send())

    def partners(self):
        def others(place, total):
            return [lax.rem(place + step, total) for step in range(1, total)]

        return [{"dp": other} for other in others(self.me, self.count)] + [
            {"tensor": other} for other in others(self.here, self.size)
        ]


def flat_scratch(rows, count, size):
    across = min(count, D // HD)
    part = (rows * across // count, D // across)
    return [
        pltpu.VMEM((count,) + part, single),
        pltpu.VMEM((size,) + part, single),
    ] + [pltpu.SemaphoreType.DMA((n,)) for n in (count, count, size, size, count, count)]


def plus_flips(place, bits):
    moved = place
    for bit in bits:
        moved = moved + (1 - 2 * lax.rem(place // 2**bit, 2)) * 2**bit
    return moved


def cube_routes(count):
    bits = list(range(1, count))
    pieces = []
    for turn in range(len(bits)):
        order = bits[turn:] + bits[:turn]
        arrivals = [()]
        steps = []
        for bit in order:
            fresh = [tuple(sorted(held + (bit,))) for held in arrivals]
            steps.append([(bit, held, whole) for held, whole in zip(arrivals, fresh)])
            arrivals = arrivals + fresh
        pieces.append((arrivals, steps))
    return pieces


class CubeGather:
    def __init__(self, whole, rows, count, sems):
        self.whole, self.rows, self.count = whole, rows, count
        self.send_sem, self.recv_sem, self.pair_send, self.pair_recv = sems
        self.routes = cube_routes(count.bit_length() - 1)
        self.me = lax.axis_index("dp")
        self.piece_rows = rows // len(self.routes)

    def region(self, piece, held):
        first = plus_flips(self.me, held) * self.rows + piece * self.piece_rows
        return self.whole.at[pl.ds(pl.multiple_of(first, 16), self.piece_rows)]

    def hop(self, piece, bit, held, slot, pair=False):
        block = self.region(piece, held)
        return pltpu.make_async_remote_copy(
            src_ref=block,
            dst_ref=block,
            send_sem=(self.pair_send if pair else self.send_sem).at[piece, slot],
            recv_sem=(self.pair_recv if pair else self.recv_sem).at[piece, slot],
            device_id={"dp": plus_flips(self.me, (bit,))},
            device_id_type=MESH,
        )

    def slot(self, piece, held):
        return self.routes[piece][0].index(held)

    def sends_of(self, piece, held):
        found = []
        for step in self.routes[piece][1]:
            for bit, source, landed in step:
                if source == held:
                    found.append(self.hop(piece, bit, held, self.slot(piece, landed)))
        found.append(self.hop(piece, 0, held, self.slot(piece, held), True))
        return found

    def start(self):
        for copies in zip(*(self.sends_of(piece, ()) for piece in range(len(self.routes)))):
            for copy in copies:
                copy.start()

    def step(self, index, which=lambda held: True):
        for piece, (_, steps) in enumerate(self.routes):
            for bit, _, landed in steps[index]:
                if not which(landed):
                    continue
                self.hop(piece, bit, landed, self.slot(piece, landed)).wait_recv()
                for copy in self.sends_of(piece, landed):
                    copy.start()

    def steps(self):
        return len(self.routes)

    def finish(self, which=lambda held: True):
        for piece, (arrivals, _) in enumerate(self.routes):
            for held in filter(which, arrivals):
                self.hop(piece, 0, (0,) + held, self.slot(piece, held), True).wait_recv()

    def drain(self):
        for piece, (arrivals, _) in enumerate(self.routes):
            for held in arrivals:
                for copy in self.sends_of(piece, held):
                    copy.wait_send()


FLOW_ORDER = (3, 1, 2, 0)
CUT = 4
SMALL_MIX = 10 + FF // D


def rope_lanes(length):
    half = ROT // 2
    inverse = 10000.0 ** (-2.0 * np.arange(half) / ROT)
    angles = np.arange(length)[:, None] * inverse[None, :]
    tables = np.zeros((3, length, HD), np.float32)
    tables[0] = 1.0
    tables[0, :, :half] = tables[0, :, half:ROT] = np.cos(angles)
    tables[1, :, :half] = -np.sin(angles)
    tables[2, :, half:ROT] = np.sin(angles)
    return tables


def forward_kernel(
    size,
    count,
    flows,
    w_in,
    w_out,
    small,
    rope,
    stored,
    cotangent,
    mix,
    all_in,
    all_out,
    all_normed,
    joined_out,
    slope_out,
    heads_out,
    chances_out,
    newest,
    d_newest,
    d_branch,
    weights,
    early_grads,
    w_in_low,
    w_out_low,
    normed,
    heads,
    chances,
    joined,
    slope,
    total,
    give,
    terms,
    back,
    earlier,
    dots,
    scales,
    sums,
    mix_low,
    mix_table,
    stage_sem,
    back_sem,
    earlier_sem,
    line_send,
    line_recv,
    term_send,
    term_recv,
    save_sem,
    flow_sem,
    *cube_sems,
):
    here = lax.axis_index("tensor")
    me = lax.axis_index("dp")
    own = flows.shape[1]
    rows_in = w_in.shape[0]
    length = own * size
    width_in, width_out = w_in.shape[1], w_out.shape[1]
    head_width = heads.shape[2]
    group_heads = head_width // HD
    attn_width = 3 * head_width
    units = width_in - attn_width
    bits = count.bit_length() - 1
    sides = ((0, 1), (1, -1))
    tile = 512

    def rows_of(block):
        return pl.ds(pl.multiple_of(block * own, own), own)

    def stage(source, width):
        spans = [(0, min(width, D))] + ([(D, width - D)] if width > D else [])
        return [
            pltpu.make_async_copy(
                source.at[:, pl.ds(first, span)],
                total.at[pl.ds(place * rows_in, rows_in), pl.ds(0, span)],
                stage_sem.at[place],
            )
            for place, (first, span) in enumerate(spans)
        ]

    def settle(source, width, target):
        for place, copy in enumerate(stage(source, width)):
            copy.wait()
            span = min(D, width - place * D)

            def cast(index, carry):
                low = pl.multiple_of(index * 16, 16)
                into = pl.multiple_of(me * rows_in + index * 16, 16)
                target[pl.ds(into, 16), pl.ds(place * D, span)] = total[
                    pl.ds(place * rows_in + low, 16), pl.ds(0, span)
                ].astype(bfloat)
                return carry

            lax.fori_loop(0, rows_in // 16, cast, 0)

    for copy in stage(w_in, width_in):
        copy.start()
    load_back = pltpu.make_async_copy(cotangent, back, back_sem)
    load_back.start()

    def load_earlier(layer):
        return pltpu.make_async_copy(
            stored.at[layer], earlier.at[layer % 2], earlier_sem.at[layer % 2]
        )

    load_earlier(0).start()
    enter(
        [(here < size - 1, {"tensor": here + 1}), (here > 0, {"tensor": here - 1})]
        + [(jnp.bool_(True), {"dp": plus_flips(me, (bit,))}) for bit in range(bits)]
    )

    def line_rows(block, half):
        if half is None:
            return rows_of(block)
        return pl.ds(pl.multiple_of(block * own + half * (own // 2), 16), own // 2)

    def line_hop(side, way, step, flow, half=None):
        block = normed.at[flow, line_rows(here - way * step, half)]
        return pltpu.make_async_remote_copy(
            src_ref=block,
            dst_ref=block,
            send_sem=line_send.at[side, step, flow if half is None else half * STREAMS],
            recv_sem=line_recv.at[side, step, flow if half is None else half * STREAMS],
            device_id={"tensor": here + way},
            device_id_type=MESH,
        )

    def line_landed(side, way, step, flow, half=None):
        block = normed.at[flow, line_rows(here - way * step, half)]
        return pltpu.make_async_remote_copy(
            src_ref=block,
            dst_ref=block,
            send_sem=line_send.at[side, step - 1, flow if half is None else half * STREAMS],
            recv_sem=line_recv.at[side, step - 1, flow if half is None else half * STREAMS],
            device_id={"tensor": here - way},
            device_id_type=MESH,
        )

    def has_next(way):
        return here < size - 1 if way > 0 else here > 0

    def has_origin(way, step):
        return here >= step if way > 0 else here < size - step

    def keep_flow(flow, block):
        return pltpu.make_async_copy(
            normed.at[flow, rows_of(block)],
            all_normed.at[flow, rows_of(block)],
            flow_sem.at[flow, block],
        )

    def send_normal(flow):
        which = 2 if flow == 3 else 0

        def normalize(index, carry):
            spot = pl.ds(pl.multiple_of(index * 16, 16), 16)
            values = flows[flow, spot].astype(single)
            centred = values - jnp.mean(values, axis=-1, keepdims=True)
            inverse = lax.rsqrt(jnp.mean(centred * centred, axis=-1, keepdims=True) + norm_eps)
            into = pl.ds(pl.multiple_of(here * own + index * 16, 16), 16)
            normed[flow, into] = (
                centred * inverse * small[which : which + 1, :] + small[which + 1 : which + 2, :]
            ).astype(bfloat)
            return carry

        lax.fori_loop(0, own // 16, normalize, 0)
        if flow:
            for side, way in sides:
                pl.when(has_next(way))(line_hop(side, way, 0, flow).start)
        keep_flow(flow, here).start()

    cube_in = CubeGather(w_in_low, rows_in, count, cube_sems[:4])
    cube_out = CubeGather(w_out_low, rows_in, count, cube_sems[4:])
    send_normal(FLOW_ORDER[0])
    settle(w_in, width_in, w_in_low)
    cube_in.start()
    for copy in stage(w_out, width_out):
        copy.start()
    for flow in FLOW_ORDER[1:]:
        send_normal(flow)
    settle(w_out, width_out, w_out_low)
    mix_low[...] = jnp.zeros_like(mix_low)
    mix_low[0:MIXH] = small[SMALL_MIX : SMALL_MIX + MIXH].astype(bfloat)
    mix_table[...] = jnp.zeros_like(mix_table)
    mix_table[0:MIXH, 0:MIXH] = mix[0:MIXH]
    mix_table[HD : HD + 1, 0:MIXH] = mix[MIXH : MIXH + 1]
    lane = lax.broadcasted_iota(jnp.int32, (16, HD), 1)
    load_back.wait()
    for layer in range(LAYER):
        if layer + 1 < LAYER:
            load_earlier(layer + 1).start()
        load_earlier(layer).wait()

        def correlate(index, carry):
            spot = pl.ds(pl.multiple_of(index * 16, 16), 16)
            held = earlier[layer % 2, spot].astype(single)
            found = jnp.zeros((16, HD), single) if layer == 0 else dots[spot]
            for stream in range(STREAMS):
                value = jnp.sum(back[stream, spot].astype(single) * held, axis=-1, keepdims=True)
                found = found + jnp.where(lane == stream * LAYERS + layer, value, 0.0)
            dots[spot] = found
            return carry

        lax.fori_loop(0, own // 16, correlate, 0)

    def line_step(step, flow_list):
        for flow in flow_list:
            for side, way in sides:

                @pl.when(has_origin(way, step))
                def _():
                    line_landed(side, way, step, flow).wait_recv()
                    pl.when(has_next(way))(line_hop(side, way, step, flow).start)
                    keep_flow(flow, here - way * step).start()

    def at_distance(step, action):
        if step == 0:
            action(here)
            return

        def one(side, carry):
            block = here - step + 2 * step * side

            @pl.when(jnp.logical_and(block >= 0, block < size))
            def _():
                action(block)

            return carry

        lax.fori_loop(0, 2, one, 0)

    def project(block, part, half=None):
        rows = line_rows(block, half)
        source = normed[part, rows]
        pre = jnp.dot(
            source,
            jnp.concatenate(
                [
                    w_in_low[:, pl.ds((head * 3 + part) * HD, HD)]
                    for head in range(group_heads)
                ],
                axis=1,
            ),
            preferred_element_type=single,
        )
        first = pl.multiple_of(here * head_width, HD)
        pre = pre + small[5 + part : 6 + part, pl.ds(first, head_width)]
        if part == 2:
            heads[part, rows] = pre.astype(bfloat)
            return
        cosine, sine_low, sine_high = rope[0, rows], rope[1, rows], rope[2, rows]
        for head in range(group_heads):
            values = pre[:, head * HD : (head + 1) * HD]
            turned = (
                values * cosine
                + pltpu.roll(values, HD - ROT // 2, 1) * sine_low
                + pltpu.roll(values, ROT // 2, 1) * sine_high
            )
            heads[part, rows, pl.ds(head * HD, HD)] = turned.astype(bfloat)

    def expand(block):
        rows = rows_of(block)

        def one(index, carry):
            first = pl.multiple_of(index * tile, tile)
            pre = jnp.dot(
                normed[3, rows],
                w_in_low[:, pl.ds(attn_width + first, tile)],
                preferred_element_type=single,
            )
            pre = pre + small[pl.ds(10 + here, 1), pl.ds(first, tile)]
            normal = 0.5 * (1.0 + lax.erf(pre * 0.7071067811865476))
            joined[rows, pl.ds(head_width + first, tile)] = (pre * normal).astype(bfloat)
            slope[rows, pl.ds(first, tile)] = (
                normal + pre * jnp.exp(-0.5 * pre * pre) * 0.3989422804014327
            ).astype(bfloat)
            return carry

        lax.fori_loop(0, units // tile, one, 0)

    def contract(which):
        if rows_in % HD:
            return
        for held in filter(which, cube_out.routes[0][0]):
            for pair in ((), (0,)):
                first = pl.multiple_of(plus_flips(me, pair + held) * rows_in, HD)
                total[:, pl.ds(first, rows_in)] = contract_last(
                    joined[:, pl.ds(head_width, units)],
                    w_out_low[pl.ds(first, rows_in), pl.ds(head_width, units)],
                )

    def contract_whole():
        def one(index, carry):
            first = pl.multiple_of(index * tile, tile)
            total[:, pl.ds(first, tile)] = contract_last(
                joined[:, pl.ds(head_width, units)],
                w_out_low[pl.ds(first, tile), pl.ds(head_width, units)],
            )
            return carry

        lax.fori_loop(0, D // tile, one, 0)

    def direct(held):
        return len(held) <= 1

    def indirect(held):
        return len(held) > 1

    def attend(block, half=None):
        rows = line_rows(block, half)
        shape = (rows.size, length)
        places = rows.start + lax.broadcasted_iota(jnp.int32, shape, 0)
        allowed = lax.broadcasted_iota(jnp.int32, shape, 1) <= places
        for head in range(group_heads):
            lanes = pl.ds(head * HD, HD)
            scores = contract_last(heads[0, rows, lanes], heads[1, :, lanes]) * HD ** (-0.5)
            scores = jnp.where(allowed, scores, masked_score)
            raised = jnp.exp(scores - jnp.max(scores, axis=-1, keepdims=True))
            low = (raised / jnp.sum(raised, axis=-1, keepdims=True)).astype(bfloat)
            chances[head, rows] = low
            joined[rows, lanes] = jnp.dot(
                low, heads[2, :, lanes], preferred_element_type=single
            ).astype(bfloat)

    def emit(block, half=None):
        rows = line_rows(block, half)

        def one(index, carry):
            first = pl.multiple_of(index * tile, tile)
            spot = (rows, pl.ds(first, tile))
            give[spot] = (
                total[spot]
                + contract_last(
                    joined[rows, pl.ds(0, head_width)],
                    w_out_low[pl.ds(first, tile), pl.ds(0, head_width)],
                )
            ).astype(bfloat)
            return carry

        lax.fori_loop(0, D // tile, one, 0)

    def save(place, source, target):
        return pltpu.make_async_copy(source, target, save_sem.at[place])

    chain = LineSum(size, give, terms, term_send, term_recv, CUT)
    ending = jnp.logical_or(here == 0, here == size - 1)

    def query_pass(side, way, step):
        @pl.when(has_origin(way, step))
        def _():
            for half in range(2):
                line_landed(side, way, step, 0, half).wait_recv()
                pl.when(has_next(way))(line_hop(side, way, step, 0, half).start)
            keep_flow(0, here - way * step).start()

    def query_side(side, way):
        for step in range(size - 1, 0, -1):
            query_pass(side, way, step)
        for half in range(2):
            pl.when(has_next(way))(line_hop(side, way, 0, 0, half).start)

    cube_in.step(0)
    cube_out.start()
    line_step(1, FLOW_ORDER[:3])
    lower = 2 * here < size
    pl.when(lower)(lambda: query_side(0, 1))
    pl.when(jnp.logical_not(lower))(lambda: query_side(1, -1))
    line_step(2, FLOW_ORDER[:1])
    for index in range(1, cube_in.steps()):
        cube_in.step(index)
    line_step(2, FLOW_ORDER[1:3])
    cube_in.finish()
    save(0, w_in_low, all_in).start()

    def early(block):
        project(block, 1)
        project(block, 2)
        expand(block)

    at_distance(0, early)
    at_distance(1, early)
    cube_out.step(0)
    at_distance(2, early)
    project(here, 0)

    @pl.when(jnp.logical_not(ending))
    def _():
        pl.when(lower)(lambda: query_side(1, -1))
        pl.when(jnp.logical_not(lower))(lambda: query_side(0, 1))

        def one(index, carry):
            project(lax.rem(here + 1 + index, size), 0)
            return carry

        lax.fori_loop(0, size - 1, one, 0)

        def two(block, carry):
            attend(block)
            return carry

        lax.fori_loop(0, size, two, 0)

    for step in range(3, size):
        line_step(step, FLOW_ORDER[:1])
        at_distance(step, expand)
    for index in range(1, cube_out.steps()):
        cube_out.step(index, direct)
    cube_out.finish(direct)
    contract(direct)

    def keys_values(block):
        project(block, 1)
        project(block, 2)

    for step in range(3, size):
        line_step(step, FLOW_ORDER[1:3])
        at_distance(step, keys_values)
    pl.when(ending)(lambda: attend(here))
    for index in range(1, cube_out.steps()):
        cube_out.step(index, indirect)
    cube_out.finish(indirect)
    save(1, w_out_low, all_out).start()
    if rows_in % HD:
        contract_whole()
    else:
        contract(indirect)

    @pl.when(jnp.logical_not(ending))
    def _():
        def one(index, carry):
            emit(lax.rem(here + 1 + index, size))
            return carry

        lax.fori_loop(0, size - 1, one, 0)

    for rank in range(size - 1):
        step = size - 1 - rank

        @pl.when(ending)
        def _():
            dest = lax.select(here == 0, size - 1 - rank, rank)
            side = lax.select(here == 0, 1, 0)

            def one(half, carry):
                block = normed.at[0, line_rows(dest, half)]
                pltpu.make_async_remote_copy(
                    src_ref=block,
                    dst_ref=block,
                    send_sem=line_send.at[side, step - 1, half * STREAMS],
                    recv_sem=line_recv.at[side, step - 1, half * STREAMS],
                    device_id={"tensor": lax.select(here == 0, 1, size - 2)},
                    device_id_type=MESH,
                ).wait_recv()
                project(dest, 0, half)
                attend(dest, half)
                emit(dest, half)
                chain.relay(chain.near, dest, half * (CUT // 2), CUT // 2)
                return carry

            lax.fori_loop(0, 2, one, 0)
            keep_flow(0, dest).start()

        @pl.when(jnp.logical_not(ending))
        def _():
            for way in (chain.near, -chain.near):
                chain.relay(way, chain.far(rank, way))

    emit(here)
    saves = [
        save(2, joined, joined_out),
        save(3, slope, slope_out),
        save(4, heads, heads_out),
        save(5, chances, chances_out),
    ]
    for copy in saves:
        copy.start()
    for place in range(CUT):
        chain.collect(place, newest)

    def sixteen(index):
        spot = pl.ds(pl.multiple_of(index * 16, 16), 16)
        return spot, pl.ds(pl.multiple_of(here * own + index * 16, 16), 16)

    def compose(index, carry):
        spot, inner = sixteen(index)
        value = flows[3, spot].astype(single) + newest[spot] + small[8:9, :] + small[9:10, :]
        newest[spot] = value
        inverse = lax.rsqrt(jnp.mean(value * value, axis=-1, keepdims=True) + mix_eps)
        scales[spot] = jnp.broadcast_to(inverse, (16, HD))
        give[inner] = (value * inverse * small[4:5, :]).astype(bfloat)
        found = dots[spot]
        for stream in range(STREAMS):
            dot = jnp.sum(back[stream, spot].astype(single) * value, axis=-1, keepdims=True)
            found = found + jnp.where(lane == stream * LAYERS + LAYER, dot, 0.0)
        dots[spot] = found
        return carry

    lax.fori_loop(0, own // 16, compose, 0)
    mix_normed = give[rows_of(here)]
    mix_pre = contract_last(mix_normed, mix_low[...])
    normal = 0.5 * (1.0 + lax.erf(mix_pre * 0.7071067811865476))
    act = mix_pre * normal
    act_slope = normal + mix_pre * jnp.exp(-0.5 * mix_pre * mix_pre) * 0.3989422804014327
    table = mix_table[0:HD]
    weights[...] = (
        jnp.dot(act, table, precision=highest_precision, preferred_element_type=single)
        + mix_table[HD : HD + 1]
    )
    d_mixing = dots[...]
    d_act = lax.dot_general(
        d_mixing,
        table,
        (((1,), (1,)), ((), ())),
        precision=highest_precision,
        preferred_element_type=single,
    )
    d_mix_pre = (d_act * act_slope).astype(bfloat)
    out_grad = lax.dot_general(
        act,
        d_mixing,
        (((0,), (0,)), ((), ())),
        precision=highest_precision,
        preferred_element_type=single,
    )
    scales_sum = jnp.sum(d_mixing, axis=0, keepdims=True)
    early_grads[MIXH:] = jnp.zeros((early_grads.shape[0] - MIXH, D), single)
    for place in range((MIXH + 7) // 8):
        rows_left = min(8, MIXH - place * 8)
        early_grads[40 : 40 + rows_left, place * HD : (place + 1) * HD] = out_grad[
            place * 8 : place * 8 + rows_left
        ]
    early_grads[40 + MIXH % 8 : 41 + MIXH % 8, MIXH // 8 * HD : MIXH // 8 * HD + HD] = scales_sum

    def spread(index, carry):
        lanes = pl.ds(pl.multiple_of(index * tile, tile), tile)
        total[0:own, lanes] = jnp.dot(
            d_mix_pre, mix_low[:, lanes], preferred_element_type=single
        )
        early_grads[0:MIXH, lanes] = contract_first(d_mix_pre, give[rows_of(here), lanes])[0:MIXH]
        return carry

    lax.fori_loop(0, D // tile, spread, 0)
    sums[...] = jnp.zeros_like(sums)

    def descend(index, carry):
        spot, inner = sixteen(index)
        value, inverse = newest[spot], scales[spot][:, 0:1]
        d_normed = total[spot]
        scaled = d_normed * small[4:5, :]
        middle = jnp.mean(scaled * value, axis=-1, keepdims=True)
        result = inverse * scaled - value * (inverse * inverse * inverse * middle)
        for stream in range(STREAMS):
            column = stream * LAYERS + LAYER
            result = result + weights[spot][:, column : column + 1] * back[stream, spot].astype(
                single
            )
        d_newest[spot] = result
        d_branch[spot] = result.astype(bfloat)
        gain = d_normed * value * inverse
        sums[0] += gain[0:8] + gain[8:16]
        sums[1] += result[0:8] + result[8:16]
        return carry

    lax.fori_loop(0, own // 16, descend, 0)
    early_grads[MIXH : MIXH + 1] = jnp.sum(sums[0], axis=0, keepdims=True)
    early_grads[MIXH + 1 : MIXH + 2] = jnp.sum(sums[1], axis=0, keepdims=True)
    for step in range(size):
        for flow in FLOW_ORDER:
            for side, way in sides:

                @pl.when(jnp.logical_and(has_next(way), has_origin(way, step)))
                def _():
                    for half in range(2) if flow == 0 else [None]:
                        line_hop(side, way, step, flow, half).wait_send()

    cube_in.drain()
    cube_out.drain()
    chain.drain()
    for flow in FLOW_ORDER:
        for block in range(size):
            keep_flow(flow, block).wait()
    save(0, w_in_low, all_in).wait()
    save(1, w_out_low, all_out).wait()
    for copy in saves:
        copy.wait()


def forward(flows, w_in, w_out, small, rope, stored, cotangent, mix_weights, size, count, identity):
    own = flows.shape[1]
    length = own * size
    rows, width_in = w_in.shape
    width_out = w_out.shape[1]
    head_width = HEADS // size * HD
    units = FF // size
    pieces = count.bit_length() - 2
    cube = [pltpu.SemaphoreType.DMA((pieces, 2**pieces))] * 8
    low = lambda *shape: jax.ShapeDtypeStruct(shape, bfloat)
    hbm = pl.BlockSpec(memory_space=pl.ANY)
    vmem = pl.BlockSpec(memory_space=pltpu.VMEM)
    return pl.pallas_call(
        lambda *refs: forward_kernel(size, count, *refs),
        out_shape=[
            low(D, width_in),
            low(D, width_out),
            low(STREAMS, length, D),
            low(length, width_out),
            low(length, units),
            low(3, length, head_width),
            low(HEADS // size, length, length),
            jax.ShapeDtypeStruct((own, D), single),
            jax.ShapeDtypeStruct((own, D), single),
            low(own, D),
            jax.ShapeDtypeStruct((own, HD), single),
            jax.ShapeDtypeStruct((48, D), single),
        ],
        in_specs=[vmem, hbm, hbm, vmem, vmem, hbm, hbm, vmem],
        out_specs=[hbm] * 7 + [vmem] * 5,
        scratch_shapes=[
            pltpu.VMEM((D, width_in), bfloat),
            pltpu.VMEM((D, width_out), bfloat),
            pltpu.VMEM((STREAMS, length, D), bfloat),
            pltpu.VMEM((3, length, head_width), bfloat),
            pltpu.VMEM((HEADS // size, length, length), bfloat),
            pltpu.VMEM((length, width_out), bfloat),
            pltpu.VMEM((length, units), bfloat),
            pltpu.VMEM((length, D), single),
            pltpu.VMEM((length, D), bfloat),
            pltpu.VMEM((size + 1, own, D), bfloat),
            pltpu.VMEM((STREAMS, own, D), bfloat),
            pltpu.VMEM((2, own, D), bfloat),
            pltpu.VMEM((own, HD), single),
            pltpu.VMEM((own, HD), single),
            pltpu.VMEM((2, 8, D), single),
            pltpu.VMEM((HD, D), bfloat),
            pltpu.VMEM((HD + 8, HD), single),
            pltpu.SemaphoreType.DMA((2,)),
            pltpu.SemaphoreType.DMA,
            pltpu.SemaphoreType.DMA((2,)),
            pltpu.SemaphoreType.DMA((2, size, STREAMS + 1)),
            pltpu.SemaphoreType.DMA((2, size, STREAMS + 1)),
            pltpu.SemaphoreType.DMA((2, size, CUT)),
            pltpu.SemaphoreType.DMA((2, size, CUT)),
            pltpu.SemaphoreType.DMA((6,)),
            pltpu.SemaphoreType.DMA((STREAMS, size)),
        ]
        + cube,
        compiler_params=pltpu.CompilerParams(
            collective_id=identity, has_side_effects=True, vmem_limit_bytes=60 * 2**20
        ),
        name="forward_%d" % identity,
    )(flows, w_in, w_out, small, jnp.asarray(rope), stored, cotangent, mix_weights)


def backward_kernel(
    size,
    count,
    d_branch,
    early_grads,
    rope,
    all_in,
    all_out,
    slope_in,
    heads_in,
    chances_in,
    joined_in,
    all_normed,
    flows_in,
    small,
    grad_in,
    grad_out,
    d_flows,
    early_sums,
    late_sums,
    arena,
    give,
    wide,
    heads,
    chances,
    back,
    d_up,
    d_pre,
    parts,
    terms,
    flows,
    total,
    sums,
    work,
    late,
    squares,
    arena_sem,
    load_sem,
    tile_sem,
    flow_sem,
    keep_sem,
    save_sem,
    line_send,
    line_recv,
    term_send,
    term_recv,
    give_sem,
    pair_sem,
    credit,
    ready,
    cube_send,
    cube_recv,
    *flat_refs,
):
    here = lax.axis_index("tensor")
    me = lax.axis_index("dp")
    bits = count.bit_length() - 1
    routes = cube_routes(bits)
    pieces = len(routes)
    subsets = sorted(routes[0][0], key=lambda held: -len(held))
    last = len(subsets) - 1
    own = flows.shape[1]
    length = own * size
    tile = arena.shape[2]
    head_width = heads.shape[2]
    group_heads = head_width // HD
    units = d_up.shape[1]
    tiles_out = (head_width + units) // tile
    tiles_in = (3 * head_width + units) // tile
    first_up = tiles_out + 3 * head_width // tile
    groups = (
        (0, tiles_out),
        (tiles_out, first_up - tiles_out),
        (first_up, tiles_out + tiles_in - first_up),
    )
    give_first = (0, tiles_out, 0)
    rows = D // count
    piece_rows = rows // pieces
    lane_rows = max(rows, HD)
    kept_first, land_first, pair_first = 0, D // 2, D - rows
    sides = ((0, 1), (1, -1))
    scale = HD ** (-0.5)
    ending = jnp.logical_or(here == 0, here == size - 1)

    def rows_of(block):
        return pl.ds(pl.multiple_of(block * own, own), own)

    def load_arena(index):
        source, place = (all_out, index) if index < tiles_out else (all_in, index - tiles_out)
        return pltpu.make_async_copy(
            source.at[:, pl.ds(place * tile, tile)], arena.at[index], arena_sem.at[index]
        )

    load_branch = pltpu.make_async_copy(d_branch, back.at[rows_of(here)], load_sem.at[0])
    load_slope = pltpu.make_async_copy(slope_in, wide.at[:, pl.ds(0, units)], load_sem.at[1])
    load_heads = pltpu.make_async_copy(heads_in, heads, load_sem.at[2])
    load_chances = pltpu.make_async_copy(chances_in, chances, load_sem.at[3])
    load_joined = pltpu.make_async_copy(joined_in, wide, load_sem.at[4])

    def load_flow(flow):
        return pltpu.make_async_copy(
            flows_in.at[flow], flows.at[flow % 2], flow_sem.at[flow % 2]
        )

    def keep_flow(flow):
        return pltpu.make_async_copy(
            flows.at[flow % 2], d_flows.at[flow], keep_sem.at[flow % 2]
        )

    load_rope = pltpu.make_async_copy(
        rope, total.at[:, pl.ds(0, rope.shape[1])], load_sem.at[5]
    )
    load_branch.start()
    half = len(flat_refs) // 2
    early = FlatSum(count, size, early_grads, early_sums, *flat_refs[:2], flat_refs[2:half])
    final = FlatSum(
        count, size, late, late_sums, *flat_refs[half : half + 2], flat_refs[half + 2 :]
    )
    enter([(jnp.bool_(True), partner) for partner in early.partners()])

    def has_next(way):
        return here < size - 1 if way > 0 else here > 0

    def has_origin(way, step):
        return here >= step if way > 0 else here < size - step

    def line_hop(side, way, step):
        block = back.at[rows_of(here - way * step)]
        return pltpu.make_async_remote_copy(
            src_ref=block if step else d_branch,
            dst_ref=block,
            send_sem=line_send.at[side, step],
            recv_sem=line_recv.at[side, step],
            device_id={"tensor": here + way},
            device_id_type=MESH,
        )

    def line_landed(side, way, step):
        block = back.at[rows_of(here - way * step)]
        return pltpu.make_async_remote_copy(
            src_ref=block,
            dst_ref=block,
            send_sem=line_send.at[side, step - 1],
            recv_sem=line_recv.at[side, step - 1],
            device_id={"tensor": here - way},
            device_id_type=MESH,
        )

    for side, way in sides:
        pl.when(has_next(way))(line_hop(side, way, 0).start)
    load_rope.start()
    for index in range(tiles_out):
        load_arena(index).start()
    load_slope.start()
    for index in range(first_up, tiles_out + tiles_in):
        load_arena(index).start()
    load_heads.start()
    load_chances.start()
    for index in range(tiles_out, first_up):
        load_arena(index).start()
    load_flow(3).start()
    load_flow(0).start()
    early.first()

    def pull(block):
        spot = rows_of(block)
        wide[spot, pl.ds(units, head_width)] = jnp.dot(
            back[spot], arena[0], preferred_element_type=single
        ).astype(bfloat)

        def one(index, carry):
            lanes = pl.ds(pl.multiple_of(index * tile, tile), tile)
            d_hidden = jnp.dot(
                back[spot], arena[head_width // tile + index], preferred_element_type=single
            )
            d_up[spot, lanes] = (d_hidden * wide[spot, lanes].astype(single)).astype(bfloat)
            return carry

        lax.fori_loop(0, units // tile, one, 0)

    def push(block):
        spot = rows_of(block)

        def one(index, carry):
            lanes = pl.ds(pl.multiple_of(index * tile, tile), tile)
            value = None
            for place in range(units // tile):
                term = contract_last(
                    d_up[spot, pl.ds(place * tile, tile)], arena[first_up + place, lanes]
                )
                value = term if value is None else value + term
            parts[3, spot, lanes] = value.astype(bfloat)
            return carry

        lax.fori_loop(0, D // tile, one, 0)

    late[...] = jnp.zeros_like(late)

    def turn_back(gradients, first, blocks):
        def table(kind):
            lanes = [
                pl.ds(pl.multiple_of((kind * size + first + block) * HD, HD), HD)
                for block in range(blocks)
            ]
            return jnp.concatenate([total[:, lane] for lane in lanes], axis=0)

        return (
            gradients * table(0)
            - pltpu.roll(gradients, HD - ROT // 2, 1) * table(1)
            - pltpu.roll(gradients, ROT // 2, 1) * table(2)
        )

    def attend_back(block):
        spot = rows_of(block)
        for head in range(group_heads):
            lanes = pl.ds(head * HD, HD)
            chance = chances[head, spot].astype(single)
            d_chance = contract_last(
                wide[spot, pl.ds(units + head * HD, HD)], heads[2, :, lanes]
            )
            centre = jnp.sum(d_chance * chance, axis=-1, keepdims=True)
            d_score = (chance * (d_chance - centre)).astype(bfloat)
            parts[1, spot, pl.ds(head * length, length)] = d_score
            d_query = jnp.dot(d_score, heads[1, :, lanes], preferred_element_type=single) * scale
            d_query = turn_back(d_query, block, 1).astype(bfloat)
            d_pre[0, spot, lanes] = d_query
            bias_lanes = pl.ds(pl.multiple_of(here * head_width + head * HD, HD), HD)
            late[4:5, bias_lanes] += jnp.sum(d_query.astype(single), axis=0, keepdims=True)

    chains = [
        LineSum(
            size,
            parts.at[flow],
            terms.at[flow],
            term_send.at[flow],
            term_recv.at[flow],
            CUT if flow == 3 else 1,
        )
        for flow in range(STREAMS)
    ]

    def relay(flow, rank):
        for sign in (1, -1):
            way = sign * chains[flow].near
            chains[flow].relay(way, chains[flow].far(rank, way))

    def middle(action):
        pl.when(jnp.logical_not(ending))(action)

    def spread_rows(flow, spot):
        def one(index, carry):
            lanes = pl.ds(pl.multiple_of(index * tile, tile), tile)
            columns = []
            for head in range(group_heads):
                place, lane = divmod((head * 3 + flow) * HD, tile)
                columns.append(arena[tiles_out + place, lanes, pl.ds(lane, HD)])
            parts[flow, spot, lanes] = contract_last(
                d_pre[flow, spot], jnp.concatenate(columns, axis=1)
            ).astype(bfloat)
            return carry

        lax.fori_loop(0, D // tile, one, 0)

    def spread(flow):
        spread_rows(flow, pl.ds(0, length))

        @pl.when(ending)
        def _():
            for rank in range(size - 1):
                relay(flow, rank)

    for index in range(tiles_out):
        load_arena(index).wait()
    load_slope.wait()
    load_branch.wait()
    pull(here)
    load_heads.wait()
    load_chances.wait()
    load_rope.wait()
    attend_back(here)
    early.second()
    for step in range(1, size):
        for side, way in sides:

            @pl.when(has_origin(way, step))
            def _():
                line_landed(side, way, step).wait_recv()
                pl.when(has_next(way))(line_hop(side, way, step).start)

        if step == 1:
            for index in range(tiles_out, tiles_out + tiles_in):
                load_arena(index).wait()
            spread_rows(0, rows_of(here))

        def both(side, carry):
            block = here - step + 2 * step * side

            @pl.when(jnp.logical_and(block >= 0, block < size))
            def _():
                pull(block)
                if step < size - 1:
                    push(block)
                attend_back(block)
                if step < size - 1:
                    spread_rows(0, rows_of(block))

            return carry

        lax.fori_loop(0, 2, both, 0)
        if step < size - 1:
            for flow in (3, 0):
                pl.when(ending)(lambda: relay(flow, size - 1 - step))
        if step == min(2, size - 1):
            early.third()

    def tell(which):
        for bit in range(bits):
            pl.semaphore_signal(
                ready.at[which, bit],
                inc=1,
                device_id={"dp": plus_flips(me, (bit,))},
                device_id_type=MESH,
            )

    tell(0)
    for head in range(group_heads):
        lanes = pl.ds(head * HD, HD)
        wide_lanes = pl.ds(head * length, length)
        d_key = contract_first(parts[1, :, wide_lanes], heads[0, :, lanes]) * scale
        d_key = turn_back(d_key, 0, size).astype(bfloat)
        d_value = contract_first(
            chances[head], wide[:, pl.ds(units + head * HD, HD)]
        ).astype(bfloat)
        d_pre[1, :, lanes] = d_key
        d_pre[2, :, lanes] = d_value
        bias_lanes = pl.ds(pl.multiple_of(here * head_width + head * HD, HD), HD)
        late[5:6, bias_lanes] = jnp.sum(d_key.astype(single), axis=0, keepdims=True)
        late[6:7, bias_lanes] = jnp.sum(d_value.astype(single), axis=0, keepdims=True)

    def first_lane(held):
        return pl.multiple_of(plus_flips(me, held) * rows // lane_rows * lane_rows, HD)

    def normal_lanes(slot):
        return pl.ds(slot * lane_rows, lane_rows)

    def load_tile(slot, held):
        return pltpu.make_async_copy(
            all_normed.at[:, :, pl.ds(first_lane(held), lane_rows)],
            chances.at[:, :, normal_lanes(slot)],
            tile_sem.at[slot],
        )

    load_joined.start()
    load_tile(0, (0,) + subsets[0]).start()
    load_tile(1, subsets[0]).start()

    @pl.when(ending)
    def _():
        block = size - 1 - here
        push(block)
        spread_rows(0, rows_of(block))
        for flow in (3, 0):
            relay(flow, 0)


    def own_rows(value, held):
        if lane_rows == rows:
            return value
        work[...] = value
        first = lax.rem(plus_flips(me, held) * rows, lane_rows)
        return work[pl.ds(pl.multiple_of(first, 16), rows)]

    def products(which, held, slot, emit):
        if which == 0:
            source = back[:, pl.ds(first_lane(held), lane_rows)]

            def one(index, carry):
                lanes = pl.ds(pl.multiple_of(index * tile, tile), tile)
                emit(own_rows(contract_first(source, wide[:, lanes]), held), index, 0)
                return carry

            lax.fori_loop(0, tiles_out, one, 0)
            return
        if which == 1:
            for part in range(3):
                value = own_rows(
                    contract_first(chances[part, :, normal_lanes(slot)], d_pre[part]), held
                )
                for head in range(group_heads):
                    place, lane = divmod((head * 3 + part) * HD, tile)
                    emit(value[:, head * HD : (head + 1) * HD], place, lane)
            return

        def one(index, carry):
            lanes = pl.ds(pl.multiple_of(index * tile, tile), tile)
            value = contract_first(chances[3, :, normal_lanes(slot)], d_up[:, lanes])
            emit(own_rows(value, held), index, 0)
            return carry

        lax.fori_loop(0, units // tile, one, 0)

    def place_of(held):
        return sum(2 ** (bit - 1) for bit in held)

    def pass_pair(which):
        first, span = groups[which]
        return pltpu.make_async_remote_copy(
            src_ref=give.at[pl.ds(give_first[which], span)],
            dst_ref=arena.at[pl.ds(first, span), pl.ds(pair_first, rows)],
            send_sem=give_sem.at[which],
            recv_sem=pair_sem.at[which],
            device_id={"dp": plus_flips(me, (0,))},
            device_id_type=MESH,
        )

    def kept_row(piece, held):
        return kept_first + place_of(held) * rows + piece * piece_rows

    def land_row(piece, landed):
        return land_first + (piece * last + place_of(landed) - 1) * piece_rows

    def cube_hop(which, piece, bit, landed):
        tiles = pl.ds(*groups[which])
        return pltpu.make_async_remote_copy(
            src_ref=arena.at[tiles, pl.ds(kept_row(piece, landed), piece_rows)],
            dst_ref=arena.at[tiles, pl.ds(land_row(piece, landed), piece_rows)],
            send_sem=cube_send.at[which, piece, place_of(landed)],
            recv_sem=cube_recv.at[which, piece, place_of(landed)],
            device_id={"dp": plus_flips(me, (bit,))},
            device_id_type=MESH,
        )

    def needs(piece, held):
        return [
            (bit, landed)
            for step in routes[piece][1]
            for bit, source, landed in step
            if source == held
        ]

    def add_landed(which, piece, held):
        for bit, landed in needs(piece, held):
            cube_hop(which, piece, bit, landed).wait_recv()
        first, span = groups[which]

        def one(index, carry):
            def column(at, inner):
                spot = pl.ds(pl.multiple_of(kept_row(piece, held) + index * 16, 16), 16)
                value = arena[first + at, spot].astype(single)
                for _, landed in needs(piece, held):
                    arrived = pl.ds(pl.multiple_of(land_row(piece, landed) + index * 16, 16), 16)
                    value = value + arena[first + at, arrived].astype(single)
                arena[first + at, spot] = value.astype(bfloat)
                if not held:
                    value = value * value
                    value = value[0:8] + value[8:16]
                    for group in range(tile // HD):
                        inner = inner + value[:, group * HD : (group + 1) * HD]
                return inner

            return lax.fori_loop(0, span, column, carry)

        found = lax.fori_loop(0, piece_rows // 16, one, jnp.zeros((8, HD), single))
        if not held:
            squares[...] += found

    def offer(which, index):
        held = subsets[index]
        if index > 0:
            pass_pair(which).wait_send()
        else:
            for bit in range(bits):
                pl.semaphore_wait(ready.at[which, bit], 1)
        if which == 1:
            load_tile(0, (0,) + held).wait()

        def emit(value, place, lane):
            give[give_first[which] + place, :, pl.ds(lane, value.shape[1])] = value.astype(bfloat)

        products(which, (0,) + held, 0, emit)
        if index > 0:
            pl.semaphore_wait(credit.at[which], 1)
        pass_pair(which).start()
        if which == 2 and index < last:
            load_tile(0, (0,) + subsets[index + 1]).start()

    def keep(which, index):
        held = subsets[index]
        first, _ = groups[which]
        if which == 1:
            load_tile(1, held).wait()
        pass_pair(which).wait_recv()

        def emit(value, place, lane):
            lanes = pl.ds(lane, value.shape[1])
            arena[first + place, pl.ds(kept_first + place_of(held) * rows, rows), lanes] = (
                value + arena[first + place, pl.ds(pair_first, rows), lanes].astype(single)
            ).astype(bfloat)

        products(which, held, 1, emit)
        if index < last:
            pl.semaphore_signal(
                credit.at[which],
                inc=1,
                device_id={"dp": plus_flips(me, (0,))},
                device_id_type=MESH,
            )
        else:
            pass_pair(which).wait_send()
        for piece, (_, steps) in enumerate(routes):
            for bit, _, landed in steps[-1]:
                if landed == held:
                    cube_hop(which, piece, bit, landed).start()
        if which == 2 and index < last:
            load_tile(1, subsets[index + 1]).start()

    def pass_on(which):
        for step in range(pieces - 2, -1, -1):
            for piece, (_, steps) in enumerate(routes):
                for bit, _, landed in steps[step]:
                    add_landed(which, piece, landed)
                    cube_hop(which, piece, bit, landed).start()

    def descend(flow):
        load_flow(flow).wait()
        gain = 2 if flow == 3 else 0
        slot = flow % 2

        def one(index, carry):
            spot = pl.ds(pl.multiple_of(index * 16, 16), 16)
            values = flows[slot, spot].astype(single)
            centred = values - jnp.mean(values, axis=-1, keepdims=True)
            inverse = lax.rsqrt(jnp.mean(centred * centred, axis=-1, keepdims=True) + norm_eps)
            unit = centred * inverse
            incoming = total[spot]
            scaled = incoming * small[gain : gain + 1, :]
            result = inverse * (
                scaled
                - jnp.mean(scaled, axis=-1, keepdims=True)
                - unit * jnp.mean(scaled * unit, axis=-1, keepdims=True)
            )
            flows[slot, spot] = result.astype(bfloat)
            unit = unit * incoming
            sums[gain] += unit[0:8] + unit[8:16]
            sums[gain + 1] += incoming[0:8] + incoming[8:16]
            return carry

        steps = own // 16 // chains[flow].cut
        for place in range(chains[flow].cut):
            chains[flow].collect(place, total)
            lax.fori_loop(place * steps, (place + 1) * steps, one, 0)
        keep_flow(flow).start()

    saves = []

    def settle(which):
        for piece in range(pieces):
            add_landed(which, piece, ())
        first, span = groups[which]
        target, offset = (grad_out, 0) if which == 0 else (grad_in, first - tiles_out)
        for place in range(span):
            saves.append(
                pltpu.make_async_copy(
                    arena.at[first + place, pl.ds(kept_first, rows)],
                    target.at[:, pl.ds((offset + place) * tile, tile)],
                    save_sem.at[first + place],
                )
            )
            saves[-1].start()

    def near(flow, rank):
        way = chains[flow].near
        middle(lambda: chains[flow].relay(way, chains[flow].far(rank, way)))

    def beyond(flow, rank):
        way = -chains[flow].near
        middle(lambda: chains[flow].relay(way, chains[flow].far(rank, way)))

    def unit_sum(index, carry):
        lanes = pl.ds(pl.multiple_of(index * 256, 256), 256)
        late[pl.ds(8 + here, 1), lanes] = jnp.sum(
            d_up[:, lanes].astype(single), axis=0, keepdims=True
        )
        return carry

    def release():
        push(here)
        tell(2)

    def closing():
        spread(2)
        tell(1)

    between = [lambda: spread(1), closing, release]
    load_joined.wait()
    for index in range(last + 1):
        offer(0, index)
        if between:
            between.pop(0)()
        if index == last:
            for action in between:
                action()
            offer(1, 0)
        keep(0, index)
        if index < 2:
            for rank in range(size - 2, 0, -1):
                middle(lambda: relay((3, 0)[index], rank))
    near(3, 0)
    offer(2, 0)
    lax.fori_loop(0, units // 256, unit_sum, 0)
    between = [lambda: near(0, 0), lambda: pass_on(0), lambda: beyond(3, 0)]
    for index in range(last + 1):
        keep(1, index)
        if index < last:
            offer(1, index + 1)
        keep(2, index)
        if index < last:
            offer(2, index + 1)
        if between:
            between.pop(0)()
    for action in between:
        action()
    sums[...] = jnp.zeros_like(sums)
    beyond(0, 0)
    near(1, 0)
    descend(3)
    descend(0)
    keep_flow(3).wait()
    load_flow(1).start()
    near(1, 1)
    beyond(1, 0)
    pass_on(1)
    pass_on(2)
    for rank in range(1, size - 1):
        if rank > 1:
            near(1, rank)
        beyond(1, rank)
    keep_flow(0).wait()
    load_flow(2).start()
    descend(1)
    squares[...] = jnp.zeros_like(squares)
    near(2, 0)
    near(2, 1)
    beyond(2, 0)
    for rank in range(1, size - 1):
        if rank > 1:
            near(2, rank)
        beyond(2, rank)
    descend(2)
    for row in range(4):
        late[row : row + 1] = jnp.sum(sums[row], axis=0, keepdims=True)
    final.first()
    for which in range(3):
        settle(which)
    final.second(jnp.sum(squares[...], axis=0, keepdims=True))
    final.third()
    final.last()
    early.last()
    for step in range(size):
        for side, way in sides:

            @pl.when(jnp.logical_and(has_next(way), has_origin(way, step)))
            def _():
                line_hop(side, way, step).wait_send()

    for which in range(3):
        for piece, (_, steps) in enumerate(routes):
            for step in steps:
                for bit, _, landed in step:
                    cube_hop(which, piece, bit, landed).wait_send()
    for chain in chains:
        chain.drain()
    keep_flow(1).wait()
    keep_flow(2).wait()
    for copy in saves:
        copy.wait()


def backward(
    d_branch, early_grads, rope, all_in, all_out, slope, heads, chances, joined, all_normed,
    flows, small, size, count, identity,
):
    own = d_branch.shape[0]
    length = own * size
    rows = D // count
    lane_rows = max(rows, HD)
    tile = 512
    head_width, units = heads.shape[2], slope.shape[1]
    width_in, width_out = all_in.shape[1], all_out.shape[1]
    tiles = (width_in + width_out) // tile
    pieces = count.bit_length() - 2
    held = 2**pieces
    bits = pieces + 1
    late_rows = 16
    low = lambda *shape: jax.ShapeDtypeStruct(shape, bfloat)
    wide = lambda *shape: jax.ShapeDtypeStruct(shape, single)
    hbm = pl.BlockSpec(memory_space=pl.ANY)
    vmem = pl.BlockSpec(memory_space=pltpu.VMEM)
    dma = pltpu.SemaphoreType.DMA
    rope = rope.reshape(3, size, own, HD).transpose(2, 0, 1, 3).reshape(own, -1)
    return pl.pallas_call(
        lambda *refs: backward_kernel(size, count, *refs),
        out_shape=[
            low(rows, width_in),
            low(rows, width_out),
            low(STREAMS, own, D),
            wide(*early_grads.shape),
            wide(late_rows, D),
        ],
        in_specs=[hbm, vmem] + [hbm] * 9 + [vmem],
        out_specs=[hbm] * 3 + [vmem] * 2,
        scratch_shapes=[
            pltpu.VMEM((tiles, D, tile), bfloat),
            pltpu.VMEM(((width_out + 3 * head_width) // tile, rows, tile), bfloat),
            pltpu.VMEM((length, width_out), bfloat),
            pltpu.VMEM(heads.shape, bfloat),
            pltpu.VMEM(chances.shape, bfloat),
            pltpu.VMEM((length, D), bfloat),
            pltpu.VMEM((length, units), bfloat),
            pltpu.VMEM((3, length, head_width), bfloat),
            pltpu.VMEM((STREAMS, length, D), bfloat),
            pltpu.VMEM((STREAMS, size + 1, own, D), bfloat),
            pltpu.VMEM((2, own, D), bfloat),
            pltpu.VMEM((own, D), single),
            pltpu.VMEM((4, 8, D), single),
            pltpu.VMEM((lane_rows, tile) if lane_rows > rows else (8, HD), single),
            pltpu.VMEM((late_rows, D), single),
            pltpu.VMEM((8, HD), single),
            dma((tiles,)),
            dma((6,)),
            dma((2,)),
            dma((2,)),
            dma((2,)),
            dma((tiles,)),
            dma((2, size)),
            dma((2, size)),
            dma((STREAMS, 2, size, CUT)),
            dma((STREAMS, 2, size, CUT)),
            dma((3,)),
            dma((3,)),
            pltpu.SemaphoreType.REGULAR((3,)),
            pltpu.SemaphoreType.REGULAR((3, bits)),
            dma((3, pieces, held)),
            dma((3, pieces, held)),
        ]
        + flat_scratch(early_grads.shape[0], count, size)
        + flat_scratch(late_rows, count, size),
        compiler_params=pltpu.CompilerParams(
            collective_id=identity, has_side_effects=True, vmem_limit_bytes=64 * 2**20 - 2**19
        ),
        name="backward_%d" % identity,
    )(
        d_branch, early_grads, jnp.asarray(rope), all_in, all_out, slope, heads, chances, joined,
        all_normed, flows, small,
    )


def finish_kernel(grad_in, grad_out, sums, early_sums, weights, newest_in, d_newest_in, stored, cotangent, d_flows, *refs):
    states, refs = (refs[0:4], refs[4:8]), refs[8:]
    small_in, mix, refs = refs[0:4], refs[4:8], refs[8:]
    norm_out, refs = refs[0], refs[1:]
    new_states, refs = (refs[0:5], refs[5:10]), refs[10:]
    new_small, new_mix, refs = refs[0:4], refs[4:8], refs[8:]
    out_streams, grad_streams, grad_stored, refs = refs[0], refs[1], refs[2], refs[3:]
    held, refs = (refs[0:2], refs[2:4], refs[4:6]), refs[6:]
    tiles_in, tiles_out, spread, passed, small_sums, newest, d_newest, small, refs = (
        *refs[0:8],
        refs[8:],
    )
    row_sem, small_load, small_save, grad_sem, load_sem, save_sem, tile_load, tile_save, pass_sem = refs
    grads = (grad_in, grad_out)
    parts = load_sem.shape[2]
    rows = grad_in.shape[0]
    step_rows = rows // parts

    def load_grad(which):
        return pltpu.make_async_copy(grads[which], held[0][which], grad_sem.at[which])

    def load(which, kind, place):
        spot = pl.ds(place * step_rows, step_rows)
        return pltpu.make_async_copy(
            states[which][kind].at[spot],
            held[1][which].at[kind, spot],
            load_sem.at[which, kind, place],
        )

    def save(which, kind, place):
        spot = pl.ds(place * step_rows, step_rows)
        source = held[1][which].at[kind, spot] if kind < 4 else held[2][which].at[spot]
        return pltpu.make_async_copy(
            source, new_states[which][kind].at[spot], save_sem.at[which, kind, place]
        )

    own = newest_in.shape[0]
    tile_rows = tiles_in.shape[2]
    tile_count = own // tile_rows
    mixes = STREAMS + LAYER

    def tile_copies(index, into):
        spot = pl.ds(index * tile_rows, tile_rows)
        first, second = (cotangent, stored) if into else (out_streams, grad_stored)
        held_tile = (tiles_in if into else tiles_out).at[index % 2]
        sem = (tile_load if into else tile_save).at[index % 2]
        pairs = [
            (first.at[:, spot], held_tile.at[0:STREAMS]),
            (second.at[:, spot], held_tile.at[STREAMS:mixes]),
        ]
        return [
            pltpu.make_async_copy(*(pair if into else pair[::-1]), sem.at[place])
            for place, pair in enumerate(pairs)
        ]

    def compose(index):
        for copy in tile_copies(index, True):
            copy.wait()
        if index > 1:
            for copy in tile_copies(index - 2, False):
                copy.wait()
        spot = pl.ds(index * tile_rows, tile_rows)
        mix_tile = weights[spot]
        slot = index % 2
        for column in range(MIXH):
            spread[column] = jnp.broadcast_to(mix_tile[:, column : column + 1], (tile_rows, HD))

        def columns(place, carry):
            lanes = pl.ds(pl.multiple_of(place * HD, HD), HD)
            value = newest[spot, lanes]
            flows = [tiles_in[slot, stream, :, lanes].astype(single) for stream in range(STREAMS)]
            results = [spread[stream * LAYERS + LAYER] * value for stream in range(STREAMS)]
            for layer in range(LAYER):
                earlier = tiles_in[slot, STREAMS + layer, :, lanes].astype(single)
                gradient = None
                for stream in range(STREAMS):
                    weight = spread[stream * LAYERS + layer]
                    results[stream] = results[stream] + weight * earlier
                    term = weight * flows[stream]
                    gradient = term if gradient is None else gradient + term
                tiles_out[slot, STREAMS + layer, :, lanes] = gradient.astype(bfloat)
            for stream in range(STREAMS):
                tiles_out[slot, stream, :, lanes] = results[stream].astype(bfloat)
            return carry

        lax.fori_loop(0, D // HD, columns, 0)
        for copy in tile_copies(index, False):
            copy.start()
        if index + 2 < tile_count:
            for copy in tile_copies(index + 2, True):
                copy.start()

    load_rows = [
        pltpu.make_async_copy(newest_in, newest, row_sem.at[0]),
        pltpu.make_async_copy(d_newest_in, d_newest, row_sem.at[1]),
    ]
    load_small = [
        pltpu.make_async_copy(small_in[kind], small.at[kind], small_load.at[kind])
        for kind in range(4)
    ]
    save_small = [
        pltpu.make_async_copy(small.at[kind], new_small[kind], small_save.at[kind])
        for kind in range(4)
    ]
    for copy in load_small:
        copy.start()
    for index in range(2):
        for copy in tile_copies(index, True):
            copy.start()
    for copy in load_rows:
        copy.start()
    for which in range(2):
        load_grad(which).start()
        for place in range(parts):
            for kind in range(4):
                load(which, kind, place).start()
    take_flows = pltpu.make_async_copy(d_flows, passed, pass_sem.at[0])
    give_flows = pltpu.make_async_copy(passed, grad_streams, pass_sem.at[1])
    take_flows.start()
    small_sums[0:4] = sums[0:4]
    small_sums[4:5] = early_sums[MIXH : MIXH + 1]
    small_sums[5:8] = sums[4:7]
    small_sums[8:9] = early_sums[MIXH + 1 : MIXH + 2]
    small_sums[9:10] = early_sums[MIXH + 1 : MIXH + 2]
    small_sums[10:SMALL_MIX] = sums[8 : 8 + SMALL_MIX - 10]
    small_sums[SMALL_MIX : SMALL_MIX + MIXH] = early_sums[0:MIXH]
    small_total = small_sums[...]
    mix_total = jnp.concatenate(
        [early_sums[40:48, place * HD : (place + 1) * HD] for place in range(5)], axis=0
    )[0 : mix[0].shape[0], 0 : mix[0].shape[1]]

    def whole_sum(values):
        return jnp.sum(jnp.sum(values, axis=1, keepdims=True), axis=0, keepdims=True)

    norm = jnp.sqrt(
        whole_sum(sums[7:8])
        + whole_sum(sums[15:16])
        + whole_sum(small_total * small_total)
        + whole_sum(mix_total * mix_total)
    )
    norm_out[...] = norm
    factor = clip_norm / jnp.maximum(norm, clip_norm)
    for copy in load_small:
        copy.wait()
    results = adamw_step(*(small[kind] for kind in range(4)), small_total, factor, small_rate)
    for kind in range(4):
        small[kind] = results[kind]
        save_small[kind].start()
    for target, result in zip(
        new_mix, adamw_step(*(ref[...] for ref in mix), mix_total, factor, small_rate)
    ):
        target[...] = result
    take_flows.wait()
    for copy in load_rows:
        copy.wait()

    def add_residual(index, carry):
        spot = pl.ds(pl.multiple_of(index * 16, 16), 16)
        passed[3, spot] = (passed[3, spot].astype(single) + d_newest[spot]).astype(bfloat)
        return carry

    lax.fori_loop(0, own // 16, add_residual, 0)
    give_flows.start()
    tiles_done = 0
    for which in range(2):
        columns = held[1][which].shape[2]
        load_grad(which).wait()
        for place in range(parts):
            for kind in range(4):
                load(which, kind, place).wait()

            def update(index, carry):
                spot = pl.ds(pl.multiple_of(place * step_rows + index * 16, 16), 16)

                def column(at, inner):
                    lanes = pl.ds(pl.multiple_of(at * 512, 512), 512)
                    results = adamw_step(
                        *(held[1][which][kind, spot, lanes] for kind in range(4)),
                        held[0][which][spot, lanes].astype(single),
                        factor,
                        learn_rate,
                    )
                    for kind in range(4):
                        held[1][which][kind, spot, lanes] = results[kind]
                    held[2][which][spot, lanes] = results[0].astype(bfloat)
                    return inner

                return lax.fori_loop(0, columns // 512, column, carry, unroll=True)

            lax.fori_loop(0, step_rows // 16, update, 0)
            for kind in range(5):
                save(which, kind, place).start()
            if tiles_done < tile_count:
                compose(tiles_done)
                tiles_done += 1
    while tiles_done < tile_count:
        compose(tiles_done)
        tiles_done += 1
    for index in range(tile_count - 2, tile_count):
        for copy in tile_copies(index, False):
            copy.wait()
    give_flows.wait()
    for copy in save_small:
        copy.wait()
    for which in range(2):
        for place in range(parts):
            for kind in range(5):
                save(which, kind, place).wait()


def finish(
    grads, sums, early_sums, weights, newest, d_newest, stored, cotangent, d_flows, in_states, out_states, small, mix
):
    wide = lambda shape: jax.ShapeDtypeStruct(shape, single)
    low = lambda shape: jax.ShapeDtypeStruct(shape, bfloat)
    hbm = pl.BlockSpec(memory_space=pl.ANY)
    vmem = pl.BlockSpec(memory_space=pltpu.VMEM)
    shapes = [in_states[0].shape, out_states[0].shape]
    parts = 4
    tile = (2, STREAMS + LAYER, 16, D)
    return pl.pallas_call(
        finish_kernel,
        out_shape=[wide((1, 1))]
        + [entry for shape in shapes for entry in [wide(shape)] * 4 + [low(shape)]]
        + [wide(small[0].shape)] * 4
        + [wide(mix[0].shape)] * 4
        + [low(cotangent.shape), low(d_flows.shape), low(stored.shape)],
        in_specs=[hbm] * 2 + [vmem] * 3 + [hbm] * 17 + [vmem] * 4,
        out_specs=[vmem] + [hbm] * 14 + [vmem] * 4 + [hbm] * 3,
        scratch_shapes=[pltpu.VMEM(shape, grads[0].dtype) for shape in shapes]
        + [pltpu.VMEM((4,) + shape, single) for shape in shapes]
        + [pltpu.VMEM(shape, bfloat) for shape in shapes]
        + [pltpu.VMEM(tile, bfloat)] * 2
        + [pltpu.VMEM((MIXH, tile[2], HD), single), pltpu.VMEM(d_flows.shape, bfloat)]
        + [pltpu.VMEM(small[0].shape, single)]
        + [pltpu.VMEM(newest.shape, single)] * 2
        + [pltpu.VMEM((4,) + small[0].shape, single)]
        + [pltpu.SemaphoreType.DMA((n,)) for n in (2, 4, 4)]
        + [
            pltpu.SemaphoreType.DMA((2,)),
            pltpu.SemaphoreType.DMA((2, 4, parts)),
            pltpu.SemaphoreType.DMA((2, 5, parts)),
            pltpu.SemaphoreType.DMA((2, 2)),
            pltpu.SemaphoreType.DMA((2, 2)),
            pltpu.SemaphoreType.DMA((2,)),
        ],
        compiler_params=pltpu.CompilerParams(vmem_limit_bytes=60 * 2**20),
        name="finish",
    )(
        *grads, sums, early_sums, weights, newest, d_newest, stored, cotangent, d_flows,
        *in_states, *out_states, *small, *mix,
    )


def shards(
    in_streams,
    stored,
    cotangent,
    in_weights,
    in_moment,
    in_second,
    in_average,
    out_weights,
    out_moment,
    output_second_moment,
    out_average,
    small_params,
    small_moment,
    small_second,
    small_average,
    mix_weights,
    mix_moment,
    mix_second,
    mix_average,
):
    groups, count = lax.axis_size("tensor"), lax.axis_size("dp")
    rope = rope_lanes(in_streams.shape[1] * groups)
    (
        full_in,
        full_out,
        normed,
        joined,
        slope,
        heads,
        chances,
        newest,
        d_newest,
        d_branch,
        weights,
        early_grads,
    ) = forward(
        in_streams,
        in_weights,
        out_weights,
        small_params,
        rope,
        stored,
        cotangent,
        mix_weights,
        groups,
        count,
        0,
    )
    grad_in, grad_out, d_flows, early_sums, sums = backward(
        d_branch,
        early_grads,
        rope,
        full_in,
        full_out,
        slope,
        heads,
        chances,
        joined,
        normed,
        in_streams,
        small_params,
        groups,
        count,
        1,
    )
    results = finish(
        (grad_in, grad_out),
        sums,
        early_sums,
        weights,
        newest,
        d_newest,
        stored,
        cotangent,
        d_flows,
        (in_weights, in_moment, in_second, in_average),
        (out_weights, out_moment, output_second_moment, out_average),
        (small_params, small_moment, small_second, small_average),
        (mix_weights, mix_moment, mix_second, mix_average),
    )
    out_streams, grad_streams, grad_stored = results[-3:]
    return (out_streams, grad_streams, grad_stored, results[0][0, 0], *results[1:-3])


def solution(mesh):
    in_specs = (
        P(None, ("dp", "tensor"), None),
        P(None, ("dp", "tensor"), None),
        P(None, ("dp", "tensor"), None),
        P("dp", "tensor"),
        P("dp", "tensor"),
        P("dp", "tensor"),
        P("dp", "tensor"),
        P("dp", "tensor"),
        P("dp", "tensor"),
        P("dp", "tensor"),
        P("dp", "tensor"),
        P(),
        P(),
        P(),
        P(),
        P(),
        P(),
        P(),
        P(),
    )
    out_specs = (
        P(None, ("dp", "tensor"), None),
        P(None, ("dp", "tensor"), None),
        P(None, ("dp", "tensor"), None),
        P(),
        P("dp", "tensor"),
        P("dp", "tensor"),
        P("dp", "tensor"),
        P("dp", "tensor"),
        P("dp", "tensor"),
        P("dp", "tensor"),
        P("dp", "tensor"),
        P("dp", "tensor"),
        P("dp", "tensor"),
        P("dp", "tensor"),
        P(),
        P(),
        P(),
        P(),
        P(),
        P(),
        P(),
        P(),
    )
    return jax.shard_map(shards, mesh=mesh, in_specs=in_specs, out_specs=out_specs, check_vma=False)
```
